128 devices in a mesh: blk: 128 (over x, y, z, core).
Axes of the slice: x: 4, y: 4, z: 4, core: 2. Of those that a mesh axis runs over, the one named last changes fastest.
Arguments:
- source_points: bfloat16 [49152, 256], P('blk')
- target_points: bfloat16 [131072, 256], P('blk')
- source_mass: float32 [49152], P('blk'), may hold values from 0.25 to 4
- target_mass: float32 [131072], P('blk'), may hold values from 0.25 to 4
- target_init: float32 [131072], P('blk'), may hold values from -1.8 to 1.8
- pair_tiles: int32 [16384, 2], P('blk'), may hold values from 0 to 7, as said below
- pair_count: int32 [16384], P('blk'), may hold values from 0 to 2, as said below
Outputs:
- source_pot: float32 [49152], P('blk')
- target_pot: float32 [131072], P('blk')
The draws below stay inside these ranges and needn't reach their ends.
Inputs may be any that keep to these rules, and one draw needn't show every extreme that they name: `pair_tiles`: the entries of a row are distinct; entries past the row's count are padding, still tile numbers below 8. Every target tile is named by a valid entry of some row, and every source device has a valid entry in some row. `pair_count`: some rows hold 2 valid entries in every draw.
All inputs are finite; a program needn't handle non-finite values.
Results may differ from the reference program's by a relative error of at most 0.0003.
Values may be sent and summed in bfloat16 or wider, within the bound.
No kernel may reach another device: no remote copies, remote signals or barrier semaphores. Data moves between devices by JAX's collectives and lax.ppermute only.
A program may use at most 192 MiB of HBM per device.

```python
import math
import jax
import jax.numpy as jnp
from jax import lax

D = 256
SROWS = 384
TROWS = 128
TSUB = 8
CAP = 2
ITERS = 2
NS = 49152
NT = 131072
N_BLK = 128


def pair_layout(key):
    row_index = jnp.arange(N_BLK * N_BLK, dtype=jnp.int32)
    source_dev = row_index // N_BLK
    owner_dev = row_index % N_BLK
    offset_rank = (source_dev - owner_dev) % N_BLK
    key_owner, key_row, key_count = jax.random.split(key, 3)
    owner_shift = jax.random.randint(key_owner, (N_BLK,), 0, TSUB)
    row_shift = jax.random.randint(key_row, (N_BLK * N_BLK,), 0, TSUB)
    forced = offset_rank < TSUB // CAP
    base_tile = jnp.where(forced, CAP * offset_rank + owner_shift[owner_dev], row_shift)
    tile_ids = (base_tile[:, None] + jnp.arange(CAP, dtype=jnp.int32)[None, :]) % TSUB
    counts = jnp.where(forced, CAP, jax.random.randint(key_count, (N_BLK * N_BLK,), 0, CAP + 1))
    return (tile_ids.astype(jnp.int32), counts.astype(jnp.int32))


def draw_pair_tiles(key, part):
    tile_ids, counts = pair_layout(key)
    return tile_ids


def draw_pair_count(key, part):
    tile_ids, counts = pair_layout(key)
    return counts


def draw_source_points(key, part):
    key = jax.random.fold_in(key, 11)
    key_main = jax.random.fold_in(key, 0)
    values = jax.random.normal(key_main, (NS, D), jnp.float32)
    return values.astype(jnp.bfloat16)


def draw_target_points(key, part):
    key = jax.random.fold_in(key, 23)
    key_main = jax.random.fold_in(key, 0)
    values = jax.random.normal(key_main, (NT, D), jnp.float32)
    return values.astype(jnp.bfloat16)


def shard_levels(key, dims, cuts, least, high):
    level = 1.0
    for dim, blocks in cuts:
        draws = jax.random.uniform(jax.random.fold_in(jax.random.fold_in(key, 6), dim), (blocks,), jnp.float32, least / len(cuts), high / len(cuts))
        level = level * jnp.repeat(jnp.exp(draws), dims[dim] // blocks).reshape((-1,) + (1,) * (len(dims) - 1 - dim))
    return level


def noise(stream_key, shape, scale, bound, pieces=(), held_as=jnp.bfloat16):
    drawn = jax.random.normal(stream_key, shape, jnp.float32) * scale
    if len(pieces) > 0:
        drawn = shard_levels(stream_key, shape, pieces, -0.22, 0.18) * drawn
    return jnp.clip(drawn, min=-bound, max=bound).astype(held_as)


def setup_inputs(seed: int = 0) -> dict:
    keys = jax.random.split(jax.random.key(seed), 8)
    return {
        "source_points": draw_source_points(jax.random.fold_in(keys[7], 71), 0),
        "target_points": draw_target_points(jax.random.fold_in(keys[7], 71), 0),
        "source_mass": jnp.clip(jnp.exp(math.log(4.0) - 2.7725887 * jax.random.uniform(keys[2], (NS,), jnp.float32) ** shard_levels(keys[2], (NS,), ((0, 128),), -0.2, 0.2)), 0.25, 4.0),
        "target_mass": jnp.clip(jnp.exp(math.log(4.0) - 2.7725887 * jax.random.uniform(keys[3], (NT,), jnp.float32) ** shard_levels(keys[3], (NT,), ((0, 128),), -0.2, 0.2)), 0.25, 4.0),
        "target_init": noise(keys[4], (NT,), 0.3, 1.8, ((0, 128),), jnp.float32),
        "pair_tiles": draw_pair_tiles(jax.random.fold_in(keys[7], 71), 0),
        "pair_count": draw_pair_count(jax.random.fold_in(keys[7], 71), 0),
    }


EPSILON = 0.1


def reference(source_points, target_points, source_mass, target_mass, target_init, pair_tiles, pair_count):
    source_rows = source_points.astype(jnp.float32).reshape(N_BLK, SROWS, D)
    target_rows = target_points.astype(jnp.float32).reshape(N_BLK * TSUB, TROWS, D)
    tile_ids = pair_tiles.reshape(N_BLK, N_BLK, CAP)
    owners = jnp.arange(N_BLK, dtype=jnp.int32)
    global_ids = (owners[None, :, None] * TSUB + tile_ids).astype(jnp.int32).reshape(N_BLK, N_BLK * CAP)
    slot_valid = (jnp.arange(CAP, dtype=jnp.int32)[None, None, :] < pair_count.reshape(N_BLK, N_BLK)[:, :, None]).reshape(N_BLK, N_BLK * CAP)
    log_source = jnp.log(source_mass).reshape(N_BLK, SROWS)
    log_target = jnp.log(target_mass).reshape(N_BLK * TSUB, TROWS)
    target_pot = target_init.reshape(N_BLK * TSUB, TROWS)
    source_pot = jnp.zeros((N_BLK, SROWS), jnp.float32)
    for iteration in range(ITERS):
        current = target_pot

        def per_source(packed):
            block, ids_here, slot_ok, log_here = packed
            tiles = target_rows[ids_here]
            source_norm = jnp.sum(block * block, axis=-1)
            tile_norm = jnp.sum(tiles * tiles, axis=-1)
            cross_term = jnp.einsum("sd,ktd->skt", block, tiles, precision=lax.Precision.HIGHEST)
            cost_tile = (source_norm[:, None, None] + tile_norm[None] - 2.0 * cross_term) / D
            g_slots = current[ids_here]
            mask_here = slot_ok[None, :, None]
            scores = jnp.where(mask_here, (g_slots[None] - cost_tile) / EPSILON, -jnp.inf)
            row_max = jnp.max(scores, axis=(1, 2))
            row_sum = jnp.sum(jnp.exp(scores - row_max[:, None, None]), axis=(1, 2))
            new_source = EPSILON * log_here - EPSILON * (row_max + jnp.log(row_sum))
            col_score = (new_source[:, None, None] - cost_tile) / EPSILON
            col_max = jnp.max(col_score, axis=0)
            col_sum = jnp.sum(jnp.exp(col_score - col_max[None]), axis=0)
            col_max = jnp.where(slot_ok[:, None], col_max, -jnp.inf)
            col_sum = jnp.where(slot_ok[:, None], col_sum, 0.0)
            return new_source, col_max, col_sum

        source_pot, col_max, col_sum = lax.map(per_source, (source_rows, global_ids, slot_valid, log_source))
        flat_ids = global_ids.reshape(-1)
        flat_max = col_max.reshape(-1, TROWS)
        flat_sum = col_sum.reshape(-1, TROWS)
        top_col = jnp.full((N_BLK * TSUB, TROWS), -jnp.inf, jnp.float32).at[flat_ids].max(flat_max)
        col_total = jnp.zeros((N_BLK * TSUB, TROWS), jnp.float32).at[flat_ids].add(flat_sum * jnp.exp(flat_max - top_col[flat_ids]))
        target_pot = EPSILON * log_target - EPSILON * (top_col + jnp.log(col_total))
    return source_pot.reshape(NS), target_pot.reshape(NT)
```

```python
import functools

import jax
import jax.numpy as jnp
from jax import lax
from jax.experimental import pallas as pl
from jax.experimental.pallas import tpu as pltpu
from jax.sharding import Mesh
from jax.sharding import PartitionSpec as P

TSUB = 8
CAP = 2
ITERS = 2
EPSILON = 0.1

DIMS = (4, 4, 4, 2)
NAMES = ("x", "y", "z", "core")
ROWS = ("y", "z")
COLS = ("x", "core")
N_ROWS = 16
N_COLS = 8
SRC = 384
TILE = 128
SUBS = SRC // TILE
FEAT = 256
TILES = N_COLS * TSUB
ITEMS = N_ROWS * N_COLS
UNROLL = 2
HALF = SRC // 2
RING = 4
GAIN = 2.0 / (FEAT * EPSILON)
SPAN = 70.0


def lse_over_first(parts):
    top = jnp.max(parts, axis=0)
    base = jnp.where(top == -jnp.inf, 0.0, top)
    return top + jnp.log(jnp.sum(jnp.exp(parts - base[None]), axis=0))


def spread(values, norm_ref):
    high, low = jnp.max(values), jnp.min(values)
    reach = GAIN * jnp.sqrt(jnp.max(norm_ref[0:8]) * jnp.max(norm_ref[8:16]))
    return 0.5 * high + 0.5 * low, 0.5 * high - 0.5 * low + reach <= SPAN


def diagonal():
    return lax.broadcasted_iota(jnp.int32, (TILE, TILE), 0) == lax.broadcasted_iota(
        jnp.int32, (TILE, TILE), 1
    )


def products(x, y):
    return GAIN * jnp.dot(x, y, preferred_element_type=jnp.float32)


def item_at(item_ref, w):
    return tuple(item_ref[8 + 8 * w + k] for k in range(7))


def exps(xa_ref, xb_ref, y_ref, ia, ib, r0, r1):
    x = jnp.concatenate([xa_ref[ia], xb_ref[ib]], axis=0)
    return jnp.exp(products(x, jnp.concatenate([y_ref[r0], y_ref[r1]], axis=1)))


def rescale(old, new):
    return jnp.where(old == new, 1.0, jnp.exp(old - new))


def row_kernel(
    combine, item_ref, xa_ref, xb_ref, y_ref, norm_ref, a_ref, lb_ref, out_ref, a_buf, u_buf, acc, top
):
    if combine:
        a = lb_ref[...] - lse_over_first(a_ref[...])
    else:
        a = a_ref[...]
    mid, fast = spread(a, norm_ref)
    n_items = item_ref[0]
    eye = diagonal()

    acc[...] = jnp.zeros_like(acc)

    @pl.when(fast)
    def _():
        u_buf[0:TILES] = jnp.exp(a - mid)
        u_buf[TILES:] = jnp.zeros((8, TILE), jnp.float32)

        def step(w, _):
            for h in range(UNROLL):
                s, ia, ib, t0, t1, r0, r1 = item_at(item_ref, UNROLL * w + h)
                e = exps(xa_ref, xb_ref, y_ref, ia, ib, r0, r1)
                acc[s] += (
                    e[:, :TILE] * u_buf[pl.ds(t0, 1), :] + e[:, TILE:] * u_buf[pl.ds(t1, 1), :]
                )
            return 0

        lax.fori_loop(0, lax.div(n_items + UNROLL - 1, UNROLL), step, 0)
        for k in range(N_ROWS * SUBS):
            s, b = k // SUBS, k % SUBS
            col = jnp.sum(acc[s, b * TILE : (b + 1) * TILE, :], axis=1, keepdims=True)
            done = mid + jnp.log(jnp.sum(jnp.where(eye, col, 0.0), axis=0, keepdims=True))
            out_ref[:, k : k + 1, :] = jnp.broadcast_to(done[None], (N_ROWS, 1, TILE))

    @pl.when(jnp.logical_not(fast))
    def _():
        a_buf[0:TILES] = a
        a_buf[TILES:] = jnp.zeros((8, TILE), jnp.float32)
        top[...] = jnp.full_like(top, -jnp.inf)

        def step(w, _):
            s, ia, ib, t0, t1, r0, r1 = item_at(item_ref, w)
            for t, r in ((t0, r0), (t1, r1)):

                @pl.when(t < TILES)
                def _(t=t, r=r):
                    x = jnp.concatenate([xa_ref[ia], xb_ref[ib]], axis=0)
                    score = products(x, y_ref[r]) + a_buf[pl.ds(t, 1), :]
                    old = top[s]
                    new = jnp.maximum(old, score)
                    acc[s] = acc[s] * rescale(old, new) + jnp.exp(score - new)
                    top[s] = new

            return 0

        lax.fori_loop(0, n_items, step, 0)

        def finish(k, _):
            s, b = lax.div(k, SUBS), lax.rem(k, SUBS)
            rows = pl.ds(pl.multiple_of(b * TILE, TILE), TILE)
            block = top[s, rows, :]
            high = jnp.max(block, axis=1, keepdims=True)
            base = jnp.where(high == -jnp.inf, 0.0, high)
            total = jnp.sum(acc[s, rows, :] * jnp.exp(block - base), axis=1, keepdims=True)
            high_row = jnp.max(jnp.where(eye, high, -jnp.inf), axis=0, keepdims=True)
            total_row = jnp.sum(jnp.where(eye, total, 0.0), axis=0, keepdims=True)
            done = high_row + jnp.log(total_row)
            out_ref[:, pl.ds(k, 1), :] = jnp.broadcast_to(done[None], (N_ROWS, 1, TILE))
            return 0

        lax.fori_loop(0, N_ROWS * SUBS, finish, 0)


def col_kernel(
    item_ref, xa_ref, xb_ref, y_ref, norm_ref, parts_ref, la_ref, out_ref, b_ref, spread_buf, acc, top
):
    b = la_ref[...] - lse_over_first(parts_ref[...])
    b_ref[...] = b
    mid, fast = spread(b, norm_ref)
    n_items = item_ref[0]
    eye = diagonal()

    def lay_out(values):
        for k in range(N_ROWS * SUBS):
            s, part = k // SUBS, k % SUBS
            row = values[k : k + 1, :]
            col = jnp.sum(jnp.where(eye, row, 0.0), axis=1, keepdims=True)
            spread_buf[s, part * TILE : (part + 1) * TILE, :] = jnp.broadcast_to(col, (TILE, TILE))

    acc[...] = jnp.zeros_like(acc)

    @pl.when(fast)
    def _():
        lay_out(jnp.exp(b - mid))

        def step(w, _):
            for h in range(UNROLL):
                s, ia, ib, t0, t1, r0, r1 = item_at(item_ref, UNROLL * w + h)
                e = exps(xa_ref, xb_ref, y_ref, ia, ib, r0, r1)
                v = spread_buf[s]
                acc[t0] += jnp.sum((e[:, :TILE] * v).reshape(SRC // 8, 8, TILE), axis=0)
                acc[t1] += jnp.sum((e[:, TILE:] * v).reshape(SRC // 8, 8, TILE), axis=0)
            return 0

        lax.fori_loop(0, lax.div(n_items + UNROLL - 1, UNROLL), step, 0)
        done = mid + jnp.log(jnp.sum(acc[0:TILES], axis=1))
        out_ref[...] = jnp.broadcast_to(done[None], out_ref.shape)

    @pl.when(jnp.logical_not(fast))
    def _():
        lay_out(b)
        top[...] = jnp.full_like(top, -jnp.inf)

        def step(w, _):
            s, ia, ib, t0, t1, r0, r1 = item_at(item_ref, w)
            for t, r in ((t0, r0), (t1, r1)):

                @pl.when(t < TILES)
                def _(t=t, r=r):
                    x = jnp.concatenate([xa_ref[ia], xb_ref[ib]], axis=0)
                    score = products(x, y_ref[r]) + spread_buf[s]
                    score = score.reshape(SRC // 8, 8, TILE)
                    old = top[t]
                    new = jnp.maximum(old, jnp.max(score, axis=0))
                    acc[t] = acc[t] * rescale(old, new) + jnp.sum(
                        jnp.exp(score - new[None]), axis=0
                    )
                    top[t] = new

            return 0

        lax.fori_loop(0, n_items, step, 0)
        high = jnp.max(top[0:TILES], axis=1)
        base = jnp.where(high == -jnp.inf, 0.0, high)
        total = jnp.sum(acc[0:TILES] * jnp.exp(top[0:TILES] - base[:, None, :]), axis=1)
        out_ref[...] = jnp.broadcast_to((high + jnp.log(total))[None], out_ref.shape)


VMEM = pl.BlockSpec(memory_space=pltpu.VMEM)
SMEM = pl.BlockSpec(memory_space=pltpu.SMEM)
LIMIT = pltpu.CompilerParams(vmem_limit_bytes=40 * 1024 * 1024)


def row_pass(items, xa, xb, ys, norms, a, lb, combine):
    return pl.pallas_call(
        functools.partial(row_kernel, combine),
        out_shape=jax.ShapeDtypeStruct((N_ROWS, N_ROWS * SUBS, TILE), jnp.float32),
        in_specs=[SMEM] + [VMEM] * 6,
        out_specs=VMEM,
        scratch_shapes=[
            pltpu.VMEM((TILES + 8, TILE), jnp.float32),
            pltpu.VMEM((TILES + 8, TILE), jnp.float32),
            pltpu.VMEM((N_ROWS, SRC, TILE), jnp.float32),
            pltpu.VMEM((N_ROWS, SRC, TILE), jnp.float32),
        ],
        compiler_params=LIMIT,
        name="row_pass",
    )(items, xa, xb, ys, norms, a, lb)


def col_pass(items, xa, xb, ys, norms, parts, la, copies):
    return pl.pallas_call(
        col_kernel,
        out_shape=(
            jax.ShapeDtypeStruct((copies, TILES, TILE), jnp.float32),
            jax.ShapeDtypeStruct((N_ROWS * SUBS, TILE), jnp.float32),
        ),
        in_specs=[SMEM] + [VMEM] * 6,
        out_specs=(VMEM, VMEM),
        scratch_shapes=[
            pltpu.VMEM((N_ROWS, SRC, TILE), jnp.float32),
            pltpu.VMEM((TILES + 1, 8, TILE), jnp.float32),
            pltpu.VMEM((TILES + 1, 8, TILE), jnp.float32),
        ],
        compiler_params=LIMIT,
        name="col_pass",
    )(items, xa, xb, ys, norms, parts, la)


def swap(blocks, axes):
    return lax.all_to_all(blocks, axes, split_axis=0, concat_axis=0, tiled=True)


def fetch(block, axis, ahead):
    size = 2 if axis == "core" else RING
    return lax.ppermute(block, axis, [((k + ahead) % size, k) for k in range(size)])


def gather_ring(block, axis):
    return [block] + [fetch(block, axis, ahead) for ahead in range(1, RING)]


def gather_sources(points):
    first, second = points[:HALF], points[HALF:]
    first = jnp.concatenate(gather_ring(first, "y"))
    second = jnp.concatenate(gather_ring(second, "z"))
    first = jnp.concatenate(gather_ring(first, "z")).reshape(N_ROWS, HALF, FEAT)
    second = jnp.concatenate(gather_ring(second, "y")).reshape(N_ROWS, HALF, FEAT)
    return first, second


def gather_targets(points):
    near = gather_ring(points, "x")
    far = [fetch(block, "core", 1) for block in near]
    return jnp.concatenate(near + far)


def work_items(ids, counts):
    slot = jnp.arange(CAP, dtype=jnp.int32)
    valid = (slot[None, None, :] < counts[:, :, None]).reshape(N_ROWS, N_COLS * CAP)
    tile = (ids + TSUB * jnp.arange(N_COLS, dtype=jnp.int32)[None, :, None]).reshape(
        N_ROWS, N_COLS * CAP
    )
    place = jnp.cumsum(valid.astype(jnp.int32), axis=1) - 1
    filled = jnp.sum(valid.astype(jnp.int32), axis=1)
    width = (filled + 1) // 2
    start = jnp.cumsum(width) - width
    total = jnp.sum(width)
    position = 2 * start[:, None] + place
    room = ITEMS + 8
    want = jnp.arange(2 * room, dtype=jnp.int32)
    hit = valid[None] & (position[None] == want[:, None, None])
    tiles = TILES + jnp.sum(jnp.where(hit, tile[None] - TILES, 0), axis=(1, 2))
    order = jnp.arange(room, dtype=jnp.int32)
    block = jnp.sum((order[:, None] >= (start + width)[None, :]).astype(jnp.int32), axis=1)
    block = jnp.minimum(block, N_ROWS - 1)
    along = {name: lax.axis_index(name) for name in NAMES}
    ky, kz = (block // RING - along["y"]) % RING, (block % RING - along["z"]) % RING
    owner, sub = tiles % TILES // TSUB, tiles % TSUB
    kx, kc = (owner // 2 - along["x"]) % RING, (owner % 2 - along["core"]) % 2
    held = ((kc * RING + kx) * TSUB + sub).reshape(room, 2)
    tiles = tiles.reshape(room, 2)
    listed = jnp.concatenate(
        [jnp.stack([block, kz * RING + ky, ky * RING + kz], axis=1), tiles, held, held[:, :1]],
        axis=1,
    ).reshape(-1)
    return jnp.concatenate([jnp.full((8,), total, jnp.int32), listed.astype(jnp.int32)])


def body(
    source_points, target_points, source_mass, target_mass, target_init, pair_tiles, pair_count
):
    unit = 1.0 / (FEAT * EPSILON)
    source_norm = jnp.sum(jnp.square(source_points.astype(jnp.float32)), axis=-1)
    target_norm = jnp.sum(jnp.square(target_points.astype(jnp.float32)), axis=-1)
    log_source = jnp.log(source_mass)
    log_target = jnp.log(target_mass)

    asked = jnp.concatenate([pair_tiles, pair_count[:, None]], axis=1).reshape(*DIMS, CAP + 1)
    asked = asked.transpose(1, 2, 0, 3, 4).reshape(N_ROWS, N_COLS * (CAP + 1))
    own = jnp.concatenate([log_source, jnp.full((8,), jnp.max(source_norm))])
    sent = jnp.concatenate(
        [asked.astype(jnp.float32), jnp.broadcast_to(own[None], (N_ROWS, SRC + 8))], axis=1
    )
    got = swap(sent, ROWS)
    wide = N_COLS * (CAP + 1)
    pairs = got[:, :wide].astype(jnp.int32).reshape(N_ROWS, N_COLS, CAP + 1)
    la = got[:, wide : wide + SRC].reshape(N_ROWS * SUBS, TILE)
    items = work_items(pairs[:, :, :CAP], pairs[:, :, CAP])

    first = jnp.concatenate(
        [
            target_init / EPSILON - target_norm * unit,
            log_target,
            jnp.full((TILE,), jnp.max(target_norm)),
        ]
    )
    firsts = swap(jnp.broadcast_to(first[None], (N_COLS,) + first.shape), COLS)
    n_targets = TSUB * TILE
    a0 = firsts[:, :n_targets].reshape(TILES, TILE)
    lb = firsts[:, n_targets : 2 * n_targets].reshape(TILES, TILE)
    norms = jnp.concatenate(
        [
            jnp.full((8, TILE), jnp.max(got[:, wide + SRC :])),
            jnp.full((8, TILE), jnp.max(firsts[:, 2 * n_targets :])),
        ]
    )

    ys = gather_targets(target_points.reshape(TSUB, TILE, FEAT).transpose(0, 2, 1))
    xa, xb = gather_sources(source_points)
    held = (items, xa, xb, ys, norms)

    row_parts = row_pass(*held, a0, lb, False)
    for iteration in range(ITERS):
        final = iteration == ITERS - 1
        col_parts, b = col_pass(*held, swap(row_parts, ROWS), la, 1 if final else N_COLS)
        if not final:
            row_parts = row_pass(*held, swap(col_parts, COLS), lb, True)
    here = lax.axis_index(ROWS)
    b_here = lax.dynamic_slice_in_dim(b, here * SUBS, SUBS).reshape(SRC)
    source_pot = EPSILON * (b_here + source_norm * unit)
    last = swap(col_parts.reshape(N_COLS, n_targets), COLS)
    target_pot = EPSILON * (log_target - lse_over_first(last) + target_norm * unit)
    return (source_pot, target_pot)


def solution(mesh):
    grid = Mesh(mesh.devices.reshape(DIMS), NAMES)
    placed = (
        P(NAMES, None),
        P(NAMES, None),
        P(NAMES),
        P(NAMES),
        P(NAMES),
        P(NAMES, None),
        P(NAMES),
    )
    return jax.shard_map(
        body, mesh=grid, in_specs=placed, out_specs=(P(NAMES), P(NAMES)), check_vma=False
    )
```

```python
import functools
import math

import jax
import jax.numpy as jnp
import numpy as np
from jax import lax
from jax.experimental import pallas as pl
from jax.experimental.pallas import tpu as pltpu
from jax.sharding import Mesh
from jax.sharding import PartitionSpec as P

TSUB = 8
CAP = 2
ITERS = 2
EPSILON = 0.1

DIMS = (4, 4, 4, 2)
NAMES = ("x", "y", "z", "core")
ROWS = ("y", "z")
COLS = ("x", "core")
N_ROWS = 16
N_COLS = 8
RING = 4
SRC = 384
TILE = 128
SUBS = SRC // TILE
FEAT = 256
TILES = N_COLS * TSUB
SLOTS = N_ROWS * N_COLS * CAP
UNROLL = 4
EXTRA = 16
LISTED = 8 + SLOTS + 4 * UNROLL
NOTHING = TILES << 8
GAIN = 2.0 / (FEAT * EPSILON)
UNIT = 1.0 / (FEAT * EPSILON)
LOG2E = math.log2(math.e)
SPAN = 70.0


def lse_over_first(parts):
    top = jnp.max(parts, axis=0)
    base = jnp.where(top == -jnp.inf, 0.0, top)
    return top + jnp.log(jnp.sum(jnp.exp(parts - base[None]), axis=0))


def spread(values, norm_ref):
    high, low = jnp.max(values), jnp.min(values)
    reach = GAIN * jnp.sqrt(jnp.max(norm_ref[0:8]) * jnp.max(norm_ref[8:16]))
    return 0.5 * high + 0.5 * low, 0.5 * high - 0.5 * low + reach <= SPAN


def diagonal():
    return lax.broadcasted_iota(jnp.int32, (TILE, TILE), 0) == lax.broadcasted_iota(
        jnp.int32, (TILE, TILE), 1
    )


def as_row(eye, col):
    return jnp.sum(jnp.where(eye, col, 0.0), axis=0, keepdims=True)


def as_col(eye, row):
    return jnp.sum(jnp.where(eye, row, 0.0), axis=1, keepdims=True)


def products(x, y):
    return jnp.dot(x, y, preferred_element_type=jnp.float32)


def item_at(item_ref, w):
    one, two = item_ref[8 + 2 * w], item_ref[9 + 2 * w]
    return (
        one >> 20,
        (one >> 16) & 15,
        (one >> 8) & 255,
        (two >> 8) & 255,
        one & 255,
        two & 255,
    )


def exps(x_ref, y_ref, h, r0, r1):
    y = jnp.concatenate([y_ref[r0], y_ref[r1]], axis=1)
    return jnp.exp2((GAIN * LOG2E) * products(x_ref[h], y))


def rescale(old, new):
    return jnp.where(old == new, 1.0, jnp.exp(old - new))


def split(values):
    high = values.astype(jnp.bfloat16).astype(jnp.float32)
    rest = values - high
    middle = rest.astype(jnp.bfloat16).astype(jnp.float32)
    return [high, middle, (rest - middle).astype(jnp.bfloat16).astype(jnp.float32)]


def start_all(pairs, sems):
    copies = [pltpu.make_async_copy(src, dst, sems.at[k]) for k, (src, dst) in enumerate(pairs)]
    for copy in copies:
        copy.start()
    return copies


def prepare_kernel(*refs):
    xo_ref, yo_ref, nx_ref, ny_ref, lb_ref = refs[7:12]
    y_ref, mass_ref, goal_ref, init_ref, tile_ref, count_ref, sems = refs[12:]
    copies = start_all(
        zip(refs[:7], (xo_ref.at[0:SRC], y_ref, mass_ref, goal_ref, init_ref, tile_ref, count_ref)),
        sems,
    )
    eye = diagonal()
    for copy in copies[2:]:
        copy.wait()
    la = jnp.log(mass_ref[...])
    lb = jnp.log(goal_ref[...])
    lb_ref[...] = lb

    copies[0].wait()
    norms = []
    for b in range(SUBS):
        x = xo_ref[b * TILE : (b + 1) * TILE, :].astype(jnp.float32)
        norms.append(as_row(eye, jnp.sum(x * x, axis=1, keepdims=True)))
    nx = jnp.concatenate(norms, axis=0)
    nx_ref[...] = nx
    bound = jnp.full((1, TILE), 1.01 * jnp.max(nx))
    left = split(la) + [bound, jnp.zeros((EXTRA - 10, TILE), jnp.float32)]
    right = [
        tile_ref[...].astype(jnp.float32),
        count_ref[...].astype(jnp.float32),
        jnp.zeros((EXTRA - 3, TILE), jnp.float32),
    ]
    extra = jnp.concatenate(
        [jnp.concatenate(left, axis=0), jnp.concatenate(right, axis=0)], axis=1
    )
    xo_ref[SRC:] = extra.astype(jnp.bfloat16)

    copies[1].wait()
    norms = []
    for t in range(TSUB):
        y = y_ref[t * TILE : (t + 1) * TILE, :].astype(jnp.float32).T
        norms.append(jnp.sum(y * y, axis=0, keepdims=True))
        yo_ref[t, 0:FEAT] = y.astype(jnp.bfloat16)
    ny = jnp.concatenate(norms, axis=0)
    ny_ref[...] = ny
    a0 = init_ref[...] / EPSILON - ny * UNIT
    parts = split(a0) + split(lb)
    bound = jnp.full((1, TILE), 1.01 * jnp.max(ny))
    for t in range(TSUB):
        rows = [part[t : t + 1] for part in parts]
        rows += [bound, jnp.zeros((EXTRA - 7, TILE), jnp.float32)]
        yo_ref[t, FEAT:] = jnp.concatenate(rows, axis=0).astype(jnp.bfloat16)


def gray(k):
    return k ^ (k >> 1)


def ring_place(offset, first):
    place = gray(offset)
    other = ((place & 1) << 1) | (place >> 1)
    return jnp.where(first == 0, place, other)


def assemble_kernel(*refs):
    at_ref = refs[0]
    x_refs, y_refs = refs[1 : 1 + 2 * RING], refs[1 + 2 * RING : 1 + 4 * RING]
    item_ref, xs_ref, ys_ref, la_ref, a_ref, lb_ref, norm_ref = refs[1 + 4 * RING : 8 + 4 * RING]
    table, numbers, x_extra, y_extra, sems, sem = refs[8 + 4 * RING :]
    x, y, z, core = (at_ref[k] for k in range(4))

    small, large = [], []
    for half in range(2):
        for later in range(RING):
            piece = x_refs[RING * half + later]
            place = pl.ds(RING * later + 2 * half, 2)
            small.append((piece.at[:, SRC:, :], x_extra.at[place]))
            large.append((piece.at[:, 0:SRC, :], xs_ref.at[place]))
    for k, piece in enumerate(y_refs):
        place = pl.ds(TSUB * k, TSUB)
        small.append((piece.at[:, FEAT:, :], y_extra.at[place]))
        large.append((piece.at[:, 0:FEAT, :], ys_ref.at[place]))
    copies = start_all(small + large, sems)
    for copy in copies[: len(small)]:
        copy.wait()

    bound = None
    for later in range(RING):
        for sooner in range(RING):
            one, two = gray(sooner), gray(later)
            off_y = jnp.where(core == 0, one, two)
            off_z = jnp.where(core == 0, two, one)
            s = RING * (y ^ off_y) + (z ^ off_z)
            extra = x_extra[RING * later + sooner].astype(jnp.float32)
            la = extra[0:3, :TILE] + extra[3:6, :TILE] + extra[6:9, :TILE]
            for b in range(SUBS):
                la_ref[pl.ds(SUBS * s + b, 1), :] = la[b : b + 1]
            here = extra[9:10, :TILE]
            bound = here if bound is None else jnp.maximum(bound, here)
            table[s] = extra[0:8, TILE:].astype(jnp.int32)
    norm_ref[0:8] = jnp.broadcast_to(bound, (8, TILE))

    copy = pltpu.make_async_copy(table, numbers, sem)
    copy.start()

    bound = None
    for k in range(2 * RING):
        side = core ^ (k // RING)
        place = k % RING
        offset = jnp.where(side == 0, gray(place), (0, 3, 1, 2)[place])
        owner = 2 * (x ^ offset) + side
        extra = y_extra[TSUB * k : TSUB * (k + 1)].astype(jnp.float32)
        rows = pl.ds(pl.multiple_of(TSUB * owner, TSUB), TSUB)
        a_ref[rows, :] = extra[:, 0] + extra[:, 1] + extra[:, 2]
        lb_ref[rows, :] = extra[:, 3] + extra[:, 4] + extra[:, 5]
        here = extra[0, 6:7]
        bound = here if bound is None else jnp.maximum(bound, here)
    norm_ref[8:16] = jnp.broadcast_to(bound, (8, TILE))

    copy.wait()
    lanes, starts = [], []
    for owner in range(N_COLS):
        px, side = owner // 2, owner % 2
        lanes.append(2 * (RING * RING * px + RING * y + z) + side)
        starts.append(TSUB * (RING * (side ^ core) + ring_place(px ^ x, side)))

    def block(s, place):
        off_y, off_z = (s >> 2) ^ y, (s & 3) ^ z
        sooner = jnp.where(core == 0, off_y, off_z)
        later = jnp.where(core == 0, off_z, off_y)
        head = (s << 20) | ((RING * gray(later) + gray(sooner)) << 16)
        for owner in range(N_COLS):
            count = numbers[s, 2, lanes[owner]]
            for e in range(CAP):
                tile = numbers[s, e, lanes[owner]]
                item_ref[place] = head | ((TSUB * owner + tile) << 8) | (starts[owner] + tile)
                place = place + jnp.where(e < count, 1, 0)
        item_ref[place] = head | NOTHING
        return place + (place & 1)

    end = lax.fori_loop(0, N_ROWS, block, jnp.int32(8))
    for k in range(2 * UNROLL):
        item_ref[end + k] = jnp.int32(NOTHING)
    item_ref[0] = (end - 8) >> 1
    for copy in copies[len(small) :]:
        copy.wait()


def row_kernel(
    combine, item_ref, x_ref, y_ref, norm_ref, a_ref, lb_ref, out_ref, a_buf, u_buf, acc, top
):
    if combine:
        a = lb_ref[...] - lse_over_first(a_ref[...])
    else:
        a = a_ref[...]
    mid, fast = spread(a, norm_ref)
    n_items = item_ref[0]
    eye = diagonal()

    acc[...] = jnp.zeros_like(acc)

    @pl.when(fast)
    def _():
        u_buf[0:TILES] = jnp.exp(a - mid)
        u_buf[TILES:] = jnp.zeros((8, TILE), jnp.float32)

        def step(w, _):
            for k in range(UNROLL):
                s, h, t0, t1, r0, r1 = item_at(item_ref, UNROLL * w + k)
                e = exps(x_ref, y_ref, h, r0, r1)
                acc[s] += (
                    e[:, :TILE] * u_buf[pl.ds(t0, 1), :] + e[:, TILE:] * u_buf[pl.ds(t1, 1), :]
                )
            return 0

        lax.fori_loop(0, lax.div(n_items + UNROLL - 1, UNROLL), step, 0)
        for k in range(N_ROWS * SUBS):
            s, b = k // SUBS, k % SUBS
            col = jnp.sum(acc[s, b * TILE : (b + 1) * TILE, :], axis=1, keepdims=True)
            done = mid + jnp.log(as_row(eye, col))
            out_ref[:, k : k + 1, :] = jnp.broadcast_to(done[None], (N_ROWS, 1, TILE))

    @pl.when(jnp.logical_not(fast))
    def _():
        a_buf[0:TILES] = a
        a_buf[TILES:] = jnp.zeros((8, TILE), jnp.float32)
        top[...] = jnp.full_like(top, -jnp.inf)

        def step(w, _):
            s, h, t0, t1, r0, r1 = item_at(item_ref, w)
            for t, r in ((t0, r0), (t1, r1)):

                @pl.when(t < TILES)
                def _(t=t, r=r):
                    score = GAIN * products(x_ref[h], y_ref[r]) + a_buf[pl.ds(t, 1), :]
                    old = top[s]
                    new = jnp.maximum(old, score)
                    acc[s] = acc[s] * rescale(old, new) + jnp.exp(score - new)
                    top[s] = new

            return 0

        lax.fori_loop(0, n_items, step, 0)

        def finish(k, _):
            s, b = lax.div(k, SUBS), lax.rem(k, SUBS)
            rows = pl.ds(pl.multiple_of(b * TILE, TILE), TILE)
            block = top[s, rows, :]
            high = jnp.max(block, axis=1, keepdims=True)
            base = jnp.where(high == -jnp.inf, 0.0, high)
            total = jnp.sum(acc[s, rows, :] * jnp.exp(block - base), axis=1, keepdims=True)
            high_row = jnp.max(jnp.where(eye, high, -jnp.inf), axis=0, keepdims=True)
            done = high_row + jnp.log(as_row(eye, total))
            out_ref[:, pl.ds(k, 1), :] = jnp.broadcast_to(done[None], (N_ROWS, 1, TILE))
            return 0

        lax.fori_loop(0, N_ROWS * SUBS, finish, 0)


def col_kernel(
    item_ref, x_ref, y_ref, norm_ref, parts_ref, la_ref, out_ref, b_ref, spread_buf, acc, top
):
    b = la_ref[...] - lse_over_first(parts_ref[...])
    b_ref[...] = b
    mid, fast = spread(b, norm_ref)
    n_items = item_ref[0]
    eye = diagonal()

    def lay_out(values):
        for k in range(N_ROWS * SUBS):
            s, part = k // SUBS, k % SUBS
            col = as_col(eye, values[k : k + 1, :])
            spread_buf[s, part * TILE : (part + 1) * TILE, :] = jnp.broadcast_to(col, (TILE, TILE))

    acc[...] = jnp.zeros_like(acc)

    @pl.when(fast)
    def _():
        lay_out(jnp.exp(b - mid))

        def step(w, _):
            for k in range(UNROLL):
                s, h, t0, t1, r0, r1 = item_at(item_ref, UNROLL * w + k)
                e = exps(x_ref, y_ref, h, r0, r1)
                v = spread_buf[s]
                acc[t0] += jnp.sum((e[:, :TILE] * v).reshape(SRC // 8, 8, TILE), axis=0)
                acc[t1] += jnp.sum((e[:, TILE:] * v).reshape(SRC // 8, 8, TILE), axis=0)
            return 0

        lax.fori_loop(0, lax.div(n_items + UNROLL - 1, UNROLL), step, 0)
        done = mid + jnp.log(jnp.sum(acc[0:TILES], axis=1))
        out_ref[...] = jnp.broadcast_to(done[None], out_ref.shape)

    @pl.when(jnp.logical_not(fast))
    def _():
        lay_out(b)
        top[...] = jnp.full_like(top, -jnp.inf)

        def step(w, _):
            s, h, t0, t1, r0, r1 = item_at(item_ref, w)
            for t, r in ((t0, r0), (t1, r1)):

                @pl.when(t < TILES)
                def _(t=t, r=r):
                    score = GAIN * products(x_ref[h], y_ref[r]) + spread_buf[s]
                    score = score.reshape(SRC // 8, 8, TILE)
                    old = top[t]
                    new = jnp.maximum(old, jnp.max(score, axis=0))
                    acc[t] = acc[t] * rescale(old, new) + jnp.sum(
                        jnp.exp(score - new[None]), axis=0
                    )
                    top[t] = new

            return 0

        lax.fori_loop(0, n_items, step, 0)
        high = jnp.max(top[0:TILES], axis=1)
        base = jnp.where(high == -jnp.inf, 0.0, high)
        total = jnp.sum(acc[0:TILES] * jnp.exp(top[0:TILES] - base[:, None, :]), axis=1)
        out_ref[...] = jnp.broadcast_to((high + jnp.log(total))[None], out_ref.shape)


VMEM = pl.BlockSpec(memory_space=pltpu.VMEM)
ANY = pl.BlockSpec(memory_space=pl.ANY)
SMEM = pl.BlockSpec(memory_space=pltpu.SMEM)


def limit(mebibytes):
    return pltpu.CompilerParams(vmem_limit_bytes=mebibytes * 1024 * 1024)


def shape(dims, dtype=jnp.float32):
    return jax.ShapeDtypeStruct(dims, dtype)


def prepare(*operands):
    return pl.pallas_call(
        prepare_kernel,
        out_shape=(
            shape((SRC + EXTRA, FEAT), jnp.bfloat16),
            shape((TSUB, FEAT + EXTRA, TILE), jnp.bfloat16),
            shape((SUBS, TILE)),
            shape((TSUB, TILE)),
            shape((TSUB, TILE)),
        ),
        in_specs=[ANY] * 7,
        out_specs=(VMEM,) * 5,
        scratch_shapes=[
            pltpu.VMEM((TSUB * TILE, FEAT), jnp.bfloat16),
            pltpu.VMEM((SUBS, TILE), jnp.float32),
            pltpu.VMEM((TSUB, TILE), jnp.float32),
            pltpu.VMEM((TSUB, TILE), jnp.float32),
            pltpu.VMEM((CAP, TILE), jnp.int32),
            pltpu.VMEM((1, TILE), jnp.int32),
            pltpu.SemaphoreType.DMA((7,)),
        ],
        compiler_params=limit(60),
        name="prepare",
    )(*operands)


def assemble(at, xs, ys):
    return pl.pallas_call(
        assemble_kernel,
        out_shape=(
            shape((LISTED,), jnp.int32),
            shape((N_ROWS, SRC, FEAT), jnp.bfloat16),
            shape((TILES, FEAT, TILE), jnp.bfloat16),
            shape((N_ROWS * SUBS, TILE)),
            shape((TILES, TILE)),
            shape((TILES, TILE)),
            shape((16, TILE)),
        ),
        in_specs=[SMEM] + [ANY] * (len(xs) + len(ys)),
        out_specs=(SMEM,) + (VMEM,) * 6,
        scratch_shapes=[
            pltpu.VMEM((N_ROWS, 8, TILE), jnp.int32),
            pltpu.SMEM((N_ROWS, 8, TILE), jnp.int32),
            pltpu.VMEM((N_ROWS, EXTRA, FEAT), jnp.bfloat16),
            pltpu.VMEM((TILES, EXTRA, TILE), jnp.bfloat16),
            pltpu.SemaphoreType.DMA((8 * RING,)),
            pltpu.SemaphoreType.DMA,
        ],
        compiler_params=limit(24),
        name="assemble",
    )(at, *xs, *ys)


def row_pass(items, xs, ys, norms, a, lb, combine):
    return pl.pallas_call(
        functools.partial(row_kernel, combine),
        out_shape=shape((N_ROWS, N_ROWS * SUBS, TILE)),
        in_specs=[SMEM] + [VMEM] * 5,
        out_specs=VMEM,
        scratch_shapes=[
            pltpu.VMEM((TILES + 8, TILE), jnp.float32),
            pltpu.VMEM((TILES + 8, TILE), jnp.float32),
            pltpu.VMEM((N_ROWS, SRC, TILE), jnp.float32),
            pltpu.VMEM((N_ROWS, SRC, TILE), jnp.float32),
        ],
        compiler_params=limit(20),
        name="row_pass",
    )(items, xs, ys, norms, a, lb)


def col_pass(items, xs, ys, norms, parts, la, copies):
    return pl.pallas_call(
        col_kernel,
        out_shape=(shape((copies, TILES, TILE)), shape((N_ROWS * SUBS, TILE))),
        in_specs=[SMEM] + [VMEM] * 5,
        out_specs=(VMEM, VMEM),
        scratch_shapes=[
            pltpu.VMEM((N_ROWS, SRC, TILE), jnp.float32),
            pltpu.VMEM((TILES + 1, 8, TILE), jnp.float32),
            pltpu.VMEM((TILES + 1, 8, TILE), jnp.float32),
        ],
        compiler_params=limit(20),
        name="col_pass",
    )(items, xs, ys, norms, parts, la)


def swap(blocks, axes):
    return lax.all_to_all(blocks, axes, split_axis=0, concat_axis=0, tiled=True)


def exchange(block, partner):
    pairs = []
    for place in range(N_ROWS * N_COLS):
        at = tuple(int(k) for k in np.unravel_index(place, DIMS))
        pairs.append((place, int(np.ravel_multi_index(partner(*at), DIMS))))
    return lax.ppermute(block, NAMES, pairs)


def gather_ring(block, one, two):
    first, second = exchange(block, one), exchange(block, two)
    return [block, first, second, exchange(second, one)]


def gather_sources(block):
    one, two = source_partner(0, 1), source_partner(0, 3)
    first, second = exchange(block, one), exchange(block, two)
    opposite = exchange(second, one)
    one, two = source_partner(1, 1), source_partner(1, 3)
    pair = jnp.stack([block, first])
    pieces = gather_ring(pair, one, two)
    pair = jnp.stack([second, opposite])
    first, second = exchange(pair, one), exchange(pair, two)
    return pieces + [pair, first, second, exchange(first, two)]


def source_partner(stage, flip):
    def partner(x, y, z, core):
        return (x, y ^ flip, z, core) if stage == core else (x, y, z ^ flip, core)

    return partner


def target_partner(order):
    return lambda x, y, z, core: (x ^ (1, 3)[order ^ core], y, z, core)


def sibling(x, y, z, core):
    return (x, y, z, core ^ 1)


def body(
    source_points, target_points, source_mass, target_mass, target_init, pair_tiles, pair_count
):
    x_block, y_block, source_norm, target_norm, log_target = prepare(
        source_points,
        target_points,
        source_mass.reshape(SUBS, TILE),
        target_mass.reshape(TSUB, TILE),
        target_init.reshape(TSUB, TILE),
        pair_tiles.T,
        pair_count.reshape(1, -1),
    )
    xs = gather_sources(x_block)
    near = gather_ring(y_block, target_partner(0), target_partner(1))
    far = [exchange(block, sibling) for block in near]

    at = jnp.stack([lax.axis_index(name) for name in NAMES]).astype(jnp.int32)
    items, xs, ys, la, a0, lb, norms = assemble(at, xs, near + far)
    held = (items, xs, ys, norms)

    row_parts = row_pass(*held, a0, lb, False)
    for iteration in range(ITERS):
        final = iteration == ITERS - 1
        col_parts, b = col_pass(*held, swap(row_parts, ROWS), la, 1 if final else N_COLS)
        if not final:
            row_parts = row_pass(*held, swap(col_parts, COLS), lb, True)
    here = lax.axis_index(ROWS)
    b_here = lax.dynamic_slice_in_dim(b, here * SUBS, SUBS)
    source_pot = EPSILON * (b_here + source_norm * UNIT)
    last = swap(col_parts.reshape(N_COLS, TSUB, TILE), COLS)
    target_pot = EPSILON * (log_target - lse_over_first(last) + target_norm * UNIT)
    return (source_pot.reshape(-1), target_pot.reshape(-1))


def solution(mesh):
    grid = Mesh(mesh.devices.reshape(DIMS), NAMES)
    placed = (
        P(NAMES, None),
        P(NAMES, None),
        P(NAMES),
        P(NAMES),
        P(NAMES),
        P(NAMES, None),
        P(NAMES),
    )
    return jax.shard_map(
        body, mesh=grid, in_specs=placed, out_specs=(P(NAMES), P(NAMES)), check_vma=False
    )
```

```python
import functools
import math

import jax
import jax.numpy as jnp
import numpy as np
from jax import lax
from jax.experimental import pallas as pl
from jax.experimental.pallas import tpu as pltpu
from jax.sharding import Mesh
from jax.sharding import PartitionSpec as P

TSUB = 8
CAP = 2
ITERS = 2
EPSILON = 0.1

DIMS = (4, 4, 4, 2)
NAMES = ("x", "y", "z", "core")
ROWS = ("y", "z")
COLS = ("x", "core")
N_ROWS = 16
N_PIECES = 15
N_COLS = 8
RING = 4
SRC = 384
TILE = 128
SUBS = SRC // TILE
FEAT = 256
TILES = N_COLS * TSUB
SLOTS = N_ROWS * N_COLS * CAP
ROW_UNROLL = 8
COL_UNROLL = 16
LAST_UNROLL = 4
EXTRA = 16
LISTED = 8 + SLOTS + 4 * LAST_UNROLL
NOTHING = TILES << 8
NORMS = 16
GAIN = 2.0 / (FEAT * EPSILON)
UNIT = 1.0 / (FEAT * EPSILON)
LOG2E = math.log2(math.e)
SPAN = 70.0


def lse_over_first(parts):
    top = jnp.max(parts, axis=0)
    base = jnp.where(top == -jnp.inf, 0.0, top)
    return top + jnp.log(jnp.sum(jnp.exp(parts - base[None]), axis=0))


def spread(values, norm_ref):
    high, low = jnp.max(values), jnp.min(values)
    reach = GAIN * jnp.sqrt(jnp.max(norm_ref[0:8]) * jnp.max(norm_ref[8:16]))
    return 0.5 * high + 0.5 * low, 0.5 * high - 0.5 * low + reach <= SPAN


def diagonal():
    return lax.broadcasted_iota(jnp.int32, (TILE, TILE), 0) == lax.broadcasted_iota(
        jnp.int32, (TILE, TILE), 1
    )


def as_row(eye, col):
    return jnp.sum(jnp.where(eye, col, 0.0), axis=0, keepdims=True)


def as_col(eye, row):
    return jnp.sum(jnp.where(eye, row, 0.0), axis=1, keepdims=True)


def products(x, y):
    return jnp.dot(x, y, preferred_element_type=jnp.float32)


def item_at(item_ref, w):
    one, two = item_ref[8 + 2 * w], item_ref[9 + 2 * w]
    return (
        one >> 20,
        (one >> 16) & 15,
        (one >> 8) & 255,
        (two >> 8) & 255,
        one & 255,
        two & 255,
    )


def exps(x, y):
    return jnp.exp2((GAIN * LOG2E) * products(x, y))


def two_tiles(y_ref, r0, r1):
    return jnp.concatenate([y_ref[r0], y_ref[r1]], axis=1)


def sweep(n_items, work, many):
    def steps(first, size):
        def step(w, _):
            for k in range(size):
                work(first + size * w + k)
            return 0

        return step

    whole = lax.div(n_items, many)
    lax.fori_loop(0, whole, steps(0, many), 0)
    left = n_items - many * whole
    lax.fori_loop(
        0, lax.div(left + LAST_UNROLL - 1, LAST_UNROLL), steps(many * whole, LAST_UNROLL), 0
    )


def rescale(old, new):
    return jnp.where(old == new, 1.0, jnp.exp(old - new))


def split(values):
    high = values.astype(jnp.bfloat16).astype(jnp.float32)
    rest = values - high
    middle = rest.astype(jnp.bfloat16).astype(jnp.float32)
    return [high, middle, (rest - middle).astype(jnp.bfloat16).astype(jnp.float32)]


def start_all(pairs, sems):
    copies = [pltpu.make_async_copy(src, dst, sems.at[k]) for k, (src, dst) in enumerate(pairs)]
    for copy in copies:
        copy.start()
    return copies


def prepare_kernel(*refs):
    xo_ref, yo_ref, nx_ref, part_ref = refs[7:11]
    y_ref, mass_ref, goal_ref, init_ref, tile_ref, count_ref, sems = refs[11:]
    copies = start_all(
        zip(refs[:7], (xo_ref.at[0:SRC], y_ref, mass_ref, goal_ref, init_ref, tile_ref, count_ref)),
        sems,
    )
    eye = diagonal()
    for copy in copies[2:]:
        copy.wait()
    la = jnp.log(mass_ref[...])
    lb = jnp.log(goal_ref[...])

    copies[0].wait()
    norms = []
    for b in range(SUBS):
        x = xo_ref[b * TILE : (b + 1) * TILE, :].astype(jnp.float32)
        norms.append(as_row(eye, jnp.sum(x * x, axis=1, keepdims=True)))
    nx = jnp.concatenate(norms, axis=0)
    nx_ref[...] = nx
    bound = jnp.full((1, TILE), 1.01 * jnp.max(nx))
    left = split(la) + [bound, jnp.zeros((EXTRA - 10, TILE), jnp.float32)]
    right = [
        tile_ref[...].astype(jnp.float32),
        count_ref[...].astype(jnp.float32),
        jnp.zeros((EXTRA - 3, TILE), jnp.float32),
    ]
    extra = jnp.concatenate(
        [jnp.concatenate(left, axis=0), jnp.concatenate(right, axis=0)], axis=1
    )
    xo_ref[SRC:] = extra.astype(jnp.bfloat16)

    copies[1].wait()
    norms = []
    for t in range(TSUB):
        y = y_ref[t * TILE : (t + 1) * TILE, :].astype(jnp.float32).T
        norms.append(jnp.sum(y * y, axis=0, keepdims=True))
        yo_ref[t, 0:FEAT] = y.astype(jnp.bfloat16)
    ny = jnp.concatenate(norms, axis=0)
    part_ref[...] = EPSILON * (lb + UNIT * ny)
    a0 = init_ref[...] / EPSILON - ny * UNIT
    parts = split(a0) + split(lb)
    bound = jnp.full((1, TILE), 1.01 * jnp.max(ny))
    for t in range(TSUB):
        rows = [part[t : t + 1] for part in parts]
        rows += [bound, jnp.zeros((EXTRA - 7, TILE), jnp.float32)]
        yo_ref[t, FEAT:] = jnp.concatenate(rows, axis=0).astype(jnp.bfloat16)


def gray(k):
    return k ^ (k >> 1)


def ring_place(offset, first):
    place = gray(offset)
    other = ((place & 1) << 1) | (place >> 1)
    return jnp.where(first == 0, place, other)


def piece_copies(x_refs, y_refs, xs, ys, x_rows, y_rows):
    pairs = []
    for half in range(2):
        for later in range(RING):
            place = pl.ds(RING * later + 2 * half, 2)
            pairs.append((x_refs[RING * half + later].at[:, x_rows, :], xs.at[place]))
    start = 0
    for piece in y_refs:
        pairs.append((piece.at[:, y_rows, :], ys.at[pl.ds(start, piece.shape[0])]))
        start += piece.shape[0]
    return pairs


def first_kernel(*refs):
    at_ref, pieces = refs[0], refs[1 : 1 + N_PIECES]
    x_refs, y_refs = pieces[: 2 * RING], pieces[2 * RING :]
    out_ref, item_ref, cols_ref, rows_ref, xs_out, ys_out = refs[1 + N_PIECES : 7 + N_PIECES]
    a_buf, u_buf, acc, top, xs, ys, sems = refs[7 + N_PIECES : 14 + N_PIECES]
    a_ref, table, numbers, x_extra, y_extra, small_sems, sem, out_sems = refs[14 + N_PIECES :]
    la_ref, lb_ref = cols_ref.at[NORMS:], rows_ref.at[NORMS:]
    x, y, z, core = (at_ref[k] for k in range(4))

    small = start_all(
        piece_copies(
            x_refs, y_refs, x_extra, y_extra, slice(SRC, SRC + EXTRA), slice(FEAT, FEAT + EXTRA)
        ),
        small_sems,
    )
    large = start_all(
        piece_copies(x_refs, y_refs, xs, ys, slice(0, SRC), slice(0, FEAT)), sems
    )
    for copy in small:
        copy.wait()

    lane = lax.broadcasted_iota(jnp.int32, (CAP, TILE), 1)
    px, side = lane >> 5, lane & 1
    start = RING * (side ^ core) + ring_place(px ^ x, side)
    entry_base = ((TSUB * (2 * px + side)) << 8) + TSUB * start

    bound = None
    for later in range(RING):
        for sooner in range(RING):
            one, two = gray(sooner), gray(later)
            off_y = jnp.where(core == 0, one, two)
            off_z = jnp.where(core == 0, two, one)
            s = RING * (y ^ off_y) + (z ^ off_z)
            extra = x_extra[RING * later + sooner].astype(jnp.float32)
            la = extra[0:3, :TILE] + extra[3:6, :TILE] + extra[6:9, :TILE]
            for b in range(SUBS):
                la_ref[pl.ds(SUBS * s + b, 1), :] = la[b : b + 1]
            here = extra[9:10, :TILE]
            bound = here if bound is None else jnp.maximum(bound, here)
            numbers_here = extra[0:3, TILE:].astype(jnp.int32)
            head = (s << 20) | ((RING * later + sooner) << 16)
            entry = head | (entry_base + 257 * numbers_here[0:CAP])
            slot = lax.broadcasted_iota(jnp.int32, (CAP, TILE), 0)
            entry = jnp.where(slot < numbers_here[CAP : CAP + 1], entry, -1)
            table[pl.ds(s, 1)] = jnp.concatenate([entry, jnp.full((6, TILE), head)], axis=0)[None]
    for ref in (cols_ref, rows_ref):
        ref[0:8] = jnp.broadcast_to(bound, (8, TILE))

    copy = pltpu.make_async_copy(table, numbers, sem)
    copy.start()

    bound = None
    for k in range(2 * RING):
        side = core ^ (k // RING)
        place = k % RING
        offset = jnp.where(side == 0, gray(place), (0, 3, 1, 2)[place])
        owner = 2 * (x ^ offset) + side
        extra = y_extra[TSUB * k : TSUB * (k + 1)].astype(jnp.float32)
        rows = pl.ds(pl.multiple_of(TSUB * owner, TSUB), TSUB)
        a_ref[rows, :] = extra[:, 0] + extra[:, 1] + extra[:, 2]
        lb_ref[rows, :] = extra[:, 3] + extra[:, 4] + extra[:, 5]
        here = extra[0, 6:7]
        bound = here if bound is None else jnp.maximum(bound, here)
    for ref in (cols_ref, rows_ref):
        ref[8:16] = jnp.broadcast_to(bound, (8, TILE))

    copy.wait()
    lanes = [
        2 * (RING * RING * (owner // 2) + RING * y + z) + owner % 2 for owner in range(N_COLS)
    ]

    def block(s, place):
        for lane in lanes:
            for e in range(CAP):
                entry = numbers[s, e, lane]
                item_ref[place] = entry
                place = place + jnp.where(entry >= 0, 1, 0)
        item_ref[place] = numbers[s, CAP, 0] | NOTHING
        return place + (place & 1)

    end = lax.fori_loop(0, N_ROWS, block, jnp.int32(8))
    for k in range(2 * LAST_UNROLL):
        item_ref[end + k] = jnp.int32(NOTHING)
    item_ref[0] = (end - 8) >> 1
    item_ref[1] = RING * y + z
    for copy in large:
        copy.wait()
    outward = start_all([(xs, xs_out), (ys, ys_out)], out_sems)
    row_core(a_ref[...], item_ref, xs, ys, cols_ref, out_ref, a_buf, u_buf, acc, top)
    for copy in outward:
        copy.wait()


def row_kernel(item_ref, x_ref, y_ref, side_ref, parts_ref, out_ref, a_buf, u_buf, acc, top):
    a = side_ref[NORMS:] - lse_over_first(parts_ref[...])
    row_core(a, item_ref, x_ref, y_ref, side_ref, out_ref, a_buf, u_buf, acc, top)


def row_core(a, item_ref, x_ref, y_ref, norm_ref, out_ref, a_buf, u_buf, acc, top):
    mid, fast = spread(a, norm_ref)
    n_items = item_ref[0]
    eye = diagonal()

    acc[...] = jnp.zeros_like(acc)

    @pl.when(fast)
    def _():
        u_buf[0:TILES] = jnp.exp(a - mid)
        u_buf[TILES:] = jnp.zeros((8, TILE), jnp.float32)

        def work(w):
            s, h, t0, t1, r0, r1 = item_at(item_ref, w)
            u0, u1 = u_buf[pl.ds(t0, 1), :], u_buf[pl.ds(t1, 1), :]
            e = exps(x_ref[h], two_tiles(y_ref, r0, r1))
            acc[s] += e[:, :TILE] * u0 + e[:, TILE:] * u1

        sweep(n_items, work, ROW_UNROLL)
        for k in range(N_ROWS * SUBS):
            s, b = k // SUBS, k % SUBS
            col = jnp.sum(acc[s, b * TILE : (b + 1) * TILE, :], axis=1, keepdims=True)
            done = mid + jnp.log(as_row(eye, col))
            out_ref[:, k : k + 1, :] = jnp.broadcast_to(done[None], (N_ROWS, 1, TILE))

    @pl.when(jnp.logical_not(fast))
    def _():
        a_buf[0:TILES] = a
        a_buf[TILES:] = jnp.zeros((8, TILE), jnp.float32)
        top[...] = jnp.full_like(top, -jnp.inf)

        def step(w, _):
            s, h, t0, t1, r0, r1 = item_at(item_ref, w)
            for t, r in ((t0, r0), (t1, r1)):

                @pl.when(t < TILES)
                def _(t=t, r=r):
                    score = GAIN * products(x_ref[h], y_ref[r]) + a_buf[pl.ds(t, 1), :]
                    old = top[s]
                    new = jnp.maximum(old, score)
                    acc[s] = acc[s] * rescale(old, new) + jnp.exp(score - new)
                    top[s] = new

            return 0

        lax.fori_loop(0, n_items, step, 0)

        def finish(k, _):
            s, b = lax.div(k, SUBS), lax.rem(k, SUBS)
            rows = pl.ds(pl.multiple_of(b * TILE, TILE), TILE)
            block = top[s, rows, :]
            high = jnp.max(block, axis=1, keepdims=True)
            base = jnp.where(high == -jnp.inf, 0.0, high)
            total = jnp.sum(acc[s, rows, :] * jnp.exp(block - base), axis=1, keepdims=True)
            high_row = jnp.max(jnp.where(eye, high, -jnp.inf), axis=0, keepdims=True)
            done = high_row + jnp.log(as_row(eye, total))
            out_ref[:, pl.ds(k, 1), :] = jnp.broadcast_to(done[None], (N_ROWS, 1, TILE))
            return 0

        lax.fori_loop(0, N_ROWS * SUBS, finish, 0)


def last_col_kernel(
    item_ref, x_ref, y_ref, side_ref, parts_ref, norm_ref, out_ref, f_ref, b_buf, *scratch
):
    b = side_ref[NORMS:] - lse_over_first(parts_ref[...])
    b_buf[...] = b
    for k in range(SUBS):
        here = b_buf[pl.ds(SUBS * item_ref[1] + k, 1), :]
        f_ref[k : k + 1, :] = EPSILON * (here + UNIT * norm_ref[k : k + 1, :])
    col_core(b, item_ref, x_ref, y_ref, side_ref, out_ref, *scratch)


def col_kernel(item_ref, x_ref, y_ref, side_ref, parts_ref, out_ref, *scratch):
    b = side_ref[NORMS:] - lse_over_first(parts_ref[...])
    col_core(b, item_ref, x_ref, y_ref, side_ref, out_ref, *scratch)


def col_core(b, item_ref, x_ref, y_ref, norm_ref, out_ref, spread_buf, acc, top):
    mid, fast = spread(b, norm_ref)
    n_items = item_ref[0]
    eye = diagonal()

    def lay_out(values):
        for k in range(N_ROWS * SUBS):
            s, part = k // SUBS, k % SUBS
            col = as_col(eye, values[k : k + 1, :])
            spread_buf[s, part * TILE : (part + 1) * TILE, :] = jnp.broadcast_to(col, (TILE, TILE))

    acc[...] = jnp.zeros_like(acc)

    @pl.when(fast)
    def _():
        lay_out(jnp.exp(b - mid))

        def work(w):
            s, h, t0, t1, r0, r1 = item_at(item_ref, w)
            e = exps(x_ref[h], two_tiles(y_ref, r0, r1))
            v = spread_buf[s]
            acc[t0] += jnp.sum((e[:, :TILE] * v).reshape(SRC // 8, 8, TILE), axis=0)
            acc[t1] += jnp.sum((e[:, TILE:] * v).reshape(SRC // 8, 8, TILE), axis=0)

        sweep(n_items, work, COL_UNROLL)
        done = mid + jnp.log(jnp.sum(acc[0:TILES], axis=1))
        out_ref[...] = jnp.broadcast_to(done[None], out_ref.shape)

    @pl.when(jnp.logical_not(fast))
    def _():
        lay_out(b)
        top[...] = jnp.full_like(top, -jnp.inf)

        def step(w, _):
            s, h, t0, t1, r0, r1 = item_at(item_ref, w)
            for t, r in ((t0, r0), (t1, r1)):

                @pl.when(t < TILES)
                def _(t=t, r=r):
                    score = GAIN * products(x_ref[h], y_ref[r]) + spread_buf[s]
                    score = score.reshape(SRC // 8, 8, TILE)
                    old = top[t]
                    new = jnp.maximum(old, jnp.max(score, axis=0))
                    acc[t] = acc[t] * rescale(old, new) + jnp.sum(
                        jnp.exp(score - new[None]), axis=0
                    )
                    top[t] = new

            return 0

        lax.fori_loop(0, n_items, step, 0)
        high = jnp.max(top[0:TILES], axis=1)
        base = jnp.where(high == -jnp.inf, 0.0, high)
        total = jnp.sum(acc[0:TILES] * jnp.exp(top[0:TILES] - base[:, None, :]), axis=1)
        out_ref[...] = jnp.broadcast_to((high + jnp.log(total))[None], out_ref.shape)


VMEM = pl.BlockSpec(memory_space=pltpu.VMEM)
ANY = pl.BlockSpec(memory_space=pl.ANY)
SMEM = pl.BlockSpec(memory_space=pltpu.SMEM)


def limit(mebibytes):
    return pltpu.CompilerParams(vmem_limit_bytes=mebibytes * 1024 * 1024)


def shape(dims, dtype=jnp.float32):
    return jax.ShapeDtypeStruct(dims, dtype)


def prepare(*operands):
    return pl.pallas_call(
        prepare_kernel,
        out_shape=(
            shape((SRC + EXTRA, FEAT), jnp.bfloat16),
            shape((TSUB, FEAT + EXTRA, TILE), jnp.bfloat16),
            shape((SUBS, TILE)),
            shape((TSUB, TILE)),
        ),
        in_specs=[ANY] * 7,
        out_specs=(VMEM,) * 4,
        scratch_shapes=[
            pltpu.VMEM((TSUB * TILE, FEAT), jnp.bfloat16),
            pltpu.VMEM((SUBS, TILE), jnp.float32),
            pltpu.VMEM((TSUB, TILE), jnp.float32),
            pltpu.VMEM((TSUB, TILE), jnp.float32),
            pltpu.VMEM((CAP, TILE), jnp.int32),
            pltpu.VMEM((1, TILE), jnp.int32),
            pltpu.SemaphoreType.DMA((7,)),
        ],
        compiler_params=limit(60),
        name="prepare",
    )(*operands)


ROW_SCRATCH = [
    pltpu.VMEM((TILES + 8, TILE), jnp.float32),
    pltpu.VMEM((TILES + 8, TILE), jnp.float32),
    pltpu.VMEM((N_ROWS, SRC, TILE), jnp.float32),
    pltpu.VMEM((N_ROWS, SRC, TILE), jnp.float32),
]
COL_SCRATCH = [
    pltpu.VMEM((N_ROWS, SRC, TILE), jnp.float32),
    pltpu.VMEM((TILES + 1, 8, TILE), jnp.float32),
    pltpu.VMEM((TILES + 1, 8, TILE), jnp.float32),
]
ROW_PARTS = shape((N_ROWS, N_ROWS * SUBS, TILE))


def first_pass(at, pieces):
    return pl.pallas_call(
        first_kernel,
        out_shape=(
            ROW_PARTS,
            shape((LISTED,), jnp.int32),
            shape((NORMS + N_ROWS * SUBS, TILE)),
            shape((NORMS + TILES, TILE)),
            shape((N_ROWS, SRC, FEAT), jnp.bfloat16),
            shape((TILES, FEAT, TILE), jnp.bfloat16),
        ),
        in_specs=[SMEM] + [ANY] * N_PIECES,
        out_specs=(VMEM, SMEM, VMEM, VMEM, ANY, ANY),
        scratch_shapes=ROW_SCRATCH
        + [
            pltpu.VMEM((N_ROWS, SRC, FEAT), jnp.bfloat16),
            pltpu.VMEM((TILES, FEAT, TILE), jnp.bfloat16),
            pltpu.SemaphoreType.DMA((N_PIECES,)),
            pltpu.VMEM((TILES, TILE), jnp.float32),
            pltpu.VMEM((N_ROWS, 8, TILE), jnp.int32),
            pltpu.SMEM((N_ROWS, 8, TILE), jnp.int32),
            pltpu.VMEM((N_ROWS, EXTRA, FEAT), jnp.bfloat16),
            pltpu.VMEM((TILES, EXTRA, TILE), jnp.bfloat16),
            pltpu.SemaphoreType.DMA((N_PIECES,)),
            pltpu.SemaphoreType.DMA,
            pltpu.SemaphoreType.DMA((2,)),
        ],
        compiler_params=limit(60),
        name="first_row_pass",
    )(at, *pieces)


def row_pass(items, *operands):
    return pl.pallas_call(
        row_kernel,
        out_shape=ROW_PARTS,
        in_specs=[SMEM] + [VMEM] * len(operands),
        out_specs=VMEM,
        scratch_shapes=ROW_SCRATCH,
        compiler_params=limit(20),
        name="row_pass",
    )(items, *operands)


def col_pass(items, *operands):
    return pl.pallas_call(
        col_kernel,
        out_shape=shape((N_COLS, TILES, TILE)),
        in_specs=[SMEM] + [VMEM] * len(operands),
        out_specs=VMEM,
        scratch_shapes=COL_SCRATCH,
        compiler_params=limit(20),
        name="col_pass",
    )(items, *operands)


def last_col_pass(items, *operands):
    return pl.pallas_call(
        last_col_kernel,
        out_shape=(shape((1, TILES, TILE)), shape((SUBS, TILE))),
        in_specs=[SMEM] + [VMEM] * len(operands),
        out_specs=(VMEM, VMEM),
        scratch_shapes=[pltpu.VMEM((N_ROWS * SUBS, TILE), jnp.float32)] + COL_SCRATCH,
        compiler_params=limit(20),
        name="last_col_pass",
    )(items, *operands)


def swap(blocks, axes):
    return lax.all_to_all(blocks, axes, split_axis=0, concat_axis=0, tiled=True)


def exchange(block, partner):
    pairs = []
    for place in range(N_ROWS * N_COLS):
        at = tuple(int(k) for k in np.unravel_index(place, DIMS))
        pairs.append((place, int(np.ravel_multi_index(partner(*at), DIMS))))
    return lax.ppermute(block, NAMES, pairs)


def gather_ring(block, one, two):
    first = exchange(block, one)
    second = exchange(block, two)
    return [block, first, second, exchange(second, one)]


def gather_sources(block):
    pair = jnp.stack([block, exchange(block, source_partner(0, 1))])
    other = exchange(pair, source_partner(0, 3))
    one, two = source_partner(1, 1), source_partner(1, 3)
    first, second = exchange(pair, one), exchange(pair, two)
    pieces = [pair, first, second, exchange(second, one)]
    first, second = exchange(other, one), exchange(other, two)
    return pieces + [other, first, second, exchange(first, two)]


def source_partner(stage, flip):
    def partner(x, y, z, core):
        return (x, y ^ flip, z, core) if stage == core else (x, y, z ^ flip, core)

    return partner


def target_partner(order):
    return lambda x, y, z, core: (x ^ (1, 3)[order ^ core], y, z, core)


def sibling(x, y, z, core):
    return (x, y, z, core ^ 1)


def body(
    source_points, target_points, source_mass, target_mass, target_init, pair_tiles, pair_count
):
    x_block, y_block, source_norm, target_part = prepare(
        source_points,
        target_points,
        source_mass.reshape(SUBS, TILE),
        target_mass.reshape(TSUB, TILE),
        target_init.reshape(TSUB, TILE),
        pair_tiles.T,
        pair_count.reshape(1, -1),
    )
    xs = gather_sources(x_block)
    near = gather_ring(y_block, target_partner(0), target_partner(1))
    far = [exchange(jnp.concatenate(near[:2]), sibling)]
    far += [exchange(block, sibling) for block in near[2:]]

    at = jnp.stack([lax.axis_index(name) for name in NAMES]).astype(jnp.int32)
    row_parts, items, cols, rows, xs, ys = first_pass(at, xs + near + far)
    for iteration in range(ITERS - 1):
        col_parts = col_pass(items, xs, ys, cols, swap(row_parts, ROWS))
        row_parts = row_pass(items, xs, ys, rows, swap(col_parts, COLS))
    col_parts, source_pot = last_col_pass(
        items, xs, ys, cols, swap(row_parts, ROWS), source_norm
    )
    last = swap(col_parts.reshape(N_COLS, TSUB, TILE), COLS)
    target_pot = target_part - EPSILON * lse_over_first(last)
    return (source_pot.reshape(-1), target_pot.reshape(-1))


def solution(mesh):
    grid = Mesh(mesh.devices.reshape(DIMS), NAMES)
    placed = (
        P(NAMES, None),
        P(NAMES, None),
        P(NAMES),
        P(NAMES),
        P(NAMES),
        P(NAMES, None),
        P(NAMES),
    )
    return jax.shard_map(
        body, mesh=grid, in_specs=placed, out_specs=(P(NAMES), P(NAMES)), check_vma=False
    )
```

```python
import functools
import math

import jax
import jax.numpy as jnp
import numpy as np
from jax import lax
from jax.experimental import pallas as pl
from jax.experimental.pallas import tpu as pltpu
from jax.sharding import Mesh
from jax.sharding import PartitionSpec as P

TSUB = 8
CAP = 2
ITERS = 2
EPSILON = 0.1

DIMS = (4, 4, 4, 2)
NAMES = ("x", "y", "z", "core")
ROWS = ("y", "z")
COLS = ("x", "core")
N_ROWS = 16
N_PIECES = 8
N_COPIES = 12
N_COLS = 8
RING = 4
SRC = 384
TILE = 128
SUBS = SRC // TILE
FEAT = 256
TILES = N_COLS * TSUB
SLOTS = N_ROWS * N_COLS * CAP
UNROLL = 16
LAST_UNROLL = 4
EXTRA = 16
LISTED = 8 + SLOTS + 4 * LAST_UNROLL
NOTHING = TILES << 8
NORMS = 16
GAIN = 2.0 / (FEAT * EPSILON)
UNIT = 1.0 / (FEAT * EPSILON)
LOG2E = math.log2(math.e)
SPAN = 70.0


def lse_over_first(parts):
    top = jnp.max(parts, axis=0)
    base = jnp.where(top == -jnp.inf, 0.0, top)
    return top + jnp.log(jnp.sum(jnp.exp(parts - base[None]), axis=0))


def spread(values, norm_ref):
    high, low = jnp.max(values), jnp.min(values)
    reach = GAIN * jnp.sqrt(jnp.max(norm_ref[0:8]) * jnp.max(norm_ref[8:16]))
    return 0.5 * high + 0.5 * low, 0.5 * high - 0.5 * low + reach <= SPAN


def diagonal():
    return lax.broadcasted_iota(jnp.int32, (TILE, TILE), 0) == lax.broadcasted_iota(
        jnp.int32, (TILE, TILE), 1
    )


def as_row(eye, col):
    return jnp.sum(jnp.where(eye, col, 0.0), axis=0, keepdims=True)


def as_col(eye, row):
    return jnp.sum(jnp.where(eye, row, 0.0), axis=1, keepdims=True)


def products(x, y):
    return jnp.dot(x, y, preferred_element_type=jnp.float32)


def item_at(item_ref, w):
    one, two = item_ref[8 + 2 * w], item_ref[9 + 2 * w]
    return (
        one >> 20,
        (one >> 16) & 15,
        (one >> 8) & 255,
        (two >> 8) & 255,
        one & 255,
        two & 255,
    )


def exps(x, y):
    return jnp.exp2((GAIN * LOG2E) * products(x, y))


def two_tiles(y_ref, r0, r1):
    return jnp.concatenate([y_ref[r0], y_ref[r1]], axis=1)


def sweep(n_items, work):
    def steps(first, size):
        def step(w, _):
            for k in range(size):
                work(first + size * w + k)
            return 0

        return step

    whole = lax.div(n_items, UNROLL)
    lax.fori_loop(0, whole, steps(0, UNROLL), 0)
    left = n_items - UNROLL * whole
    lax.fori_loop(
        0, lax.div(left + LAST_UNROLL - 1, LAST_UNROLL), steps(UNROLL * whole, LAST_UNROLL), 0
    )


def rescale(old, new):
    return jnp.where(old == new, 1.0, jnp.exp(old - new))


def split(values):
    high = values.astype(jnp.bfloat16).astype(jnp.float32)
    rest = values - high
    middle = rest.astype(jnp.bfloat16).astype(jnp.float32)
    return [high, middle, (rest - middle).astype(jnp.bfloat16).astype(jnp.float32)]


def start_all(pairs, sems):
    copies = [pltpu.make_async_copy(src, dst, sems.at[k]) for k, (src, dst) in enumerate(pairs)]
    for copy in copies:
        copy.start()
    return copies


def prepare_kernel(*refs):
    xo_ref, yo_ref, nx_ref, part_ref = refs[7:11]
    y_ref, mass_ref, goal_ref, init_ref, tile_ref, count_ref, sems = refs[11:]
    copies = start_all(
        zip(refs[:7], (xo_ref.at[0:SRC], y_ref, mass_ref, goal_ref, init_ref, tile_ref, count_ref)),
        sems,
    )
    eye = diagonal()
    for copy in copies[2:]:
        copy.wait()
    la = jnp.log(mass_ref[...])
    lb = jnp.log(goal_ref[...])

    copies[0].wait()
    norms = []
    for b in range(SUBS):
        x = xo_ref[b * TILE : (b + 1) * TILE, :].astype(jnp.float32)
        norms.append(as_row(eye, jnp.sum(x * x, axis=1, keepdims=True)))
    nx = jnp.concatenate(norms, axis=0)
    nx_ref[...] = nx
    bound = jnp.full((1, TILE), 1.01 * jnp.max(nx))
    left = split(la) + [bound, jnp.zeros((EXTRA - 10, TILE), jnp.float32)]
    right = [
        tile_ref[...].astype(jnp.float32),
        count_ref[...].astype(jnp.float32),
        jnp.zeros((EXTRA - 3, TILE), jnp.float32),
    ]
    extra = jnp.concatenate(
        [jnp.concatenate(left, axis=0), jnp.concatenate(right, axis=0)], axis=1
    )
    xo_ref[SRC:] = extra.astype(jnp.bfloat16)

    copies[1].wait()
    norms = []
    for t in range(TSUB):
        y = y_ref[t * TILE : (t + 1) * TILE, :].astype(jnp.float32).T
        norms.append(jnp.sum(y * y, axis=0, keepdims=True))
        yo_ref[t, 0:FEAT] = y.astype(jnp.bfloat16)
    ny = jnp.concatenate(norms, axis=0)
    part_ref[...] = EPSILON * (lb + UNIT * ny)
    a0 = init_ref[...] / EPSILON - ny * UNIT
    parts = split(a0) + split(lb)
    bound = jnp.full((1, TILE), 1.01 * jnp.max(ny))
    for t in range(TSUB):
        rows = [part[t : t + 1] for part in parts]
        rows += [bound, jnp.zeros((EXTRA - 7, TILE), jnp.float32)]
        yo_ref[t, FEAT:] = jnp.concatenate(rows, axis=0).astype(jnp.bfloat16)


def gray(k):
    return k ^ (k >> 1)


def ring_place(offset, first):
    place = gray(offset)
    other = ((place & 1) << 1) | (place >> 1)
    return jnp.where(first == 0, place, other)


def piece_copies(x_refs, y_refs, xs, ys, x_rows, y_rows):
    pairs = []
    for half in range(2):
        for k in range(RING):
            later = k if half == 0 else (0, 2, 1, 3)[k]
            piece = x_refs[2 * half + k // 2].at[pl.ds(2 * (k % 2), 2), x_rows, :]
            pairs.append((piece, xs.at[pl.ds(RING * later + 2 * half, 2)]))
    start = 0
    for piece in y_refs:
        pairs.append((piece.at[:, y_rows, :], ys.at[pl.ds(start, piece.shape[0])]))
        start += piece.shape[0]
    return pairs


def first_kernel(*refs):
    at_ref, pieces = refs[0], refs[1 : 1 + N_PIECES]
    x_refs, y_refs = pieces[:RING], pieces[RING:]
    out_ref, item_ref, cols_ref, rows_ref, xs_out, ys_out = refs[1 + N_PIECES : 7 + N_PIECES]
    a_buf, u_buf, acc, top, xs, ys, sems = refs[7 + N_PIECES : 14 + N_PIECES]
    a_ref, table, numbers, x_extra, y_extra, small_sems, sem, out_sems = refs[14 + N_PIECES :]
    la_ref, lb_ref = cols_ref.at[NORMS:], rows_ref.at[NORMS:]
    x, y, z, core = (at_ref[k] for k in range(4))

    small = start_all(
        piece_copies(
            x_refs, y_refs, x_extra, y_extra, slice(SRC, SRC + EXTRA), slice(FEAT, FEAT + EXTRA)
        ),
        small_sems,
    )
    large = start_all(
        piece_copies(x_refs, y_refs, xs, ys, slice(0, SRC), slice(0, FEAT)), sems
    )
    for copy in small:
        copy.wait()

    lane = lax.broadcasted_iota(jnp.int32, (CAP, TILE), 1)
    px, side = lane >> 5, lane & 1
    start = RING * (side ^ core) + ring_place(px ^ x, side)
    entry_base = ((TSUB * (2 * px + side)) << 8) + TSUB * start

    bound = None
    for later in range(RING):
        for sooner in range(RING):
            one, two = gray(sooner), gray(later)
            off_y = jnp.where(core == 0, one, two)
            off_z = jnp.where(core == 0, two, one)
            s = RING * (y ^ off_y) + (z ^ off_z)
            extra = x_extra[RING * later + sooner].astype(jnp.float32)
            la = extra[0:3, :TILE] + extra[3:6, :TILE] + extra[6:9, :TILE]
            for b in range(SUBS):
                la_ref[pl.ds(SUBS * s + b, 1), :] = la[b : b + 1]
            here = extra[9:10, :TILE]
            bound = here if bound is None else jnp.maximum(bound, here)
            numbers_here = extra[0:3, TILE:].astype(jnp.int32)
            head = (s << 20) | ((RING * later + sooner) << 16)
            entry = head | (entry_base + 257 * numbers_here[0:CAP])
            slot = lax.broadcasted_iota(jnp.int32, (CAP, TILE), 0)
            entry = jnp.where(slot < numbers_here[CAP : CAP + 1], entry, -1)
            table[pl.ds(s, 1)] = jnp.concatenate([entry, jnp.full((6, TILE), head)], axis=0)[None]
    for ref in (cols_ref, rows_ref):
        ref[0:8] = jnp.broadcast_to(bound, (8, TILE))

    copy = pltpu.make_async_copy(table, numbers, sem)
    copy.start()

    bound = None
    for k in range(2 * RING):
        side = core ^ (k // RING)
        place = k % RING
        offset = jnp.where(side == 0, gray(place), (0, 3, 1, 2)[place])
        owner = 2 * (x ^ offset) + side
        extra = y_extra[TSUB * k : TSUB * (k + 1)].astype(jnp.float32)
        rows = pl.ds(pl.multiple_of(TSUB * owner, TSUB), TSUB)
        a_ref[rows, :] = extra[:, 0] + extra[:, 1] + extra[:, 2]
        lb_ref[rows, :] = extra[:, 3] + extra[:, 4] + extra[:, 5]
        here = extra[0, 6:7]
        bound = here if bound is None else jnp.maximum(bound, here)
    for ref in (cols_ref, rows_ref):
        ref[8:16] = jnp.broadcast_to(bound, (8, TILE))

    copy.wait()
    lanes = [
        2 * (RING * RING * (owner // 2) + RING * y + z) + owner % 2 for owner in range(N_COLS)
    ]

    def block(s, place):
        for lane in lanes:
            for e in range(CAP):
                entry = numbers[s, e, lane]
                item_ref[place] = entry
                place = place + jnp.where(entry >= 0, 1, 0)
        item_ref[place] = numbers[s, CAP, 0] | NOTHING
        return place + (place & 1)

    end = lax.fori_loop(0, N_ROWS, block, jnp.int32(8))
    for k in range(2 * LAST_UNROLL):
        item_ref[end + k] = jnp.int32(NOTHING)
    item_ref[0] = (end - 8) >> 1
    item_ref[1] = RING * y + z
    for copy in large:
        copy.wait()
    outward = start_all([(xs, xs_out), (ys, ys_out)], out_sems)
    row_core(a_ref[...], item_ref, xs, ys, cols_ref, out_ref, a_buf, u_buf, acc, top)
    for copy in outward:
        copy.wait()


def row_kernel(item_ref, x_ref, y_ref, side_ref, parts_ref, out_ref, a_buf, u_buf, acc, top):
    a = side_ref[NORMS:] - lse_over_first(parts_ref[...])
    row_core(a, item_ref, x_ref, y_ref, side_ref, out_ref, a_buf, u_buf, acc, top)


def row_core(a, item_ref, x_ref, y_ref, norm_ref, out_ref, a_buf, u_buf, acc, top):
    mid, fast = spread(a, norm_ref)
    n_items = item_ref[0]
    eye = diagonal()

    acc[...] = jnp.zeros_like(acc)

    @pl.when(fast)
    def _():
        u_buf[0:TILES] = jnp.exp(a - mid)
        u_buf[TILES:] = jnp.zeros((8, TILE), jnp.float32)

        def work(w):
            s, h, t0, t1, r0, r1 = item_at(item_ref, w)
            u0, u1 = u_buf[pl.ds(t0, 1), :], u_buf[pl.ds(t1, 1), :]
            e = exps(x_ref[h], two_tiles(y_ref, r0, r1))
            acc[s] += e[:, :TILE] * u0 + e[:, TILE:] * u1

        sweep(n_items, work)
        for k in range(N_ROWS * SUBS):
            s, b = k // SUBS, k % SUBS
            col = jnp.sum(acc[s, b * TILE : (b + 1) * TILE, :], axis=1, keepdims=True)
            a_buf[k : k + 1, :] = as_row(eye, col)
        done = mid + jnp.log(a_buf[0 : N_ROWS * SUBS])
        out_ref[...] = jnp.broadcast_to(done[None], out_ref.shape)

    @pl.when(jnp.logical_not(fast))
    def _():
        a_buf[0:TILES] = a
        a_buf[TILES:] = jnp.zeros((8, TILE), jnp.float32)
        top[...] = jnp.full_like(top, -jnp.inf)

        def step(w, _):
            s, h, t0, t1, r0, r1 = item_at(item_ref, w)
            for t, r in ((t0, r0), (t1, r1)):

                @pl.when(t < TILES)
                def _(t=t, r=r):
                    score = GAIN * products(x_ref[h], y_ref[r]) + a_buf[pl.ds(t, 1), :]
                    old = top[s]
                    new = jnp.maximum(old, score)
                    acc[s] = acc[s] * rescale(old, new) + jnp.exp(score - new)
                    top[s] = new

            return 0

        lax.fori_loop(0, n_items, step, 0)

        def finish(k, _):
            s, b = lax.div(k, SUBS), lax.rem(k, SUBS)
            rows = pl.ds(pl.multiple_of(b * TILE, TILE), TILE)
            block = top[s, rows, :]
            high = jnp.max(block, axis=1, keepdims=True)
            base = jnp.where(high == -jnp.inf, 0.0, high)
            total = jnp.sum(acc[s, rows, :] * jnp.exp(block - base), axis=1, keepdims=True)
            high_row = jnp.max(jnp.where(eye, high, -jnp.inf), axis=0, keepdims=True)
            done = high_row + jnp.log(as_row(eye, total))
            out_ref[:, pl.ds(k, 1), :] = jnp.broadcast_to(done[None], (N_ROWS, 1, TILE))
            return 0

        lax.fori_loop(0, N_ROWS * SUBS, finish, 0)


def last_col_kernel(
    item_ref, x_ref, y_ref, side_ref, parts_ref, norm_ref, out_ref, f_ref, b_buf, *scratch
):
    b = side_ref[NORMS:] - lse_over_first(parts_ref[...])
    b_buf[...] = b
    for k in range(SUBS):
        here = b_buf[pl.ds(SUBS * item_ref[1] + k, 1), :]
        f_ref[k : k + 1, :] = EPSILON * (here + UNIT * norm_ref[k : k + 1, :])
    col_core(b, item_ref, x_ref, y_ref, side_ref, out_ref, *scratch)


def col_kernel(item_ref, x_ref, y_ref, side_ref, parts_ref, out_ref, *scratch):
    b = side_ref[NORMS:] - lse_over_first(parts_ref[...])
    col_core(b, item_ref, x_ref, y_ref, side_ref, out_ref, *scratch)


def col_core(b, item_ref, x_ref, y_ref, norm_ref, out_ref, spread_buf, acc, top):
    mid, fast = spread(b, norm_ref)
    n_items = item_ref[0]
    eye = diagonal()

    def lay_out(values):
        for k in range(N_ROWS * SUBS):
            s, part = k // SUBS, k % SUBS
            col = as_col(eye, values[k : k + 1, :])
            spread_buf[s, part * TILE : (part + 1) * TILE, :] = jnp.broadcast_to(col, (TILE, TILE))

    acc[...] = jnp.zeros_like(acc)

    @pl.when(fast)
    def _():
        lay_out(jnp.exp(b - mid))

        def work(w):
            s, h, t0, t1, r0, r1 = item_at(item_ref, w)
            e = exps(x_ref[h], two_tiles(y_ref, r0, r1))
            v = spread_buf[s]
            acc[t0] += jnp.sum((e[:, :TILE] * v).reshape(SRC // 8, 8, TILE), axis=0)
            acc[t1] += jnp.sum((e[:, TILE:] * v).reshape(SRC // 8, 8, TILE), axis=0)

        sweep(n_items, work)
        done = mid + jnp.log(jnp.sum(acc[0:TILES], axis=1))
        out_ref[...] = jnp.broadcast_to(done[None], out_ref.shape)

    @pl.when(jnp.logical_not(fast))
    def _():
        lay_out(b)
        top[...] = jnp.full_like(top, -jnp.inf)

        def step(w, _):
            s, h, t0, t1, r0, r1 = item_at(item_ref, w)
            for t, r in ((t0, r0), (t1, r1)):

                @pl.when(t < TILES)
                def _(t=t, r=r):
                    score = GAIN * products(x_ref[h], y_ref[r]) + spread_buf[s]
                    score = score.reshape(SRC // 8, 8, TILE)
                    old = top[t]
                    new = jnp.maximum(old, jnp.max(score, axis=0))
                    acc[t] = acc[t] * rescale(old, new) + jnp.sum(
                        jnp.exp(score - new[None]), axis=0
                    )
                    top[t] = new

            return 0

        lax.fori_loop(0, n_items, step, 0)
        high = jnp.max(top[0:TILES], axis=1)
        base = jnp.where(high == -jnp.inf, 0.0, high)
        total = jnp.sum(acc[0:TILES] * jnp.exp(top[0:TILES] - base[:, None, :]), axis=1)
        out_ref[...] = jnp.broadcast_to((high + jnp.log(total))[None], out_ref.shape)


VMEM = pl.BlockSpec(memory_space=pltpu.VMEM)
ANY = pl.BlockSpec(memory_space=pl.ANY)
SMEM = pl.BlockSpec(memory_space=pltpu.SMEM)


def limit(mebibytes):
    return pltpu.CompilerParams(vmem_limit_bytes=mebibytes * 1024 * 1024)


def shape(dims, dtype=jnp.float32):
    return jax.ShapeDtypeStruct(dims, dtype)


def prepare(*operands):
    return pl.pallas_call(
        prepare_kernel,
        out_shape=(
            shape((SRC + EXTRA, FEAT), jnp.bfloat16),
            shape((TSUB, FEAT + EXTRA, TILE), jnp.bfloat16),
            shape((SUBS, TILE)),
            shape((TSUB, TILE)),
        ),
        in_specs=[ANY] * 7,
        out_specs=(VMEM,) * 4,
        scratch_shapes=[
            pltpu.VMEM((TSUB * TILE, FEAT), jnp.bfloat16),
            pltpu.VMEM((SUBS, TILE), jnp.float32),
            pltpu.VMEM((TSUB, TILE), jnp.float32),
            pltpu.VMEM((TSUB, TILE), jnp.float32),
            pltpu.VMEM((CAP, TILE), jnp.int32),
            pltpu.VMEM((1, TILE), jnp.int32),
            pltpu.SemaphoreType.DMA((7,)),
        ],
        compiler_params=limit(60),
        name="prepare",
    )(*operands)


ROW_SCRATCH = [
    pltpu.VMEM((TILES + 8, TILE), jnp.float32),
    pltpu.VMEM((TILES + 8, TILE), jnp.float32),
    pltpu.VMEM((N_ROWS, SRC, TILE), jnp.float32),
    pltpu.VMEM((N_ROWS, SRC, TILE), jnp.float32),
]
COL_SCRATCH = [
    pltpu.VMEM((N_ROWS, SRC, TILE), jnp.float32),
    pltpu.VMEM((TILES + 1, 8, TILE), jnp.float32),
    pltpu.VMEM((TILES + 1, 8, TILE), jnp.float32),
]
ROW_PARTS = shape((N_ROWS, N_ROWS * SUBS, TILE))


def first_pass(at, pieces):
    return pl.pallas_call(
        first_kernel,
        out_shape=(
            ROW_PARTS,
            shape((LISTED,), jnp.int32),
            shape((NORMS + N_ROWS * SUBS, TILE)),
            shape((NORMS + TILES, TILE)),
            shape((N_ROWS, SRC, FEAT), jnp.bfloat16),
            shape((TILES, FEAT, TILE), jnp.bfloat16),
        ),
        in_specs=[SMEM] + [ANY] * N_PIECES,
        out_specs=(VMEM, SMEM, VMEM, VMEM, ANY, ANY),
        scratch_shapes=ROW_SCRATCH
        + [
            pltpu.VMEM((N_ROWS, SRC, FEAT), jnp.bfloat16),
            pltpu.VMEM((TILES, FEAT, TILE), jnp.bfloat16),
            pltpu.SemaphoreType.DMA((N_COPIES,)),
            pltpu.VMEM((TILES, TILE), jnp.float32),
            pltpu.VMEM((N_ROWS, 8, TILE), jnp.int32),
            pltpu.SMEM((N_ROWS, 8, TILE), jnp.int32),
            pltpu.VMEM((N_ROWS, EXTRA, FEAT), jnp.bfloat16),
            pltpu.VMEM((TILES, EXTRA, TILE), jnp.bfloat16),
            pltpu.SemaphoreType.DMA((N_COPIES,)),
            pltpu.SemaphoreType.DMA,
            pltpu.SemaphoreType.DMA((2,)),
        ],
        compiler_params=limit(60),
        name="first_row_pass",
    )(at, *pieces)


def row_pass(items, *operands):
    return pl.pallas_call(
        row_kernel,
        out_shape=ROW_PARTS,
        in_specs=[SMEM] + [VMEM] * len(operands),
        out_specs=VMEM,
        scratch_shapes=ROW_SCRATCH,
        compiler_params=limit(20),
        name="row_pass",
    )(items, *operands)


def col_pass(items, *operands):
    return pl.pallas_call(
        col_kernel,
        out_shape=shape((N_COLS, TILES, TILE)),
        in_specs=[SMEM] + [VMEM] * len(operands),
        out_specs=VMEM,
        scratch_shapes=COL_SCRATCH,
        compiler_params=limit(20),
        name="col_pass",
    )(items, *operands)


def last_col_pass(items, *operands):
    return pl.pallas_call(
        last_col_kernel,
        out_shape=(shape((1, TILES, TILE)), shape((SUBS, TILE))),
        in_specs=[SMEM] + [VMEM] * len(operands),
        out_specs=(VMEM, VMEM),
        scratch_shapes=[pltpu.VMEM((N_ROWS * SUBS, TILE), jnp.float32)] + COL_SCRATCH,
        compiler_params=limit(20),
        name="last_col_pass",
    )(items, *operands)


def swap(blocks, axes):
    return lax.all_to_all(blocks, axes, split_axis=0, concat_axis=0, tiled=True)


def exchange(block, partner):
    pairs = []
    for place in range(N_ROWS * N_COLS):
        at = tuple(int(k) for k in np.unravel_index(place, DIMS))
        pairs.append((place, int(np.ravel_multi_index(partner(*at), DIMS))))
    return lax.ppermute(block, NAMES, pairs)


def doubled(block, partner):
    return jnp.concatenate([block, exchange(block, partner)])


def gather_sources(block):
    pair = doubled(block[None], source_partner(0, 1))
    other = exchange(pair, source_partner(0, 3))
    one, two = source_partner(1, 1), source_partner(1, 3)
    pair, other = doubled(pair, one), doubled(other, two)
    return [pair, exchange(pair, two), other, exchange(other, one)]


def gather_targets(block):
    pair = doubled(block, target_partner(0))
    pieces = [pair, exchange(pair, target_partner(1))]
    return pieces + [exchange(piece, sibling) for piece in pieces]


def source_partner(stage, flip):
    def partner(x, y, z, core):
        return (x, y ^ flip, z, core) if stage == core else (x, y, z ^ flip, core)

    return partner


def target_partner(order):
    return lambda x, y, z, core: (x ^ (1, 3)[order ^ core], y, z, core)


def sibling(x, y, z, core):
    return (x, y, z, core ^ 1)


def body(
    source_points, target_points, source_mass, target_mass, target_init, pair_tiles, pair_count
):
    x_block, y_block, source_norm, target_part = prepare(
        source_points,
        target_points,
        source_mass.reshape(SUBS, TILE),
        target_mass.reshape(TSUB, TILE),
        target_init.reshape(TSUB, TILE),
        pair_tiles.T,
        pair_count.reshape(1, -1),
    )
    pieces = gather_sources(x_block) + gather_targets(y_block)

    at = jnp.stack([lax.axis_index(name) for name in NAMES]).astype(jnp.int32)
    row_parts, items, cols, rows, xs, ys = first_pass(at, pieces)
    for iteration in range(ITERS - 1):
        col_parts = col_pass(items, xs, ys, cols, swap(row_parts, ROWS))
        row_parts = row_pass(items, xs, ys, rows, swap(col_parts, COLS))
    col_parts, source_pot = last_col_pass(
        items, xs, ys, cols, swap(row_parts, ROWS), source_norm
    )
    last = swap(col_parts.reshape(N_COLS, TSUB, TILE), COLS)
    target_pot = target_part - EPSILON * lse_over_first(last)
    return (source_pot.reshape(-1), target_pot.reshape(-1))


def solution(mesh):
    grid = Mesh(mesh.devices.reshape(DIMS), NAMES)
    placed = (
        P(NAMES, None),
        P(NAMES, None),
        P(NAMES),
        P(NAMES),
        P(NAMES),
        P(NAMES, None),
        P(NAMES),
    )
    return jax.shard_map(
        body, mesh=grid, in_specs=placed, out_specs=(P(NAMES), P(NAMES)), check_vma=False
    )
```

```python
import functools
import math

import jax
import jax.numpy as jnp
import numpy as np
from jax import lax
from jax.experimental import pallas as pl
from jax.experimental.pallas import tpu as pltpu
from jax.sharding import Mesh
from jax.sharding import PartitionSpec as P

TSUB = 8
CAP = 2
ITERS = 2
EPSILON = 0.1

DIMS = (4, 4, 4, 2)
NAMES = ("x", "y", "z", "core")
ROWS = ("y", "z")
COLS = ("x", "core")
N_ROWS = 16
N_PIECES = 12
N_COLS = 8
RING = 4
SRC = 384
TILE = 128
SUBS = SRC // TILE
FEAT = 256
TILES = N_COLS * TSUB
SLOTS = N_ROWS * N_COLS * CAP
UNROLL = 16
LAST_UNROLL = 4
EXTRA = 16
LISTED = 8 + SLOTS + 4 * LAST_UNROLL
NOTHING = TILES << 8
NORMS = 16
GAIN = 2.0 / (FEAT * EPSILON)
UNIT = 1.0 / (FEAT * EPSILON)
LOG2E = math.log2(math.e)
SPAN = 70.0


def lse_over_first(parts):
    top = jnp.max(parts, axis=0)
    base = jnp.where(top == -jnp.inf, 0.0, top)
    return top + jnp.log(jnp.sum(jnp.exp(parts - base[None]), axis=0))


def spread(values, norm_ref):
    high, low = jnp.max(values), jnp.min(values)
    reach = GAIN * jnp.sqrt(jnp.max(norm_ref[0:8]) * jnp.max(norm_ref[8:16]))
    return 0.5 * high + 0.5 * low, 0.5 * high - 0.5 * low + reach <= SPAN


def diagonal():
    return lax.broadcasted_iota(jnp.int32, (TILE, TILE), 0) == lax.broadcasted_iota(
        jnp.int32, (TILE, TILE), 1
    )


def as_row(eye, col):
    return jnp.sum(jnp.where(eye, col, 0.0), axis=0, keepdims=True)


def as_col(eye, row):
    return jnp.sum(jnp.where(eye, row, 0.0), axis=1, keepdims=True)


def products(x, y):
    return jnp.dot(x, y, preferred_element_type=jnp.float32)


def item_at(item_ref, w):
    one, two = item_ref[8 + 2 * w], item_ref[9 + 2 * w]
    return (
        one >> 20,
        (one >> 16) & 15,
        (one >> 8) & 255,
        (two >> 8) & 255,
        one & 255,
        two & 255,
    )


def exps(x, y):
    return jnp.exp2((GAIN * LOG2E) * products(x, y))


def two_tiles(y_ref, r0, r1):
    return jnp.concatenate([y_ref[r0], y_ref[r1]], axis=1)


def sweep(n_items, work):
    def steps(first, size):
        def step(w, _):
            for k in range(size):
                work(first + size * w + k)
            return 0

        return step

    whole = lax.div(n_items, UNROLL)
    lax.fori_loop(0, whole, steps(0, UNROLL), 0)
    left = n_items - UNROLL * whole
    lax.fori_loop(
        0, lax.div(left + LAST_UNROLL - 1, LAST_UNROLL), steps(UNROLL * whole, LAST_UNROLL), 0
    )


def rescale(old, new):
    return jnp.where(old == new, 1.0, jnp.exp(old - new))


def split(values):
    high = values.astype(jnp.bfloat16).astype(jnp.float32)
    rest = values - high
    middle = rest.astype(jnp.bfloat16).astype(jnp.float32)
    return [high, middle, (rest - middle).astype(jnp.bfloat16).astype(jnp.float32)]


def start_all(pairs, sems):
    copies = [pltpu.make_async_copy(src, dst, sems.at[k]) for k, (src, dst) in enumerate(pairs)]
    for copy in copies:
        copy.start()
    return copies


def prepare_kernel(*refs):
    xo_ref, yo_ref, nx_ref, part_ref = refs[7:11]
    y_ref, mass_ref, goal_ref, init_ref, tile_ref, count_ref, sems = refs[11:]
    copies = start_all(
        zip(refs[:7], (xo_ref.at[0:SRC], y_ref, mass_ref, goal_ref, init_ref, tile_ref, count_ref)),
        sems,
    )
    eye = diagonal()
    for copy in copies[2:]:
        copy.wait()
    la = jnp.log(mass_ref[...])
    lb = jnp.log(goal_ref[...])

    copies[0].wait()
    norms = []
    for b in range(SUBS):
        x = xo_ref[b * TILE : (b + 1) * TILE, :].astype(jnp.float32)
        norms.append(as_row(eye, jnp.sum(x * x, axis=1, keepdims=True)))
    nx = jnp.concatenate(norms, axis=0)
    nx_ref[...] = nx
    bound = jnp.full((1, TILE), 1.01 * jnp.max(nx))
    left = split(la) + [bound, jnp.zeros((EXTRA - 10, TILE), jnp.float32)]
    right = [
        tile_ref[...].astype(jnp.float32),
        count_ref[...].astype(jnp.float32),
        jnp.zeros((EXTRA - 3, TILE), jnp.float32),
    ]
    extra = jnp.concatenate(
        [jnp.concatenate(left, axis=0), jnp.concatenate(right, axis=0)], axis=1
    )
    xo_ref[SRC:] = extra.astype(jnp.bfloat16)

    copies[1].wait()
    norms = []
    for t in range(TSUB):
        y = y_ref[t * TILE : (t + 1) * TILE, :].astype(jnp.float32).T
        norms.append(jnp.sum(y * y, axis=0, keepdims=True))
        yo_ref[t, 0:FEAT] = y.astype(jnp.bfloat16)
    ny = jnp.concatenate(norms, axis=0)
    part_ref[...] = EPSILON * (lb + UNIT * ny)
    a0 = init_ref[...] / EPSILON - ny * UNIT
    parts = split(a0) + split(lb)
    bound = jnp.full((1, TILE), 1.01 * jnp.max(ny))
    for t in range(TSUB):
        rows = [part[t : t + 1] for part in parts]
        rows += [bound, jnp.zeros((EXTRA - 7, TILE), jnp.float32)]
        yo_ref[t, FEAT:] = jnp.concatenate(rows, axis=0).astype(jnp.bfloat16)


def gray(k):
    return k ^ (k >> 1)


def ring_place(offset, first):
    place = gray(offset)
    other = ((place & 1) << 1) | (place >> 1)
    return jnp.where(first == 0, place, other)


def piece_copies(x_refs, y_refs, xs, ys, x_rows, y_rows):
    pairs = []
    for half in range(2):
        for later in range(RING):
            place = pl.ds(RING * later + 2 * half, 2)
            pairs.append((x_refs[RING * half + later].at[:, x_rows, :], xs.at[place]))
    start = 0
    for piece in y_refs:
        pairs.append((piece.at[:, y_rows, :], ys.at[pl.ds(start, piece.shape[0])]))
        start += piece.shape[0]
    return pairs


def first_kernel(*refs):
    at_ref, pieces = refs[0], refs[1 : 1 + N_PIECES]
    x_refs, y_refs = pieces[: 2 * RING], pieces[2 * RING :]
    out_ref, item_ref, cols_ref, rows_ref, xs, ys = refs[1 + N_PIECES : 7 + N_PIECES]
    a_buf, u_buf, acc, top, sems = refs[7 + N_PIECES : 12 + N_PIECES]
    a_ref, table, numbers, x_extra, y_extra, small_sems, sem = refs[12 + N_PIECES :]
    la_ref, lb_ref = cols_ref.at[NORMS:], rows_ref.at[NORMS:]
    x, y, z, core = (at_ref[k] for k in range(4))

    small = start_all(
        piece_copies(
            x_refs, y_refs, x_extra, y_extra, slice(SRC, SRC + EXTRA), slice(FEAT, FEAT + EXTRA)
        ),
        small_sems,
    )
    large = start_all(
        piece_copies(x_refs, y_refs, xs, ys, slice(0, SRC), slice(0, FEAT)), sems
    )
    for copy in small:
        copy.wait()

    lane = lax.broadcasted_iota(jnp.int32, (CAP, TILE), 1)
    px, side = lane >> 5, lane & 1
    start = RING * (side ^ core) + ring_place(px ^ x, side)
    entry_base = ((TSUB * (2 * px + side)) << 8) + TSUB * start

    bound = None
    for later in range(RING):
        for sooner in range(RING):
            one, two = gray(sooner), gray(later)
            off_y = jnp.where(core == 0, one, two)
            off_z = jnp.where(core == 0, two, one)
            s = RING * (y ^ off_y) + (z ^ off_z)
            extra = x_extra[RING * later + sooner].astype(jnp.float32)
            la = extra[0:3, :TILE] + extra[3:6, :TILE] + extra[6:9, :TILE]
            for b in range(SUBS):
                la_ref[pl.ds(SUBS * s + b, 1), :] = la[b : b + 1]
            here = extra[9:10, :TILE]
            bound = here if bound is None else jnp.maximum(bound, here)
            numbers_here = extra[0:3, TILE:].astype(jnp.int32)
            head = (s << 20) | ((RING * later + sooner) << 16)
            entry = head | (entry_base + 257 * numbers_here[0:CAP])
            slot = lax.broadcasted_iota(jnp.int32, (CAP, TILE), 0)
            entry = jnp.where(slot < numbers_here[CAP : CAP + 1], entry, -1)
            table[pl.ds(s, 1)] = jnp.concatenate([entry, jnp.full((6, TILE), head)], axis=0)[None]
    for ref in (cols_ref, rows_ref):
        ref[0:8] = jnp.broadcast_to(bound, (8, TILE))

    copy = pltpu.make_async_copy(table, numbers, sem)
    copy.start()

    bound = None
    for k in range(2 * RING):
        side = core ^ (k // RING)
        place = k % RING
        offset = jnp.where(side == 0, gray(place), (0, 3, 1, 2)[place])
        owner = 2 * (x ^ offset) + side
        extra = y_extra[TSUB * k : TSUB * (k + 1)].astype(jnp.float32)
        rows = pl.ds(pl.multiple_of(TSUB * owner, TSUB), TSUB)
        a_ref[rows, :] = extra[:, 0] + extra[:, 1] + extra[:, 2]
        lb_ref[rows, :] = extra[:, 3] + extra[:, 4] + extra[:, 5]
        here = extra[0, 6:7]
        bound = here if bound is None else jnp.maximum(bound, here)
    for ref in (cols_ref, rows_ref):
        ref[8:16] = jnp.broadcast_to(bound, (8, TILE))

    copy.wait()
    lanes = [
        2 * (RING * RING * (owner // 2) + RING * y + z) + owner % 2 for owner in range(N_COLS)
    ]

    def block(s, place):
        for lane in lanes:
            for e in range(CAP):
                entry = numbers[s, e, lane]
                item_ref[place] = entry
                place = place + jnp.where(entry >= 0, 1, 0)
        item_ref[place] = numbers[s, CAP, 0] | NOTHING
        return place + (place & 1)

    end = lax.fori_loop(0, N_ROWS, block, jnp.int32(8))
    for k in range(2 * LAST_UNROLL):
        item_ref[end + k] = jnp.int32(NOTHING)
    item_ref[0] = (end - 8) >> 1
    item_ref[1] = RING * y + z
    for copy in large:
        copy.wait()
    row_core(a_ref[...], item_ref, xs, ys, cols_ref, out_ref, a_buf, u_buf, acc, top)


def row_kernel(item_ref, x_ref, y_ref, side_ref, parts_ref, out_ref, a_buf, u_buf, acc, top):
    a = side_ref[NORMS:] - lse_over_first(parts_ref[...])
    row_core(a, item_ref, x_ref, y_ref, side_ref, out_ref, a_buf, u_buf, acc, top)


def row_core(a, item_ref, x_ref, y_ref, norm_ref, out_ref, a_buf, u_buf, acc, top):
    mid, fast = spread(a, norm_ref)
    n_items = item_ref[0]
    eye = diagonal()

    acc[...] = jnp.zeros_like(acc)

    @pl.when(fast)
    def _():
        u_buf[0:TILES] = jnp.exp(a - mid)
        u_buf[TILES:] = jnp.zeros((8, TILE), jnp.float32)

        def work(w):
            s, h, t0, t1, r0, r1 = item_at(item_ref, w)
            u0, u1 = u_buf[pl.ds(t0, 1), :], u_buf[pl.ds(t1, 1), :]
            e = exps(x_ref[h], two_tiles(y_ref, r0, r1))
            acc[s] += e[:, :TILE] * u0 + e[:, TILE:] * u1

        sweep(n_items, work)
        for k in range(N_ROWS * SUBS):
            s, b = k // SUBS, k % SUBS
            col = jnp.sum(acc[s, b * TILE : (b + 1) * TILE, :], axis=1, keepdims=True)
            a_buf[k : k + 1, :] = as_row(eye, col)
        done = mid + jnp.log(a_buf[0 : N_ROWS * SUBS])
        out_ref[...] = jnp.broadcast_to(done[None], out_ref.shape)

    @pl.when(jnp.logical_not(fast))
    def _():
        a_buf[0:TILES] = a
        a_buf[TILES:] = jnp.zeros((8, TILE), jnp.float32)
        top[...] = jnp.full_like(top, -jnp.inf)

        def step(w, _):
            s, h, t0, t1, r0, r1 = item_at(item_ref, w)
            for t, r in ((t0, r0), (t1, r1)):

                @pl.when(t < TILES)
                def _(t=t, r=r):
                    score = GAIN * products(x_ref[h], y_ref[r]) + a_buf[pl.ds(t, 1), :]
                    old = top[s]
                    new = jnp.maximum(old, score)
                    acc[s] = acc[s] * rescale(old, new) + jnp.exp(score - new)
                    top[s] = new

            return 0

        lax.fori_loop(0, n_items, step, 0)

        def finish(k, _):
            s, b = lax.div(k, SUBS), lax.rem(k, SUBS)
            rows = pl.ds(pl.multiple_of(b * TILE, TILE), TILE)
            block = top[s, rows, :]
            high = jnp.max(block, axis=1, keepdims=True)
            base = jnp.where(high == -jnp.inf, 0.0, high)
            total = jnp.sum(acc[s, rows, :] * jnp.exp(block - base), axis=1, keepdims=True)
            high_row = jnp.max(jnp.where(eye, high, -jnp.inf), axis=0, keepdims=True)
            done = high_row + jnp.log(as_row(eye, total))
            out_ref[:, pl.ds(k, 1), :] = jnp.broadcast_to(done[None], (N_ROWS, 1, TILE))
            return 0

        lax.fori_loop(0, N_ROWS * SUBS, finish, 0)


def last_col_kernel(
    item_ref, x_ref, y_ref, side_ref, parts_ref, norm_ref, out_ref, f_ref, b_buf, *scratch
):
    b = side_ref[NORMS:] - lse_over_first(parts_ref[...])
    b_buf[...] = b
    for k in range(SUBS):
        here = b_buf[pl.ds(SUBS * item_ref[1] + k, 1), :]
        f_ref[k : k + 1, :] = EPSILON * (here + UNIT * norm_ref[k : k + 1, :])
    col_core(b, item_ref, x_ref, y_ref, side_ref, out_ref, *scratch)


def col_kernel(item_ref, x_ref, y_ref, side_ref, parts_ref, out_ref, *scratch):
    b = side_ref[NORMS:] - lse_over_first(parts_ref[...])
    col_core(b, item_ref, x_ref, y_ref, side_ref, out_ref, *scratch)


def col_core(b, item_ref, x_ref, y_ref, norm_ref, out_ref, spread_buf, acc, top):
    mid, fast = spread(b, norm_ref)
    n_items = item_ref[0]
    eye = diagonal()

    def lay_out(values):
        for k in range(N_ROWS * SUBS):
            s, part = k // SUBS, k % SUBS
            col = as_col(eye, values[k : k + 1, :])
            spread_buf[s, part * TILE : (part + 1) * TILE, :] = jnp.broadcast_to(col, (TILE, TILE))

    acc[...] = jnp.zeros_like(acc)

    @pl.when(fast)
    def _():
        lay_out(jnp.exp(b - mid))

        def work(w):
            s, h, t0, t1, r0, r1 = item_at(item_ref, w)
            e = exps(x_ref[h], two_tiles(y_ref, r0, r1))
            v = spread_buf[s]
            acc[t0] += jnp.sum((e[:, :TILE] * v).reshape(SRC // 8, 8, TILE), axis=0)
            acc[t1] += jnp.sum((e[:, TILE:] * v).reshape(SRC // 8, 8, TILE), axis=0)

        sweep(n_items, work)
        done = mid + jnp.log(jnp.sum(acc[0:TILES], axis=1))
        out_ref[...] = jnp.broadcast_to(done[None], out_ref.shape)

    @pl.when(jnp.logical_not(fast))
    def _():
        lay_out(b)
        top[...] = jnp.full_like(top, -jnp.inf)

        def step(w, _):
            s, h, t0, t1, r0, r1 = item_at(item_ref, w)
            for t, r in ((t0, r0), (t1, r1)):

                @pl.when(t < TILES)
                def _(t=t, r=r):
                    score = GAIN * products(x_ref[h], y_ref[r]) + spread_buf[s]
                    score = score.reshape(SRC // 8, 8, TILE)
                    old = top[t]
                    new = jnp.maximum(old, jnp.max(score, axis=0))
                    acc[t] = acc[t] * rescale(old, new) + jnp.sum(
                        jnp.exp(score - new[None]), axis=0
                    )
                    top[t] = new

            return 0

        lax.fori_loop(0, n_items, step, 0)
        high = jnp.max(top[0:TILES], axis=1)
        base = jnp.where(high == -jnp.inf, 0.0, high)
        total = jnp.sum(acc[0:TILES] * jnp.exp(top[0:TILES] - base[:, None, :]), axis=1)
        out_ref[...] = jnp.broadcast_to((high + jnp.log(total))[None], out_ref.shape)


VMEM = pl.BlockSpec(memory_space=pltpu.VMEM)
ANY = pl.BlockSpec(memory_space=pl.ANY)
SMEM = pl.BlockSpec(memory_space=pltpu.SMEM)


def limit(mebibytes):
    return pltpu.CompilerParams(vmem_limit_bytes=mebibytes * 1024 * 1024)


def shape(dims, dtype=jnp.float32):
    return jax.ShapeDtypeStruct(dims, dtype)


def prepare(*operands):
    return pl.pallas_call(
        prepare_kernel,
        out_shape=(
            shape((SRC + EXTRA, FEAT), jnp.bfloat16),
            shape((TSUB, FEAT + EXTRA, TILE), jnp.bfloat16),
            shape((SUBS, TILE)),
            shape((TSUB, TILE)),
        ),
        in_specs=[ANY] * 7,
        out_specs=(VMEM,) * 4,
        scratch_shapes=[
            pltpu.VMEM((TSUB * TILE, FEAT), jnp.bfloat16),
            pltpu.VMEM((SUBS, TILE), jnp.float32),
            pltpu.VMEM((TSUB, TILE), jnp.float32),
            pltpu.VMEM((TSUB, TILE), jnp.float32),
            pltpu.VMEM((CAP, TILE), jnp.int32),
            pltpu.VMEM((1, TILE), jnp.int32),
            pltpu.SemaphoreType.DMA((7,)),
        ],
        compiler_params=limit(60),
        name="prepare",
    )(*operands)


ROW_SCRATCH = [
    pltpu.VMEM((TILES + 8, TILE), jnp.float32),
    pltpu.VMEM((TILES + 8, TILE), jnp.float32),
    pltpu.VMEM((N_ROWS, SRC, TILE), jnp.float32),
    pltpu.VMEM((N_ROWS, SRC, TILE), jnp.float32),
]
COL_SCRATCH = [
    pltpu.VMEM((N_ROWS, SRC, TILE), jnp.float32),
    pltpu.VMEM((TILES + 1, 8, TILE), jnp.float32),
    pltpu.VMEM((TILES + 1, 8, TILE), jnp.float32),
]
ROW_PARTS = shape((N_ROWS, N_ROWS * SUBS, TILE))


def first_pass(at, pieces):
    return pl.pallas_call(
        first_kernel,
        out_shape=(
            ROW_PARTS,
            shape((LISTED,), jnp.int32),
            shape((NORMS + N_ROWS * SUBS, TILE)),
            shape((NORMS + TILES, TILE)),
            shape((N_ROWS, SRC, FEAT), jnp.bfloat16),
            shape((TILES, FEAT, TILE), jnp.bfloat16),
        ),
        in_specs=[SMEM] + [ANY] * N_PIECES,
        out_specs=(VMEM, SMEM, VMEM, VMEM, VMEM, VMEM),
        scratch_shapes=ROW_SCRATCH
        + [
            pltpu.SemaphoreType.DMA((N_PIECES,)),
            pltpu.VMEM((TILES, TILE), jnp.float32),
            pltpu.VMEM((N_ROWS, 8, TILE), jnp.int32),
            pltpu.SMEM((N_ROWS, 8, TILE), jnp.int32),
            pltpu.VMEM((N_ROWS, EXTRA, FEAT), jnp.bfloat16),
            pltpu.VMEM((TILES, EXTRA, TILE), jnp.bfloat16),
            pltpu.SemaphoreType.DMA((N_PIECES,)),
            pltpu.SemaphoreType.DMA,
        ],
        compiler_params=limit(24),
        name="first_row_pass",
    )(at, *[pltpu.with_memory_space_constraint(piece, pltpu.HBM) for piece in pieces])


def row_pass(items, *operands):
    return pl.pallas_call(
        row_kernel,
        out_shape=ROW_PARTS,
        in_specs=[SMEM] + [VMEM] * len(operands),
        out_specs=VMEM,
        scratch_shapes=ROW_SCRATCH,
        compiler_params=limit(20),
        name="row_pass",
    )(items, *operands)


def col_pass(items, *operands):
    return pl.pallas_call(
        col_kernel,
        out_shape=shape((N_COLS, TILES, TILE)),
        in_specs=[SMEM] + [VMEM] * len(operands),
        out_specs=VMEM,
        scratch_shapes=COL_SCRATCH,
        compiler_params=limit(20),
        name="col_pass",
    )(items, *operands)


def last_col_pass(items, *operands):
    return pl.pallas_call(
        last_col_kernel,
        out_shape=(shape((1, TILES, TILE)), shape((SUBS, TILE))),
        in_specs=[SMEM] + [VMEM] * len(operands),
        out_specs=(VMEM, VMEM),
        scratch_shapes=[pltpu.VMEM((N_ROWS * SUBS, TILE), jnp.float32)] + COL_SCRATCH,
        compiler_params=limit(20),
        name="last_col_pass",
    )(items, *operands)


def swap(blocks, axes):
    return lax.all_to_all(blocks, axes, split_axis=0, concat_axis=0, tiled=True)


def exchange(block, partner):
    pairs = []
    for place in range(N_ROWS * N_COLS):
        at = tuple(int(k) for k in np.unravel_index(place, DIMS))
        pairs.append((place, int(np.ravel_multi_index(partner(*at), DIMS))))
    return lax.ppermute(block, NAMES, pairs)


def doubled(block, partner):
    return jnp.concatenate([block, exchange(block, partner)])


def after(value, events):
    return lax.optimization_barrier((value, events))[0]


def gather_all(sources, targets):
    along = [source_partner(0, flip) for flip in (1, 3)]
    across = [source_partner(1, flip) for flip in (1, 3)]
    beside = [target_partner(order) for order in (0, 1)]

    pair = jnp.stack([sources, exchange(sources, along[0])])
    tiles = jnp.concatenate([targets, exchange(targets, beside[0])])
    other = exchange(pair, along[1])
    first, second = exchange(pair, across[0]), exchange(pair, across[1])
    further = exchange(after(tiles, pair), beside[1])
    relayed = exchange(first, across[1])
    pieces = [pair, first, second, relayed]
    near = exchange(after(tiles, (first, second)), sibling)
    first, second = exchange(other, across[0]), exchange(other, across[1])
    pieces += [other, first, second, exchange(second, across[0])]
    far = exchange(after(further, (first, second)), sibling)
    return pieces + [tiles, further, near, far]


def source_partner(stage, flip):
    def partner(x, y, z, core):
        return (x, y ^ flip, z, core) if stage == core else (x, y, z ^ flip, core)

    return partner


def target_partner(order):
    return lambda x, y, z, core: (x ^ (1, 3)[order ^ core], y, z, core)


def sibling(x, y, z, core):
    return (x, y, z, core ^ 1)


def body(
    source_points, target_points, source_mass, target_mass, target_init, pair_tiles, pair_count
):
    x_block, y_block, source_norm, target_part = prepare(
        source_points,
        target_points,
        source_mass.reshape(SUBS, TILE),
        target_mass.reshape(TSUB, TILE),
        target_init.reshape(TSUB, TILE),
        pair_tiles.T,
        pair_count.reshape(1, -1),
    )
    pieces = gather_all(x_block, y_block)

    at = jnp.stack([lax.axis_index(name) for name in NAMES]).astype(jnp.int32)
    row_parts, items, cols, rows, xs, ys = first_pass(at, pieces)
    for iteration in range(ITERS - 1):
        col_parts = col_pass(items, xs, ys, cols, swap(row_parts, ROWS))
        row_parts = row_pass(items, xs, ys, rows, swap(col_parts, COLS))
    col_parts, source_pot = last_col_pass(
        items, xs, ys, cols, swap(row_parts, ROWS), source_norm
    )
    last = swap(col_parts.reshape(N_COLS, TSUB, TILE), COLS)
    target_pot = target_part - EPSILON * lse_over_first(last)
    return (source_pot.reshape(-1), target_pot.reshape(-1))


def solution(mesh):
    grid = Mesh(mesh.devices.reshape(DIMS), NAMES)
    placed = (
        P(NAMES, None),
        P(NAMES, None),
        P(NAMES),
        P(NAMES),
        P(NAMES),
        P(NAMES, None),
        P(NAMES),
    )
    return jax.shard_map(
        body, mesh=grid, in_specs=placed, out_specs=(P(NAMES), P(NAMES)), check_vma=False
    )
```

```python
import functools
import math

import jax
import jax.numpy as jnp
import numpy as np
from jax import lax
from jax.experimental import pallas as pl
from jax.experimental.pallas import tpu as pltpu
from jax.sharding import Mesh
from jax.sharding import PartitionSpec as P

TSUB = 8
CAP = 2
ITERS = 2
EPSILON = 0.1

DIMS = (4, 4, 4, 2)
NAMES = ("x", "y", "z", "core")
ROWS = ("y", "z")
COLS = ("x", "core")
N_ROWS = 16
N_PIECES = 12
N_COLS = 8
RING = 4
SRC = 384
TILE = 128
SUBS = SRC // TILE
FEAT = 256
TILES = N_COLS * TSUB
SLOTS = N_ROWS * N_COLS * CAP
UNROLL = 16
LAST_UNROLL = 4
EXTRA = 16
LISTED = 8 + SLOTS + 4 * LAST_UNROLL
NOTHING = TILES << 8
NORMS = 16
GAIN = 2.0 / (FEAT * EPSILON)
UNIT = 1.0 / (FEAT * EPSILON)
LOG2E = math.log2(math.e)
SPAN = 70.0


def lse_over_first(parts):
    top = jnp.max(parts, axis=0)
    base = jnp.where(top == -jnp.inf, 0.0, top)
    return top + jnp.log(jnp.sum(jnp.exp(parts - base[None]), axis=0))


def spread(values, norm_ref):
    high, low = jnp.max(values), jnp.min(values)
    reach = GAIN * jnp.sqrt(jnp.max(norm_ref[0:8]) * jnp.max(norm_ref[8:16]))
    return 0.5 * high + 0.5 * low, 0.5 * high - 0.5 * low + reach <= SPAN


def diagonal():
    return lax.broadcasted_iota(jnp.int32, (TILE, TILE), 0) == lax.broadcasted_iota(
        jnp.int32, (TILE, TILE), 1
    )


def as_row(eye, col):
    return jnp.sum(jnp.where(eye, col, 0.0), axis=0, keepdims=True)


def as_col(eye, row):
    return jnp.sum(jnp.where(eye, row, 0.0), axis=1, keepdims=True)


def products(x, y):
    return jnp.dot(x, y, preferred_element_type=jnp.float32)


def item_at(item_ref, w):
    one, two = item_ref[8 + 2 * w], item_ref[9 + 2 * w]
    return (
        one >> 20,
        (one >> 16) & 15,
        (one >> 8) & 255,
        (two >> 8) & 255,
        one & 255,
        two & 255,
    )


def exps(x, y):
    return jnp.exp2((GAIN * LOG2E) * products(x, y))


def two_tiles(y_ref, r0, r1):
    return jnp.concatenate([y_ref[r0], y_ref[r1]], axis=1)


def sweep(n_items, work):
    def steps(first, size):
        def step(w, _):
            for k in range(size):
                work(first + size * w + k)
            return 0

        return step

    whole = lax.div(n_items, UNROLL)
    lax.fori_loop(0, whole, steps(0, UNROLL), 0)
    left = n_items - UNROLL * whole
    lax.fori_loop(
        0, lax.div(left + LAST_UNROLL - 1, LAST_UNROLL), steps(UNROLL * whole, LAST_UNROLL), 0
    )


def rescale(old, new):
    return jnp.where(old == new, 1.0, jnp.exp(old - new))


def split(values):
    high = values.astype(jnp.bfloat16).astype(jnp.float32)
    rest = values - high
    middle = rest.astype(jnp.bfloat16).astype(jnp.float32)
    return [high, middle, (rest - middle).astype(jnp.bfloat16).astype(jnp.float32)]


def start_all(pairs, sems):
    copies = [pltpu.make_async_copy(src, dst, sems.at[k]) for k, (src, dst) in enumerate(pairs)]
    for copy in copies:
        copy.start()
    return copies


def prepare_kernel(*refs):
    xo_ref, yo_ref, nx_ref, part_ref = refs[7:11]
    y_ref, mass_ref, goal_ref, init_ref, tile_ref, count_ref, sems = refs[11:]
    copies = start_all(
        zip(refs[:7], (xo_ref.at[0:SRC], y_ref, mass_ref, goal_ref, init_ref, tile_ref, count_ref)),
        sems,
    )
    eye = diagonal()
    for copy in copies[2:]:
        copy.wait()
    la = jnp.log(mass_ref[...])
    lb = jnp.log(goal_ref[...])

    copies[0].wait()
    norms = []
    for b in range(SUBS):
        x = xo_ref[b * TILE : (b + 1) * TILE, :].astype(jnp.float32)
        norms.append(as_row(eye, jnp.sum(x * x, axis=1, keepdims=True)))
    nx = jnp.concatenate(norms, axis=0)
    nx_ref[...] = nx
    bound = jnp.full((1, TILE), 1.01 * jnp.max(nx))
    left = split(la) + [bound, jnp.zeros((EXTRA - 10, TILE), jnp.float32)]
    right = [
        tile_ref[...].astype(jnp.float32),
        count_ref[...].astype(jnp.float32),
        jnp.zeros((EXTRA - 3, TILE), jnp.float32),
    ]
    extra = jnp.concatenate(
        [jnp.concatenate(left, axis=0), jnp.concatenate(right, axis=0)], axis=1
    )
    xo_ref[SRC:] = extra.astype(jnp.bfloat16)

    copies[1].wait()
    norms = []
    for t in range(TSUB):
        y = y_ref[t * TILE : (t + 1) * TILE, :].astype(jnp.float32).T
        norms.append(jnp.sum(y * y, axis=0, keepdims=True))
        yo_ref[t, 0:FEAT] = y.astype(jnp.bfloat16)
    ny = jnp.concatenate(norms, axis=0)
    part_ref[...] = EPSILON * (lb + UNIT * ny)
    a0 = init_ref[...] / EPSILON - ny * UNIT
    parts = split(a0) + split(lb)
    bound = jnp.full((1, TILE), 1.01 * jnp.max(ny))
    for t in range(TSUB):
        rows = [part[t : t + 1] for part in parts]
        rows += [bound, jnp.zeros((EXTRA - 7, TILE), jnp.float32)]
        yo_ref[t, FEAT:] = jnp.concatenate(rows, axis=0).astype(jnp.bfloat16)


def gray(k):
    return k ^ (k >> 1)


def ring_place(offset, first):
    place = gray(offset)
    other = ((place & 1) << 1) | (place >> 1)
    return jnp.where(first == 0, place, other)


def piece_copies(x_refs, y_refs, xs, ys, x_rows, y_rows):
    pairs = []
    for half in range(2):
        for later in range(RING):
            place = pl.ds(RING * later + 2 * half, 2)
            pairs.append((x_refs[RING * half + later].at[:, x_rows, :], xs.at[place]))
    start = 0
    for piece in y_refs:
        pairs.append((piece.at[:, y_rows, :], ys.at[pl.ds(start, piece.shape[0])]))
        start += piece.shape[0]
    return pairs


def first_kernel(*refs):
    at_ref, pieces = refs[0], refs[1 : 1 + N_PIECES]
    x_refs, y_refs = pieces[: 2 * RING], pieces[2 * RING :]
    out_ref, item_ref, cols_ref, rows_ref, xs, ys = refs[1 + N_PIECES : 7 + N_PIECES]
    a_buf, u_buf, acc, top, sems = refs[7 + N_PIECES : 12 + N_PIECES]
    a_ref, table, compact, numbers, x_extra, y_extra, small_sems, sem = refs[12 + N_PIECES :]
    la_ref, lb_ref = cols_ref.at[NORMS:], rows_ref.at[NORMS:]
    x, y, z, core = (at_ref[k] for k in range(4))

    small = start_all(
        piece_copies(
            x_refs, y_refs, x_extra, y_extra, slice(SRC, SRC + EXTRA), slice(FEAT, FEAT + EXTRA)
        ),
        small_sems,
    )
    large = start_all(
        piece_copies(x_refs, y_refs, xs, ys, slice(0, SRC), slice(0, FEAT)), sems
    )
    for copy in small:
        copy.wait()

    lane = lax.broadcasted_iota(jnp.int32, (CAP, TILE), 1)
    px, side = lane >> 5, lane & 1
    start = RING * (side ^ core) + ring_place(px ^ x, side)
    entry_base = ((TSUB * (2 * px + side)) << 8) + TSUB * start

    bound = None
    for later in range(RING):
        for sooner in range(RING):
            one, two = gray(sooner), gray(later)
            off_y = jnp.where(core == 0, one, two)
            off_z = jnp.where(core == 0, two, one)
            s = RING * (y ^ off_y) + (z ^ off_z)
            extra = x_extra[RING * later + sooner].astype(jnp.float32)
            la = extra[0:3, :TILE] + extra[3:6, :TILE] + extra[6:9, :TILE]
            for b in range(SUBS):
                la_ref[pl.ds(SUBS * s + b, 1), :] = la[b : b + 1]
            here = extra[9:10, :TILE]
            bound = here if bound is None else jnp.maximum(bound, here)
            numbers_here = extra[0:3, TILE:].astype(jnp.int32)
            head = (s << 20) | ((RING * later + sooner) << 16)
            entry = head | (entry_base + 257 * numbers_here[0:CAP])
            slot = lax.broadcasted_iota(jnp.int32, (CAP, TILE), 0)
            entry = jnp.where(slot < numbers_here[CAP : CAP + 1], entry, -1)
            for e in range(CAP):
                table[pl.ds(N_ROWS * e + s, 1), :] = entry[e : e + 1]
    for ref in (cols_ref, rows_ref):
        ref[0:8] = jnp.broadcast_to(bound, (8, TILE))

    lane = lax.broadcasted_iota(jnp.int32, (N_ROWS, TILE), 1) & (2 * N_ROWS - 1)
    moved = pltpu.roll(table[...], (TILE - 2 * (RING * y + z)) & (TILE - 1), axis=1)
    second = pltpu.roll(moved[N_ROWS:], 2, axis=1)
    compact[...] = jnp.where(lane < 2, moved[:N_ROWS], second)
    copy = pltpu.make_async_copy(compact, numbers, sem)
    copy.start()

    bound = None
    for k in range(2 * RING):
        side = core ^ (k // RING)
        place = k % RING
        offset = jnp.where(side == 0, gray(place), (0, 3, 1, 2)[place])
        owner = 2 * (x ^ offset) + side
        extra = y_extra[TSUB * k : TSUB * (k + 1)].astype(jnp.float32)
        rows = pl.ds(pl.multiple_of(TSUB * owner, TSUB), TSUB)
        a_ref[rows, :] = extra[:, 0] + extra[:, 1] + extra[:, 2]
        lb_ref[rows, :] = extra[:, 3] + extra[:, 4] + extra[:, 5]
        here = extra[0, 6:7]
        bound = here if bound is None else jnp.maximum(bound, here)
    for ref in (cols_ref, rows_ref):
        ref[8:16] = jnp.broadcast_to(bound, (8, TILE))

    copy.wait()

    def block(s, place):
        for px in range(RING):
            for side in range(2):
                for e in range(CAP):
                    entry = numbers[s, 2 * N_ROWS * px + 2 * e + side]
                    item_ref[place] = entry
                    place = place + jnp.where(entry >= 0, 1, 0)
        item_ref[place] = jnp.int32(NOTHING)
        return place + (place & 1)

    end = lax.fori_loop(0, N_ROWS, block, jnp.int32(8))
    for k in range(2 * LAST_UNROLL):
        item_ref[end + k] = jnp.int32(NOTHING)
    item_ref[0] = (end - 8) >> 1
    item_ref[1] = RING * y + z
    for copy in large:
        copy.wait()
    row_core(a_ref[...], item_ref, xs, ys, cols_ref, out_ref, a_buf, u_buf, acc, top)


def row_kernel(item_ref, x_ref, y_ref, side_ref, parts_ref, out_ref, a_buf, u_buf, acc, top):
    a = side_ref[NORMS:] - lse_over_first(parts_ref[...])
    row_core(a, item_ref, x_ref, y_ref, side_ref, out_ref, a_buf, u_buf, acc, top)


def row_core(a, item_ref, x_ref, y_ref, norm_ref, out_ref, a_buf, u_buf, acc, top):
    mid, fast = spread(a, norm_ref)
    n_items = item_ref[0]
    eye = diagonal()

    acc[...] = jnp.zeros_like(acc)

    @pl.when(fast)
    def _():
        u_buf[0:TILES] = jnp.exp(a - mid)
        u_buf[TILES:] = jnp.zeros((8, TILE), jnp.float32)

        def work(w):
            s, h, t0, t1, r0, r1 = item_at(item_ref, w)
            u0, u1 = u_buf[pl.ds(t0, 1), :], u_buf[pl.ds(t1, 1), :]
            e = exps(x_ref[h], two_tiles(y_ref, r0, r1))
            acc[s] += e[:, :TILE] * u0 + e[:, TILE:] * u1

        sweep(n_items, work)
        for k in range(N_ROWS * SUBS):
            s, b = k // SUBS, k % SUBS
            col = jnp.sum(acc[s, b * TILE : (b + 1) * TILE, :], axis=1, keepdims=True)
            a_buf[k : k + 1, :] = as_row(eye, col)
        done = mid + jnp.log(a_buf[0 : N_ROWS * SUBS])
        out_ref[...] = jnp.broadcast_to(done[None], out_ref.shape)

    @pl.when(jnp.logical_not(fast))
    def _():
        a_buf[0:TILES] = a
        a_buf[TILES:] = jnp.zeros((8, TILE), jnp.float32)
        top[...] = jnp.full_like(top, -jnp.inf)

        def step(w, _):
            s, h, t0, t1, r0, r1 = item_at(item_ref, w)
            for t, r in ((t0, r0), (t1, r1)):

                @pl.when(t < TILES)
                def _(t=t, r=r):
                    score = GAIN * products(x_ref[h], y_ref[r]) + a_buf[pl.ds(t, 1), :]
                    old = top[s]
                    new = jnp.maximum(old, score)
                    acc[s] = acc[s] * rescale(old, new) + jnp.exp(score - new)
                    top[s] = new

            return 0

        lax.fori_loop(0, n_items, step, 0)

        def finish(k, _):
            s, b = lax.div(k, SUBS), lax.rem(k, SUBS)
            rows = pl.ds(pl.multiple_of(b * TILE, TILE), TILE)
            block = top[s, rows, :]
            high = jnp.max(block, axis=1, keepdims=True)
            base = jnp.where(high == -jnp.inf, 0.0, high)
            total = jnp.sum(acc[s, rows, :] * jnp.exp(block - base), axis=1, keepdims=True)
            high_row = jnp.max(jnp.where(eye, high, -jnp.inf), axis=0, keepdims=True)
            done = high_row + jnp.log(as_row(eye, total))
            out_ref[:, pl.ds(k, 1), :] = jnp.broadcast_to(done[None], (N_ROWS, 1, TILE))
            return 0

        lax.fori_loop(0, N_ROWS * SUBS, finish, 0)


def last_col_kernel(
    item_ref, x_ref, y_ref, side_ref, parts_ref, norm_ref, out_ref, f_ref, b_buf, *scratch
):
    b = side_ref[NORMS:] - lse_over_first(parts_ref[...])
    b_buf[...] = b
    for k in range(SUBS):
        here = b_buf[pl.ds(SUBS * item_ref[1] + k, 1), :]
        f_ref[k : k + 1, :] = EPSILON * (here + UNIT * norm_ref[k : k + 1, :])
    col_core(b, item_ref, x_ref, y_ref, side_ref, out_ref, *scratch)


def col_kernel(item_ref, x_ref, y_ref, side_ref, parts_ref, out_ref, *scratch):
    b = side_ref[NORMS:] - lse_over_first(parts_ref[...])
    col_core(b, item_ref, x_ref, y_ref, side_ref, out_ref, *scratch)


def col_core(b, item_ref, x_ref, y_ref, norm_ref, out_ref, spread_buf, acc, top):
    mid, fast = spread(b, norm_ref)
    n_items = item_ref[0]
    eye = diagonal()

    def lay_out(values):
        for k in range(N_ROWS * SUBS):
            s, part = k // SUBS, k % SUBS
            col = as_col(eye, values[k : k + 1, :])
            spread_buf[s, part * TILE : (part + 1) * TILE, :] = jnp.broadcast_to(col, (TILE, TILE))

    acc[...] = jnp.zeros_like(acc)

    @pl.when(fast)
    def _():
        lay_out(jnp.exp(b - mid))

        def work(w):
            s, h, t0, t1, r0, r1 = item_at(item_ref, w)
            e = exps(x_ref[h], two_tiles(y_ref, r0, r1))
            v = spread_buf[s]
            acc[t0] += jnp.sum((e[:, :TILE] * v).reshape(SRC // 8, 8, TILE), axis=0)
            acc[t1] += jnp.sum((e[:, TILE:] * v).reshape(SRC // 8, 8, TILE), axis=0)

        sweep(n_items, work)
        done = mid + jnp.log(jnp.sum(acc[0:TILES], axis=1))
        out_ref[...] = jnp.broadcast_to(done[None], out_ref.shape)

    @pl.when(jnp.logical_not(fast))
    def _():
        lay_out(b)
        top[...] = jnp.full_like(top, -jnp.inf)

        def step(w, _):
            s, h, t0, t1, r0, r1 = item_at(item_ref, w)
            for t, r in ((t0, r0), (t1, r1)):

                @pl.when(t < TILES)
                def _(t=t, r=r):
                    score = GAIN * products(x_ref[h], y_ref[r]) + spread_buf[s]
                    score = score.reshape(SRC // 8, 8, TILE)
                    old = top[t]
                    new = jnp.maximum(old, jnp.max(score, axis=0))
                    acc[t] = acc[t] * rescale(old, new) + jnp.sum(
                        jnp.exp(score - new[None]), axis=0
                    )
                    top[t] = new

            return 0

        lax.fori_loop(0, n_items, step, 0)
        high = jnp.max(top[0:TILES], axis=1)
        base = jnp.where(high == -jnp.inf, 0.0, high)
        total = jnp.sum(acc[0:TILES] * jnp.exp(top[0:TILES] - base[:, None, :]), axis=1)
        out_ref[...] = jnp.broadcast_to((high + jnp.log(total))[None], out_ref.shape)


VMEM = pl.BlockSpec(memory_space=pltpu.VMEM)
ANY = pl.BlockSpec(memory_space=pl.ANY)
SMEM = pl.BlockSpec(memory_space=pltpu.SMEM)


def limit(mebibytes):
    return pltpu.CompilerParams(vmem_limit_bytes=mebibytes * 1024 * 1024)


def shape(dims, dtype=jnp.float32):
    return jax.ShapeDtypeStruct(dims, dtype)


def prepare(*operands):
    return pl.pallas_call(
        prepare_kernel,
        out_shape=(
            shape((SRC + EXTRA, FEAT), jnp.bfloat16),
            shape((TSUB, FEAT + EXTRA, TILE), jnp.bfloat16),
            shape((SUBS, TILE)),
            shape((TSUB, TILE)),
        ),
        in_specs=[ANY] * 7,
        out_specs=(VMEM,) * 4,
        scratch_shapes=[
            pltpu.VMEM((TSUB * TILE, FEAT), jnp.bfloat16),
            pltpu.VMEM((SUBS, TILE), jnp.float32),
            pltpu.VMEM((TSUB, TILE), jnp.float32),
            pltpu.VMEM((TSUB, TILE), jnp.float32),
            pltpu.VMEM((CAP, TILE), jnp.int32),
            pltpu.VMEM((1, TILE), jnp.int32),
            pltpu.SemaphoreType.DMA((7,)),
        ],
        compiler_params=limit(60),
        name="prepare",
    )(*operands)


ROW_SCRATCH = [
    pltpu.VMEM((TILES + 8, TILE), jnp.float32),
    pltpu.VMEM((TILES + 8, TILE), jnp.float32),
    pltpu.VMEM((N_ROWS, SRC, TILE), jnp.float32),
    pltpu.VMEM((N_ROWS, SRC, TILE), jnp.float32),
]
COL_SCRATCH = [
    pltpu.VMEM((N_ROWS, SRC, TILE), jnp.float32),
    pltpu.VMEM((TILES + 1, 8, TILE), jnp.float32),
    pltpu.VMEM((TILES + 1, 8, TILE), jnp.float32),
]
ROW_PARTS = shape((N_ROWS, N_ROWS * SUBS, TILE))


def first_pass(at, pieces):
    return pl.pallas_call(
        first_kernel,
        out_shape=(
            ROW_PARTS,
            shape((LISTED,), jnp.int32),
            shape((NORMS + N_ROWS * SUBS, TILE)),
            shape((NORMS + TILES, TILE)),
            shape((N_ROWS, SRC, FEAT), jnp.bfloat16),
            shape((TILES, FEAT, TILE), jnp.bfloat16),
        ),
        in_specs=[SMEM] + [ANY] * N_PIECES,
        out_specs=(VMEM, SMEM, VMEM, VMEM, VMEM, VMEM),
        scratch_shapes=ROW_SCRATCH
        + [
            pltpu.SemaphoreType.DMA((N_PIECES,)),
            pltpu.VMEM((TILES, TILE), jnp.float32),
            pltpu.VMEM((CAP * N_ROWS, TILE), jnp.int32),
            pltpu.VMEM((N_ROWS, TILE), jnp.int32),
            pltpu.SMEM((N_ROWS, TILE), jnp.int32),
            pltpu.VMEM((N_ROWS, EXTRA, FEAT), jnp.bfloat16),
            pltpu.VMEM((TILES, EXTRA, TILE), jnp.bfloat16),
            pltpu.SemaphoreType.DMA((N_PIECES,)),
            pltpu.SemaphoreType.DMA,
        ],
        compiler_params=limit(24),
        name="first_row_pass",
    )(at, *[pltpu.with_memory_space_constraint(piece, pltpu.HBM) for piece in pieces])


def row_pass(items, *operands):
    return pl.pallas_call(
        row_kernel,
        out_shape=ROW_PARTS,
        in_specs=[SMEM] + [VMEM] * len(operands),
        out_specs=VMEM,
        scratch_shapes=ROW_SCRATCH,
        compiler_params=limit(20),
        name="row_pass",
    )(items, *operands)


def col_pass(items, *operands):
    return pl.pallas_call(
        col_kernel,
        out_shape=shape((N_COLS, TILES, TILE)),
        in_specs=[SMEM] + [VMEM] * len(operands),
        out_specs=VMEM,
        scratch_shapes=COL_SCRATCH,
        compiler_params=limit(20),
        name="col_pass",
    )(items, *operands)


def last_col_pass(items, *operands):
    return pl.pallas_call(
        last_col_kernel,
        out_shape=(shape((1, TILES, TILE)), shape((SUBS, TILE))),
        in_specs=[SMEM] + [VMEM] * len(operands),
        out_specs=(VMEM, VMEM),
        scratch_shapes=[pltpu.VMEM((N_ROWS * SUBS, TILE), jnp.float32)] + COL_SCRATCH,
        compiler_params=limit(20),
        name="last_col_pass",
    )(items, *operands)


def swap(blocks, axes):
    return lax.all_to_all(blocks, axes, split_axis=0, concat_axis=0, tiled=True)


def exchange(block, partner):
    pairs = []
    for place in range(N_ROWS * N_COLS):
        at = tuple(int(k) for k in np.unravel_index(place, DIMS))
        pairs.append((place, int(np.ravel_multi_index(partner(*at), DIMS))))
    return lax.ppermute(block, NAMES, pairs)


def doubled(block, partner):
    return jnp.concatenate([block, exchange(block, partner)])


def after(value, events):
    return lax.optimization_barrier((value, events))[0]


def gather_all(sources, targets):
    along = [source_partner(0, flip) for flip in (1, 3)]
    across = [source_partner(1, flip) for flip in (1, 3)]
    beside = [target_partner(order) for order in (0, 1)]

    pair = jnp.stack([sources, exchange(sources, along[0])])
    tiles = jnp.concatenate([targets, exchange(targets, beside[0])])
    other = exchange(pair, along[1])
    first, second = exchange(pair, across[0]), exchange(pair, across[1])
    further = exchange(after(tiles, pair), beside[1])
    relayed = exchange(first, across[1])
    pieces = [pair, first, second, relayed]
    near = exchange(after(tiles, (first, second)), sibling)
    first, second = exchange(other, across[0]), exchange(other, across[1])
    pieces += [other, first, second, exchange(second, across[0])]
    far = exchange(after(further, (relayed, first, pieces[-1])), sibling)
    return pieces + [tiles, further, near, far]


def source_partner(stage, flip):
    def partner(x, y, z, core):
        return (x, y ^ flip, z, core) if stage == core else (x, y, z ^ flip, core)

    return partner


def target_partner(order):
    return lambda x, y, z, core: (x ^ (1, 3)[order ^ core], y, z, core)


def sibling(x, y, z, core):
    return (x, y, z, core ^ 1)


def body(
    source_points, target_points, source_mass, target_mass, target_init, pair_tiles, pair_count
):
    x_block, y_block, source_norm, target_part = prepare(
        source_points,
        target_points,
        source_mass.reshape(SUBS, TILE),
        target_mass.reshape(TSUB, TILE),
        target_init.reshape(TSUB, TILE),
        pair_tiles.T,
        pair_count.reshape(1, -1),
    )
    pieces = gather_all(x_block, y_block)

    at = jnp.stack([lax.axis_index(name) for name in NAMES]).astype(jnp.int32)
    row_parts, items, cols, rows, xs, ys = first_pass(at, pieces)
    for iteration in range(ITERS - 1):
        col_parts = col_pass(items, xs, ys, cols, swap(row_parts, ROWS))
        row_parts = row_pass(items, xs, ys, rows, swap(col_parts, COLS))
    col_parts, source_pot = last_col_pass(
        items, xs, ys, cols, swap(row_parts, ROWS), source_norm
    )
    last = swap(col_parts.reshape(N_COLS, TSUB, TILE), COLS)
    target_pot = target_part - EPSILON * lse_over_first(last)
    return (source_pot.reshape(-1), target_pot.reshape(-1))


def solution(mesh):
    grid = Mesh(mesh.devices.reshape(DIMS), NAMES)
    placed = (
        P(NAMES, None),
        P(NAMES, None),
        P(NAMES),
        P(NAMES),
        P(NAMES),
        P(NAMES, None),
        P(NAMES),
    )
    return jax.shard_map(
        body, mesh=grid, in_specs=placed, out_specs=(P(NAMES), P(NAMES)), check_vma=False
    )
```

```python
import functools
import math

import jax
import jax.numpy as jnp
import numpy as np
from jax import lax
from jax.experimental import pallas as pl
from jax.experimental.pallas import tpu as pltpu
from jax.sharding import Mesh
from jax.sharding import PartitionSpec as P

TSUB = 8
CAP = 2
ITERS = 2
EPSILON = 0.1

DIMS = (4, 4, 4, 2)
NAMES = ("x", "y", "z", "core")
ROWS = ("y", "z")
COLS = ("x", "core")
N_ROWS = 16
N_PIECES = 12
N_COLS = 8
RING = 4
SRC = 384
TILE = 128
SUBS = SRC // TILE
FEAT = 256
TILES = N_COLS * TSUB
SLOTS = N_ROWS * N_COLS * CAP
UNROLL = 16
LAST_UNROLL = 4
EXTRA = 16
LISTED = 8 + SLOTS + 4 * LAST_UNROLL
NOTHING = TILES << 8
NORMS = 16
GAIN = 2.0 / (FEAT * EPSILON)
UNIT = 1.0 / (FEAT * EPSILON)
LOG2E = math.log2(math.e)
SPAN = 70.0


def lse_over_first(parts):
    top = jnp.max(parts, axis=0)
    base = jnp.where(top == -jnp.inf, 0.0, top)
    return top + jnp.log(jnp.sum(jnp.exp(parts - base[None]), axis=0))


def spread(values, norm_ref):
    high, low = jnp.max(values), jnp.min(values)
    reach = GAIN * jnp.sqrt(jnp.max(norm_ref[0:8]) * jnp.max(norm_ref[8:16]))
    return 0.5 * high + 0.5 * low, 0.5 * high - 0.5 * low + reach <= SPAN


def diagonal():
    return lax.broadcasted_iota(jnp.int32, (TILE, TILE), 0) == lax.broadcasted_iota(
        jnp.int32, (TILE, TILE), 1
    )


def as_row(eye, col):
    return jnp.sum(jnp.where(eye, col, 0.0), axis=0, keepdims=True)


def as_col(eye, row):
    return jnp.sum(jnp.where(eye, row, 0.0), axis=1, keepdims=True)


def products(x, y):
    return jnp.dot(x, y, preferred_element_type=jnp.float32)


def item_at(item_ref, w):
    one, two = item_ref[8 + 2 * w], item_ref[9 + 2 * w]
    return (
        one >> 20,
        (one >> 16) & 15,
        (one >> 8) & 255,
        (two >> 8) & 255,
        one & 255,
        two & 255,
    )


def exps(x, y):
    return jnp.exp2((GAIN * LOG2E) * products(x, y))


def two_tiles(y_ref, r0, r1):
    return jnp.concatenate([y_ref[r0], y_ref[r1]], axis=1)


def sweep(n_items, work):
    def steps(first, size):
        def step(w, _):
            for k in range(size):
                work(first + size * w + k)
            return 0

        return step

    whole = lax.div(n_items, UNROLL)
    lax.fori_loop(0, whole, steps(0, UNROLL), 0)
    left = n_items - UNROLL * whole
    lax.fori_loop(
        0, lax.div(left + LAST_UNROLL - 1, LAST_UNROLL), steps(UNROLL * whole, LAST_UNROLL), 0
    )


def rescale(old, new):
    return jnp.where(old == new, 1.0, jnp.exp(old - new))


def split(values):
    high = values.astype(jnp.bfloat16).astype(jnp.float32)
    rest = values - high
    middle = rest.astype(jnp.bfloat16).astype(jnp.float32)
    return [high, middle, (rest - middle).astype(jnp.bfloat16).astype(jnp.float32)]


def start_all(pairs, sems):
    copies = [pltpu.make_async_copy(src, dst, sems.at[k]) for k, (src, dst) in enumerate(pairs)]
    for copy in copies:
        copy.start()
    return copies


def source_kernel(*refs):
    xo_ref, nx_ref, mass_ref, tile_ref, count_ref, sems = refs[4:]
    copies = start_all(zip(refs[:4], (xo_ref.at[0:SRC], mass_ref, tile_ref, count_ref)), sems)
    eye = diagonal()
    for copy in copies:
        copy.wait()
    la = jnp.log(mass_ref[...])
    norms = []
    for b in range(SUBS):
        x = xo_ref[b * TILE : (b + 1) * TILE, :].astype(jnp.float32)
        norms.append(as_row(eye, jnp.sum(x * x, axis=1, keepdims=True)))
    nx = jnp.concatenate(norms, axis=0)
    nx_ref[...] = nx
    bound = jnp.full((1, TILE), 1.01 * jnp.max(nx))
    left = split(la) + [bound, jnp.zeros((EXTRA - 10, TILE), jnp.float32)]
    right = [
        tile_ref[...].astype(jnp.float32),
        count_ref[...].astype(jnp.float32),
        jnp.zeros((EXTRA - 3, TILE), jnp.float32),
    ]
    extra = jnp.concatenate(
        [jnp.concatenate(left, axis=0), jnp.concatenate(right, axis=0)], axis=1
    )
    xo_ref[SRC:] = extra.astype(jnp.bfloat16)


def target_kernel(*refs):
    yo_ref, part_ref, y_ref, goal_ref, init_ref, sems = refs[3:]
    copies = start_all(zip(refs[:3], (y_ref, goal_ref, init_ref)), sems)
    for copy in copies:
        copy.wait()
    lb = jnp.log(goal_ref[...])
    norms = []
    for t in range(TSUB):
        y = y_ref[t * TILE : (t + 1) * TILE, :].astype(jnp.float32).T
        norms.append(jnp.sum(y * y, axis=0, keepdims=True))
        yo_ref[t, 0:FEAT] = y.astype(jnp.bfloat16)
    ny = jnp.concatenate(norms, axis=0)
    part_ref[...] = EPSILON * (lb + UNIT * ny)
    a0 = init_ref[...] / EPSILON - ny * UNIT
    parts = split(a0) + split(lb)
    bound = jnp.full((1, TILE), 1.01 * jnp.max(ny))
    for t in range(TSUB):
        rows = [part[t : t + 1] for part in parts]
        rows += [bound, jnp.zeros((EXTRA - 7, TILE), jnp.float32)]
        yo_ref[t, FEAT:] = jnp.concatenate(rows, axis=0).astype(jnp.bfloat16)


def gray(k):
    return k ^ (k >> 1)


def ring_place(offset, first):
    place = gray(offset)
    other = ((place & 1) << 1) | (place >> 1)
    return jnp.where(first == 0, place, other)


def piece_copies(x_refs, y_refs, xs, ys, x_rows, y_rows):
    pairs = []
    for half in range(2):
        for later in range(RING):
            place = pl.ds(RING * later + 2 * half, 2)
            pairs.append((x_refs[RING * half + later].at[:, x_rows, :], xs.at[place]))
    start = 0
    for piece in y_refs:
        pairs.append((piece.at[:, y_rows, :], ys.at[pl.ds(start, piece.shape[0])]))
        start += piece.shape[0]
    return pairs


def first_kernel(*refs):
    at_ref, pieces = refs[0], refs[1 : 1 + N_PIECES]
    x_refs, y_refs = pieces[: 2 * RING], pieces[2 * RING :]
    out_ref, item_ref, cols_ref, rows_ref, xs, ys = refs[1 + N_PIECES : 7 + N_PIECES]
    a_buf, u_buf, acc, top, sems = refs[7 + N_PIECES : 12 + N_PIECES]
    a_ref, table, compact, numbers, x_extra, y_extra, small_sems, sem = refs[12 + N_PIECES :]
    la_ref, lb_ref = cols_ref.at[NORMS:], rows_ref.at[NORMS:]
    x, y, z, core = (at_ref[k] for k in range(4))

    small = start_all(
        piece_copies(
            x_refs, y_refs, x_extra, y_extra, slice(SRC, SRC + EXTRA), slice(FEAT, FEAT + EXTRA)
        ),
        small_sems,
    )
    large = start_all(
        piece_copies(x_refs, y_refs, xs, ys, slice(0, SRC), slice(0, FEAT)), sems
    )
    for copy in small:
        copy.wait()

    lane = lax.broadcasted_iota(jnp.int32, (CAP, TILE), 1)
    px, side = lane >> 5, lane & 1
    start = RING * (side ^ core) + ring_place(px ^ x, side)
    entry_base = ((TSUB * (2 * px + side)) << 8) + TSUB * start

    bound = None
    for later in range(RING):
        for sooner in range(RING):
            one, two = gray(sooner), gray(later)
            off_y = jnp.where(core == 0, one, two)
            off_z = jnp.where(core == 0, two, one)
            s = RING * (y ^ off_y) + (z ^ off_z)
            extra = x_extra[RING * later + sooner].astype(jnp.float32)
            la = extra[0:3, :TILE] + extra[3:6, :TILE] + extra[6:9, :TILE]
            for b in range(SUBS):
                la_ref[pl.ds(SUBS * s + b, 1), :] = la[b : b + 1]
            here = extra[9:10, :TILE]
            bound = here if bound is None else jnp.maximum(bound, here)
            numbers_here = extra[0:3, TILE:].astype(jnp.int32)
            head = (s << 20) | ((RING * later + sooner) << 16)
            entry = head | (entry_base + 257 * numbers_here[0:CAP])
            slot = lax.broadcasted_iota(jnp.int32, (CAP, TILE), 0)
            entry = jnp.where(slot < numbers_here[CAP : CAP + 1], entry, -1)
            for e in range(CAP):
                table[pl.ds(N_ROWS * e + s, 1), :] = entry[e : e + 1]
    for ref in (cols_ref, rows_ref):
        ref[0:8] = jnp.broadcast_to(bound, (8, TILE))

    lane = lax.broadcasted_iota(jnp.int32, (N_ROWS, TILE), 1) & (2 * N_ROWS - 1)
    moved = pltpu.roll(table[...], (TILE - 2 * (RING * y + z)) & (TILE - 1), axis=1)
    second = pltpu.roll(moved[N_ROWS:], 2, axis=1)
    compact[...] = jnp.where(lane < 2, moved[:N_ROWS], second)
    copy = pltpu.make_async_copy(compact, numbers, sem)
    copy.start()

    bound = None
    for k in range(2 * RING):
        side = core ^ (k // RING)
        place = k % RING
        offset = jnp.where(side == 0, gray(place), (0, 3, 1, 2)[place])
        owner = 2 * (x ^ offset) + side
        extra = y_extra[TSUB * k : TSUB * (k + 1)].astype(jnp.float32)
        rows = pl.ds(pl.multiple_of(TSUB * owner, TSUB), TSUB)
        a_ref[rows, :] = extra[:, 0] + extra[:, 1] + extra[:, 2]
        lb_ref[rows, :] = extra[:, 3] + extra[:, 4] + extra[:, 5]
        here = extra[0, 6:7]
        bound = here if bound is None else jnp.maximum(bound, here)
    for ref in (cols_ref, rows_ref):
        ref[8:16] = jnp.broadcast_to(bound, (8, TILE))

    copy.wait()

    def block(s, place):
        for px in range(RING):
            for side in range(2):
                for e in range(CAP):
                    entry = numbers[s, 2 * N_ROWS * px + 2 * e + side]
                    item_ref[place] = entry
                    place = place + jnp.where(entry >= 0, 1, 0)
        item_ref[place] = jnp.int32(NOTHING)
        return place + (place & 1)

    end = lax.fori_loop(0, N_ROWS, block, jnp.int32(8))
    for k in range(2 * LAST_UNROLL):
        item_ref[end + k] = jnp.int32(NOTHING)
    item_ref[0] = (end - 8) >> 1
    item_ref[1] = RING * y + z
    for copy in large:
        copy.wait()
    row_core(a_ref[...], item_ref, xs, ys, cols_ref, out_ref, a_buf, u_buf, acc, top)


def row_kernel(item_ref, x_ref, y_ref, side_ref, parts_ref, out_ref, a_buf, u_buf, acc, top):
    a = side_ref[NORMS:] - lse_over_first(parts_ref[...])
    row_core(a, item_ref, x_ref, y_ref, side_ref, out_ref, a_buf, u_buf, acc, top)


def row_core(a, item_ref, x_ref, y_ref, norm_ref, out_ref, a_buf, u_buf, acc, top):
    mid, fast = spread(a, norm_ref)
    n_items = item_ref[0]
    eye = diagonal()

    acc[...] = jnp.zeros_like(acc)

    @pl.when(fast)
    def _():
        u_buf[0:TILES] = jnp.exp(a - mid)
        u_buf[TILES:] = jnp.zeros((8, TILE), jnp.float32)

        def work(w):
            s, h, t0, t1, r0, r1 = item_at(item_ref, w)
            u0, u1 = u_buf[pl.ds(t0, 1), :], u_buf[pl.ds(t1, 1), :]
            e = exps(x_ref[h], two_tiles(y_ref, r0, r1))
            acc[s] += e[:, :TILE] * u0 + e[:, TILE:] * u1

        sweep(n_items, work)
        for k in range(N_ROWS * SUBS):
            s, b = k // SUBS, k % SUBS
            col = jnp.sum(acc[s, b * TILE : (b + 1) * TILE, :], axis=1, keepdims=True)
            a_buf[k : k + 1, :] = as_row(eye, col)
        done = mid + jnp.log(a_buf[0 : N_ROWS * SUBS])
        out_ref[...] = jnp.broadcast_to(done[None], out_ref.shape)

    @pl.when(jnp.logical_not(fast))
    def _():
        a_buf[0:TILES] = a
        a_buf[TILES:] = jnp.zeros((8, TILE), jnp.float32)
        top[...] = jnp.full_like(top, -jnp.inf)

        def step(w, _):
            s, h, t0, t1, r0, r1 = item_at(item_ref, w)
            for t, r in ((t0, r0), (t1, r1)):

                @pl.when(t < TILES)
                def _(t=t, r=r):
                    score = GAIN * products(x_ref[h], y_ref[r]) + a_buf[pl.ds(t, 1), :]
                    old = top[s]
                    new = jnp.maximum(old, score)
                    acc[s] = acc[s] * rescale(old, new) + jnp.exp(score - new)
                    top[s] = new

            return 0

        lax.fori_loop(0, n_items, step, 0)

        def finish(k, _):
            s, b = lax.div(k, SUBS), lax.rem(k, SUBS)
            rows = pl.ds(pl.multiple_of(b * TILE, TILE), TILE)
            block = top[s, rows, :]
            high = jnp.max(block, axis=1, keepdims=True)
            base = jnp.where(high == -jnp.inf, 0.0, high)
            total = jnp.sum(acc[s, rows, :] * jnp.exp(block - base), axis=1, keepdims=True)
            high_row = jnp.max(jnp.where(eye, high, -jnp.inf), axis=0, keepdims=True)
            done = high_row + jnp.log(as_row(eye, total))
            out_ref[:, pl.ds(k, 1), :] = jnp.broadcast_to(done[None], (N_ROWS, 1, TILE))
            return 0

        lax.fori_loop(0, N_ROWS * SUBS, finish, 0)


def last_col_kernel(
    item_ref, x_ref, y_ref, side_ref, parts_ref, norm_ref, out_ref, f_ref, b_buf, *scratch
):
    b = side_ref[NORMS:] - lse_over_first(parts_ref[...])
    b_buf[...] = b
    for k in range(SUBS):
        here = b_buf[pl.ds(SUBS * item_ref[1] + k, 1), :]
        f_ref[k : k + 1, :] = EPSILON * (here + UNIT * norm_ref[k : k + 1, :])
    col_core(b, item_ref, x_ref, y_ref, side_ref, out_ref, *scratch)


def col_kernel(item_ref, x_ref, y_ref, side_ref, parts_ref, out_ref, *scratch):
    b = side_ref[NORMS:] - lse_over_first(parts_ref[...])
    col_core(b, item_ref, x_ref, y_ref, side_ref, out_ref, *scratch)


def col_core(b, item_ref, x_ref, y_ref, norm_ref, out_ref, spread_buf, acc, top):
    mid, fast = spread(b, norm_ref)
    n_items = item_ref[0]
    eye = diagonal()

    def lay_out(values):
        for k in range(N_ROWS * SUBS):
            s, part = k // SUBS, k % SUBS
            col = as_col(eye, values[k : k + 1, :])
            spread_buf[s, part * TILE : (part + 1) * TILE, :] = jnp.broadcast_to(col, (TILE, TILE))

    acc[...] = jnp.zeros_like(acc)

    @pl.when(fast)
    def _():
        lay_out(jnp.exp(b - mid))

        def work(w):
            s, h, t0, t1, r0, r1 = item_at(item_ref, w)
            e = exps(x_ref[h], two_tiles(y_ref, r0, r1))
            v = spread_buf[s]
            acc[t0] += jnp.sum((e[:, :TILE] * v).reshape(SRC // 8, 8, TILE), axis=0)
            acc[t1] += jnp.sum((e[:, TILE:] * v).reshape(SRC // 8, 8, TILE), axis=0)

        sweep(n_items, work)
        done = mid + jnp.log(jnp.sum(acc[0:TILES], axis=1))
        out_ref[...] = jnp.broadcast_to(done[None], out_ref.shape)

    @pl.when(jnp.logical_not(fast))
    def _():
        lay_out(b)
        top[...] = jnp.full_like(top, -jnp.inf)

        def step(w, _):
            s, h, t0, t1, r0, r1 = item_at(item_ref, w)
            for t, r in ((t0, r0), (t1, r1)):

                @pl.when(t < TILES)
                def _(t=t, r=r):
                    score = GAIN * products(x_ref[h], y_ref[r]) + spread_buf[s]
                    score = score.reshape(SRC // 8, 8, TILE)
                    old = top[t]
                    new = jnp.maximum(old, jnp.max(score, axis=0))
                    acc[t] = acc[t] * rescale(old, new) + jnp.sum(
                        jnp.exp(score - new[None]), axis=0
                    )
                    top[t] = new

            return 0

        lax.fori_loop(0, n_items, step, 0)
        high = jnp.max(top[0:TILES], axis=1)
        base = jnp.where(high == -jnp.inf, 0.0, high)
        total = jnp.sum(acc[0:TILES] * jnp.exp(top[0:TILES] - base[:, None, :]), axis=1)
        out_ref[...] = jnp.broadcast_to((high + jnp.log(total))[None], out_ref.shape)


VMEM = pl.BlockSpec(memory_space=pltpu.VMEM)
ANY = pl.BlockSpec(memory_space=pl.ANY)
SMEM = pl.BlockSpec(memory_space=pltpu.SMEM)


def limit(mebibytes):
    return pltpu.CompilerParams(vmem_limit_bytes=mebibytes * 1024 * 1024)


def shape(dims, dtype=jnp.float32):
    return jax.ShapeDtypeStruct(dims, dtype)


def prepare_sources(*operands):
    return pl.pallas_call(
        source_kernel,
        out_shape=(shape((SRC + EXTRA, FEAT), jnp.bfloat16), shape((SUBS, TILE))),
        in_specs=[ANY] * 4,
        out_specs=(VMEM,) * 2,
        scratch_shapes=[
            pltpu.VMEM((SUBS, TILE), jnp.float32),
            pltpu.VMEM((CAP, TILE), jnp.int32),
            pltpu.VMEM((1, TILE), jnp.int32),
            pltpu.SemaphoreType.DMA((4,)),
        ],
        compiler_params=limit(60),
        name="prepare_sources",
    )(*operands)


def prepare_targets(*operands):
    return pl.pallas_call(
        target_kernel,
        out_shape=(
            shape((TSUB, FEAT + EXTRA, TILE), jnp.bfloat16),
            shape((TSUB, TILE)),
        ),
        in_specs=[ANY] * 3,
        out_specs=(VMEM,) * 2,
        scratch_shapes=[
            pltpu.VMEM((TSUB * TILE, FEAT), jnp.bfloat16),
            pltpu.VMEM((TSUB, TILE), jnp.float32),
            pltpu.VMEM((TSUB, TILE), jnp.float32),
            pltpu.SemaphoreType.DMA((3,)),
        ],
        compiler_params=limit(60),
        name="prepare_targets",
    )(*operands)


ROW_SCRATCH = [
    pltpu.VMEM((TILES + 8, TILE), jnp.float32),
    pltpu.VMEM((TILES + 8, TILE), jnp.float32),
    pltpu.VMEM((N_ROWS, SRC, TILE), jnp.float32),
    pltpu.VMEM((N_ROWS, SRC, TILE), jnp.float32),
]
COL_SCRATCH = [
    pltpu.VMEM((N_ROWS, SRC, TILE), jnp.float32),
    pltpu.VMEM((TILES + 1, 8, TILE), jnp.float32),
    pltpu.VMEM((TILES + 1, 8, TILE), jnp.float32),
]
ROW_PARTS = shape((N_ROWS, N_ROWS * SUBS, TILE))


def first_pass(at, pieces):
    return pl.pallas_call(
        first_kernel,
        out_shape=(
            ROW_PARTS,
            shape((LISTED,), jnp.int32),
            shape((NORMS + N_ROWS * SUBS, TILE)),
            shape((NORMS + TILES, TILE)),
            shape((N_ROWS, SRC, FEAT), jnp.bfloat16),
            shape((TILES, FEAT, TILE), jnp.bfloat16),
        ),
        in_specs=[SMEM] + [ANY] * N_PIECES,
        out_specs=(VMEM, SMEM, VMEM, VMEM, VMEM, VMEM),
        scratch_shapes=ROW_SCRATCH
        + [
            pltpu.SemaphoreType.DMA((N_PIECES,)),
            pltpu.VMEM((TILES, TILE), jnp.float32),
            pltpu.VMEM((CAP * N_ROWS, TILE), jnp.int32),
            pltpu.VMEM((N_ROWS, TILE), jnp.int32),
            pltpu.SMEM((N_ROWS, TILE), jnp.int32),
            pltpu.VMEM((N_ROWS, EXTRA, FEAT), jnp.bfloat16),
            pltpu.VMEM((TILES, EXTRA, TILE), jnp.bfloat16),
            pltpu.SemaphoreType.DMA((N_PIECES,)),
            pltpu.SemaphoreType.DMA,
        ],
        compiler_params=limit(24),
        name="first_row_pass",
    )(at, *[pltpu.with_memory_space_constraint(piece, pltpu.HBM) for piece in pieces])


def row_pass(items, *operands):
    return pl.pallas_call(
        row_kernel,
        out_shape=ROW_PARTS,
        in_specs=[SMEM] + [VMEM] * len(operands),
        out_specs=VMEM,
        scratch_shapes=ROW_SCRATCH,
        compiler_params=limit(20),
        name="row_pass",
    )(items, *operands)


def col_pass(items, *operands):
    return pl.pallas_call(
        col_kernel,
        out_shape=shape((N_COLS, TILES, TILE)),
        in_specs=[SMEM] + [VMEM] * len(operands),
        out_specs=VMEM,
        scratch_shapes=COL_SCRATCH,
        compiler_params=limit(20),
        name="col_pass",
    )(items, *operands)


def last_col_pass(items, *operands):
    return pl.pallas_call(
        last_col_kernel,
        out_shape=(shape((1, TILES, TILE)), shape((SUBS, TILE))),
        in_specs=[SMEM] + [VMEM] * len(operands),
        out_specs=(VMEM, VMEM),
        scratch_shapes=[pltpu.VMEM((N_ROWS * SUBS, TILE), jnp.float32)] + COL_SCRATCH,
        compiler_params=limit(20),
        name="last_col_pass",
    )(items, *operands)


def swap(blocks, axes):
    return lax.all_to_all(blocks, axes, split_axis=0, concat_axis=0, tiled=True)


def exchange(block, partner):
    pairs = []
    for place in range(N_ROWS * N_COLS):
        at = tuple(int(k) for k in np.unravel_index(place, DIMS))
        pairs.append((place, int(np.ravel_multi_index(partner(*at), DIMS))))
    return lax.ppermute(block, NAMES, pairs)


def doubled(block, partner):
    return jnp.concatenate([block, exchange(block, partner)])


def after(value, events):
    return lax.optimization_barrier((value, events))[0]


def gather_all(sources, targets):
    along = [source_partner(0, flip) for flip in (1, 3)]
    across = [source_partner(1, flip) for flip in (1, 3)]
    beside = [target_partner(order) for order in (0, 1)]

    pair = jnp.stack([sources, exchange(sources, along[0])])
    tiles = jnp.concatenate([targets, exchange(after(targets, pair), beside[0])])
    other = exchange(pair, along[1])
    first, second = exchange(pair, across[0]), exchange(pair, across[1])
    further = exchange(after(tiles, first), beside[1])
    relayed = exchange(first, across[1])
    pieces = [pair, first, second, relayed]
    near = exchange(after(tiles, (first, second)), sibling)
    first, second = exchange(other, across[0]), exchange(other, across[1])
    pieces += [other, first, second, exchange(second, across[0])]
    far = exchange(after(further, (relayed, first, pieces[-1])), sibling)
    return pieces + [tiles, further, near, far]


def source_partner(stage, flip):
    def partner(x, y, z, core):
        return (x, y ^ flip, z, core) if stage == core else (x, y, z ^ flip, core)

    return partner


def target_partner(order):
    return lambda x, y, z, core: (x ^ (1, 3)[order ^ core], y, z, core)


def sibling(x, y, z, core):
    return (x, y, z, core ^ 1)


def body(
    source_points, target_points, source_mass, target_mass, target_init, pair_tiles, pair_count
):
    x_block, source_norm = prepare_sources(
        source_points, source_mass.reshape(SUBS, TILE), pair_tiles.T, pair_count.reshape(1, -1)
    )
    y_block, target_part = prepare_targets(
        target_points, target_mass.reshape(TSUB, TILE), target_init.reshape(TSUB, TILE)
    )
    pieces = gather_all(x_block, y_block)

    at = jnp.stack([lax.axis_index(name) for name in NAMES]).astype(jnp.int32)
    row_parts, items, cols, rows, xs, ys = first_pass(at, pieces)
    for iteration in range(ITERS - 1):
        col_parts = col_pass(items, xs, ys, cols, swap(row_parts, ROWS))
        row_parts = row_pass(items, xs, ys, rows, swap(col_parts, COLS))
    col_parts, source_pot = last_col_pass(
        items, xs, ys, cols, swap(row_parts, ROWS), source_norm
    )
    last = swap(col_parts.reshape(N_COLS, TSUB, TILE), COLS)
    target_pot = target_part - EPSILON * lse_over_first(last)
    return (source_pot.reshape(-1), target_pot.reshape(-1))


def solution(mesh):
    grid = Mesh(mesh.devices.reshape(DIMS), NAMES)
    placed = (
        P(NAMES, None),
        P(NAMES, None),
        P(NAMES),
        P(NAMES),
        P(NAMES),
        P(NAMES, None),
        P(NAMES),
    )
    return jax.shard_map(
        body, mesh=grid, in_specs=placed, out_specs=(P(NAMES), P(NAMES)), check_vma=False
    )
```

```python
import functools
import math

import jax
import jax.numpy as jnp
import numpy as np
from jax import lax
from jax.experimental import pallas as pl
from jax.experimental.pallas import tpu as pltpu
from jax.sharding import Mesh
from jax.sharding import PartitionSpec as P

TSUB = 8
CAP = 2
ITERS = 2
EPSILON = 0.1

DIMS = (4, 4, 4, 2)
NAMES = ("x", "y", "z", "core")
ROWS = ("y", "z")
COLS = ("x", "core")
N_ROWS = 16
N_PIECES = 12
N_COLS = 8
RING = 4
SRC = 384
TILE = 128
SUBS = SRC // TILE
FEAT = 256
TILES = N_COLS * TSUB
SLOTS = N_ROWS * N_COLS * CAP
UNROLL = 16
LAST_UNROLL = 4
EXTRA = 16
LISTED = 8 + SLOTS + 4 * LAST_UNROLL
NOTHING = TILES << 8
NORMS = 16
GAIN = 2.0 / (FEAT * EPSILON)
UNIT = 1.0 / (FEAT * EPSILON)
LOG2E = math.log2(math.e)
SPAN = 70.0


def lse_over_first(parts):
    top = jnp.max(parts, axis=0)
    base = jnp.where(top == -jnp.inf, 0.0, top)
    return top + jnp.log(jnp.sum(jnp.exp(parts - base[None]), axis=0))


def spread(values, norm_ref):
    high, low = jnp.max(values), jnp.min(values)
    reach = GAIN * jnp.sqrt(jnp.max(norm_ref[0:8]) * jnp.max(norm_ref[8:16]))
    return 0.5 * high + 0.5 * low, 0.5 * high - 0.5 * low + reach <= SPAN


def diagonal():
    return lax.broadcasted_iota(jnp.int32, (TILE, TILE), 0) == lax.broadcasted_iota(
        jnp.int32, (TILE, TILE), 1
    )


def as_row(eye, col):
    return jnp.sum(jnp.where(eye, col, 0.0), axis=0, keepdims=True)


def as_col(eye, row):
    return jnp.sum(jnp.where(eye, row, 0.0), axis=1, keepdims=True)


def products(x, y):
    return jnp.dot(x, y, preferred_element_type=jnp.float32)


def item_at(item_ref, w):
    one, two = item_ref[8 + 2 * w], item_ref[9 + 2 * w]
    return (
        one >> 20,
        (one >> 16) & 15,
        (one >> 8) & 255,
        (two >> 8) & 255,
        one & 255,
        two & 255,
    )


def exps(x, y):
    return jnp.exp2((GAIN * LOG2E) * products(x, y))


def two_tiles(y_ref, r0, r1):
    return jnp.concatenate([y_ref[r0], y_ref[r1]], axis=1)


def sweep(n_items, work):
    def steps(first, size):
        def step(w, _):
            for k in range(size):
                work(first + size * w + k)
            return 0

        return step

    whole = lax.div(n_items, UNROLL)
    lax.fori_loop(0, whole, steps(0, UNROLL), 0)
    left = n_items - UNROLL * whole
    lax.fori_loop(
        0, lax.div(left + LAST_UNROLL - 1, LAST_UNROLL), steps(UNROLL * whole, LAST_UNROLL), 0
    )


def rescale(old, new):
    return jnp.where(old == new, 1.0, jnp.exp(old - new))


def split(values):
    high = values.astype(jnp.bfloat16).astype(jnp.float32)
    rest = values - high
    middle = rest.astype(jnp.bfloat16).astype(jnp.float32)
    return [high, middle, (rest - middle).astype(jnp.bfloat16).astype(jnp.float32)]


def start_all(pairs, sems):
    copies = [pltpu.make_async_copy(src, dst, sems.at[k]) for k, (src, dst) in enumerate(pairs)]
    for copy in copies:
        copy.start()
    return copies


def prepare_kernel(*refs):
    xo_ref, yo_ref, nx_ref, part_ref = refs[7:11]
    y_ref, mass_ref, goal_ref, init_ref, tile_ref, count_ref, sems = refs[11:]
    copies = start_all(
        zip(refs[:7], (xo_ref.at[0:SRC], y_ref, mass_ref, goal_ref, init_ref, tile_ref, count_ref)),
        sems,
    )
    eye = diagonal()
    for copy in copies[2:]:
        copy.wait()
    la = jnp.log(mass_ref[...])
    lb = jnp.log(goal_ref[...])

    copies[0].wait()
    norms = []
    for b in range(SUBS):
        x = xo_ref[b * TILE : (b + 1) * TILE, :].astype(jnp.float32)
        norms.append(as_row(eye, jnp.sum(x * x, axis=1, keepdims=True)))
    nx = jnp.concatenate(norms, axis=0)
    nx_ref[...] = nx
    bound = jnp.full((1, TILE), 1.01 * jnp.max(nx))
    left = split(la) + [bound, jnp.zeros((EXTRA - 10, TILE), jnp.float32)]
    right = [
        tile_ref[...].astype(jnp.float32),
        count_ref[...].astype(jnp.float32),
        jnp.zeros((EXTRA - 3, TILE), jnp.float32),
    ]
    extra = jnp.concatenate(
        [jnp.concatenate(left, axis=0), jnp.concatenate(right, axis=0)], axis=1
    )
    xo_ref[SRC:] = extra.astype(jnp.bfloat16)

    copies[1].wait()
    norms = []
    for t in range(TSUB):
        y = y_ref[t * TILE : (t + 1) * TILE, :].astype(jnp.float32).T
        norms.append(jnp.sum(y * y, axis=0, keepdims=True))
        yo_ref[t, 0:FEAT] = y.astype(jnp.bfloat16)
    ny = jnp.concatenate(norms, axis=0)
    part_ref[...] = EPSILON * (lb + UNIT * ny)
    a0 = init_ref[...] / EPSILON - ny * UNIT
    parts = split(a0) + split(lb)
    bound = jnp.full((1, TILE), 1.01 * jnp.max(ny))
    for t in range(TSUB):
        rows = [part[t : t + 1] for part in parts]
        rows += [bound, jnp.zeros((EXTRA - 7, TILE), jnp.float32)]
        yo_ref[t, FEAT:] = jnp.concatenate(rows, axis=0).astype(jnp.bfloat16)


def gray(k):
    return k ^ (k >> 1)


def ring_place(offset, first):
    place = gray(offset)
    other = ((place & 1) << 1) | (place >> 1)
    return jnp.where(first == 0, place, other)


def piece_copies(x_refs, y_refs, xs, ys, x_rows, y_rows):
    pairs = []
    for half in range(2):
        for later in range(RING):
            place = pl.ds(RING * later + 2 * half, 2)
            pairs.append((x_refs[RING * half + later].at[:, x_rows, :], xs.at[place]))
    start = 0
    for piece in y_refs:
        pairs.append((piece.at[:, y_rows, :], ys.at[pl.ds(start, piece.shape[0])]))
        start += piece.shape[0]
    return pairs


def first_kernel(*refs):
    at_ref, pieces = refs[0], refs[1 : 1 + N_PIECES]
    x_refs, y_refs = pieces[: 2 * RING], pieces[2 * RING :]
    out_ref, item_ref, cols_ref, rows_ref, xs, ys = refs[1 + N_PIECES : 7 + N_PIECES]
    a_buf, u_buf, acc, top, sems = refs[7 + N_PIECES : 12 + N_PIECES]
    a_ref, table, compact, numbers, x_extra, y_extra, small_sems, sem = refs[12 + N_PIECES :]
    la_ref, lb_ref = cols_ref.at[NORMS:], rows_ref.at[NORMS:]
    x, y, z, core = (at_ref[k] for k in range(4))

    small = start_all(
        piece_copies(
            x_refs, y_refs, x_extra, y_extra, slice(SRC, SRC + EXTRA), slice(FEAT, FEAT + EXTRA)
        ),
        small_sems,
    )
    large = start_all(
        piece_copies(x_refs, y_refs, xs, ys, slice(0, SRC), slice(0, FEAT)), sems
    )
    for copy in small:
        copy.wait()

    lane = lax.broadcasted_iota(jnp.int32, (CAP, TILE), 1)
    px, side = lane >> 5, lane & 1
    start = RING * (side ^ core) + ring_place(px ^ x, side)
    entry_base = ((TSUB * (2 * px + side)) << 8) + TSUB * start

    bound = None
    for later in range(RING):
        for sooner in range(RING):
            one, two = gray(sooner), gray(later)
            off_y = jnp.where(core == 0, one, two)
            off_z = jnp.where(core == 0, two, one)
            s = RING * (y ^ off_y) + (z ^ off_z)
            extra = x_extra[RING * later + sooner].astype(jnp.float32)
            la = extra[0:3, :TILE] + extra[3:6, :TILE] + extra[6:9, :TILE]
            for b in range(SUBS):
                la_ref[pl.ds(SUBS * s + b, 1), :] = la[b : b + 1]
            here = extra[9:10, :TILE]
            bound = here if bound is None else jnp.maximum(bound, here)
            numbers_here = extra[0:3, TILE:].astype(jnp.int32)
            head = (s << 20) | ((RING * later + sooner) << 16)
            entry = head | (entry_base + 257 * numbers_here[0:CAP])
            slot = lax.broadcasted_iota(jnp.int32, (CAP, TILE), 0)
            entry = jnp.where(slot < numbers_here[CAP : CAP + 1], entry, -1)
            for e in range(CAP):
                table[pl.ds(N_ROWS * e + s, 1), :] = entry[e : e + 1]
    for ref in (cols_ref, rows_ref):
        ref[0:8] = jnp.broadcast_to(bound, (8, TILE))

    lane = lax.broadcasted_iota(jnp.int32, (N_ROWS, TILE), 1) & (2 * N_ROWS - 1)
    moved = pltpu.roll(table[...], (TILE - 2 * (RING * y + z)) & (TILE - 1), axis=1)
    second = pltpu.roll(moved[N_ROWS:], 2, axis=1)
    compact[...] = jnp.where(lane < 2, moved[:N_ROWS], second)
    copy = pltpu.make_async_copy(compact, numbers, sem)
    copy.start()
    acc[...] = jnp.zeros_like(acc)

    bound = None
    for k in range(2 * RING):
        side = core ^ (k // RING)
        place = k % RING
        offset = jnp.where(side == 0, gray(place), (0, 3, 1, 2)[place])
        owner = 2 * (x ^ offset) + side
        extra = y_extra[TSUB * k : TSUB * (k + 1)].astype(jnp.float32)
        rows = pl.ds(pl.multiple_of(TSUB * owner, TSUB), TSUB)
        a_ref[rows, :] = extra[:, 0] + extra[:, 1] + extra[:, 2]
        lb_ref[rows, :] = extra[:, 3] + extra[:, 4] + extra[:, 5]
        here = extra[0, 6:7]
        bound = here if bound is None else jnp.maximum(bound, here)
    for ref in (cols_ref, rows_ref):
        ref[8:16] = jnp.broadcast_to(bound, (8, TILE))

    copy.wait()

    def block(s, place):
        for px in range(RING):
            for side in range(2):
                for e in range(CAP):
                    entry = numbers[s, 2 * N_ROWS * px + 2 * e + side]
                    item_ref[place] = entry
                    place = place + jnp.where(entry >= 0, 1, 0)
        item_ref[place] = jnp.int32(NOTHING)
        return place + (place & 1)

    end = lax.fori_loop(0, N_ROWS, block, jnp.int32(8))
    for k in range(2 * LAST_UNROLL):
        item_ref[end + k] = jnp.int32(NOTHING)
    item_ref[0] = (end - 8) >> 1
    item_ref[1] = RING * y + z
    for copy in large:
        copy.wait()
    row_core(a_ref[...], item_ref, xs, ys, cols_ref, out_ref, a_buf, u_buf, acc, top)


def row_kernel(item_ref, x_ref, y_ref, side_ref, parts_ref, out_ref, a_buf, u_buf, acc, top):
    acc[...] = jnp.zeros_like(acc)
    a = side_ref[NORMS:] - lse_over_first(parts_ref[...])
    row_core(a, item_ref, x_ref, y_ref, side_ref, out_ref, a_buf, u_buf, acc, top)


def row_core(a, item_ref, x_ref, y_ref, norm_ref, out_ref, a_buf, u_buf, acc, top):
    mid, fast = spread(a, norm_ref)
    n_items = item_ref[0]
    eye = diagonal()

    @pl.when(fast)
    def _():
        u_buf[0:TILES] = jnp.exp(a - mid)
        u_buf[TILES:] = jnp.zeros((8, TILE), jnp.float32)

        def work(w):
            s, h, t0, t1, r0, r1 = item_at(item_ref, w)
            u0, u1 = u_buf[pl.ds(t0, 1), :], u_buf[pl.ds(t1, 1), :]
            e = exps(x_ref[h], two_tiles(y_ref, r0, r1))
            acc[s] += e[:, :TILE] * u0 + e[:, TILE:] * u1

        sweep(n_items, work)
        for k in range(N_ROWS * SUBS):
            s, b = k // SUBS, k % SUBS
            col = jnp.sum(acc[s, b * TILE : (b + 1) * TILE, :], axis=1, keepdims=True)
            a_buf[k : k + 1, :] = as_row(eye, col)
        done = mid + jnp.log(a_buf[0 : N_ROWS * SUBS])
        out_ref[...] = jnp.broadcast_to(done[None], out_ref.shape)

    @pl.when(jnp.logical_not(fast))
    def _():
        a_buf[0:TILES] = a
        a_buf[TILES:] = jnp.zeros((8, TILE), jnp.float32)
        top[...] = jnp.full_like(top, -jnp.inf)

        def step(w, _):
            s, h, t0, t1, r0, r1 = item_at(item_ref, w)
            for t, r in ((t0, r0), (t1, r1)):

                @pl.when(t < TILES)
                def _(t=t, r=r):
                    score = GAIN * products(x_ref[h], y_ref[r]) + a_buf[pl.ds(t, 1), :]
                    old = top[s]
                    new = jnp.maximum(old, score)
                    acc[s] = acc[s] * rescale(old, new) + jnp.exp(score - new)
                    top[s] = new

            return 0

        lax.fori_loop(0, n_items, step, 0)

        def finish(k, _):
            s, b = lax.div(k, SUBS), lax.rem(k, SUBS)
            rows = pl.ds(pl.multiple_of(b * TILE, TILE), TILE)
            block = top[s, rows, :]
            high = jnp.max(block, axis=1, keepdims=True)
            base = jnp.where(high == -jnp.inf, 0.0, high)
            total = jnp.sum(acc[s, rows, :] * jnp.exp(block - base), axis=1, keepdims=True)
            high_row = jnp.max(jnp.where(eye, high, -jnp.inf), axis=0, keepdims=True)
            done = high_row + jnp.log(as_row(eye, total))
            out_ref[:, pl.ds(k, 1), :] = jnp.broadcast_to(done[None], (N_ROWS, 1, TILE))
            return 0

        lax.fori_loop(0, N_ROWS * SUBS, finish, 0)


def last_col_kernel(
    item_ref, x_ref, y_ref, side_ref, parts_ref, norm_ref, out_ref, f_ref, b_buf, *scratch
):
    b = side_ref[NORMS:] - lse_over_first(parts_ref[...])
    b_buf[...] = b
    for k in range(SUBS):
        here = b_buf[pl.ds(SUBS * item_ref[1] + k, 1), :]
        f_ref[k : k + 1, :] = EPSILON * (here + UNIT * norm_ref[k : k + 1, :])
    col_core(b, item_ref, x_ref, y_ref, side_ref, out_ref, *scratch)


def col_kernel(item_ref, x_ref, y_ref, side_ref, parts_ref, out_ref, *scratch):
    b = side_ref[NORMS:] - lse_over_first(parts_ref[...])
    col_core(b, item_ref, x_ref, y_ref, side_ref, out_ref, *scratch)


def col_core(b, item_ref, x_ref, y_ref, norm_ref, out_ref, spread_buf, acc, top):
    mid, fast = spread(b, norm_ref)
    n_items = item_ref[0]
    eye = diagonal()

    def lay_out(values):
        for k in range(N_ROWS * SUBS):
            s, part = k // SUBS, k % SUBS
            col = as_col(eye, values[k : k + 1, :])
            spread_buf[s, part * TILE : (part + 1) * TILE, :] = jnp.broadcast_to(col, (TILE, TILE))

    acc[...] = jnp.zeros_like(acc)

    @pl.when(fast)
    def _():
        lay_out(jnp.exp(b - mid))

        def work(w):
            s, h, t0, t1, r0, r1 = item_at(item_ref, w)
            e = exps(x_ref[h], two_tiles(y_ref, r0, r1))
            v = spread_buf[s]
            acc[t0] += jnp.sum((e[:, :TILE] * v).reshape(SRC // 8, 8, TILE), axis=0)
            acc[t1] += jnp.sum((e[:, TILE:] * v).reshape(SRC // 8, 8, TILE), axis=0)

        sweep(n_items, work)
        done = mid + jnp.log(jnp.sum(acc[0:TILES], axis=1))
        out_ref[...] = jnp.broadcast_to(done[None], out_ref.shape)

    @pl.when(jnp.logical_not(fast))
    def _():
        lay_out(b)
        top[...] = jnp.full_like(top, -jnp.inf)

        def step(w, _):
            s, h, t0, t1, r0, r1 = item_at(item_ref, w)
            for t, r in ((t0, r0), (t1, r1)):

                @pl.when(t < TILES)
                def _(t=t, r=r):
                    score = GAIN * products(x_ref[h], y_ref[r]) + spread_buf[s]
                    score = score.reshape(SRC // 8, 8, TILE)
                    old = top[t]
                    new = jnp.maximum(old, jnp.max(score, axis=0))
                    acc[t] = acc[t] * rescale(old, new) + jnp.sum(
                        jnp.exp(score - new[None]), axis=0
                    )
                    top[t] = new

            return 0

        lax.fori_loop(0, n_items, step, 0)
        high = jnp.max(top[0:TILES], axis=1)
        base = jnp.where(high == -jnp.inf, 0.0, high)
        total = jnp.sum(acc[0:TILES] * jnp.exp(top[0:TILES] - base[:, None, :]), axis=1)
        out_ref[...] = jnp.broadcast_to((high + jnp.log(total))[None], out_ref.shape)


VMEM = pl.BlockSpec(memory_space=pltpu.VMEM)
ANY = pl.BlockSpec(memory_space=pl.ANY)
SMEM = pl.BlockSpec(memory_space=pltpu.SMEM)


def limit(mebibytes):
    return pltpu.CompilerParams(vmem_limit_bytes=mebibytes * 1024 * 1024)


def shape(dims, dtype=jnp.float32):
    return jax.ShapeDtypeStruct(dims, dtype)


def prepare(*operands):
    return pl.pallas_call(
        prepare_kernel,
        out_shape=(
            shape((SRC + EXTRA, FEAT), jnp.bfloat16),
            shape((TSUB, FEAT + EXTRA, TILE), jnp.bfloat16),
            shape((SUBS, TILE)),
            shape((TSUB, TILE)),
        ),
        in_specs=[ANY] * 7,
        out_specs=(VMEM,) * 4,
        scratch_shapes=[
            pltpu.VMEM((TSUB * TILE, FEAT), jnp.bfloat16),
            pltpu.VMEM((SUBS, TILE), jnp.float32),
            pltpu.VMEM((TSUB, TILE), jnp.float32),
            pltpu.VMEM((TSUB, TILE), jnp.float32),
            pltpu.VMEM((CAP, TILE), jnp.int32),
            pltpu.VMEM((1, TILE), jnp.int32),
            pltpu.SemaphoreType.DMA((7,)),
        ],
        compiler_params=limit(60),
        name="prepare",
    )(*operands)


ROW_SCRATCH = [
    pltpu.VMEM((TILES + 8, TILE), jnp.float32),
    pltpu.VMEM((TILES + 8, TILE), jnp.float32),
    pltpu.VMEM((N_ROWS, SRC, TILE), jnp.float32),
    pltpu.VMEM((N_ROWS, SRC, TILE), jnp.float32),
]
COL_SCRATCH = [
    pltpu.VMEM((N_ROWS, SRC, TILE), jnp.float32),
    pltpu.VMEM((TILES + 1, 8, TILE), jnp.float32),
    pltpu.VMEM((TILES + 1, 8, TILE), jnp.float32),
]
ROW_PARTS = shape((N_ROWS, N_ROWS * SUBS, TILE))


def first_pass(at, pieces):
    return pl.pallas_call(
        first_kernel,
        out_shape=(
            ROW_PARTS,
            shape((LISTED,), jnp.int32),
            shape((NORMS + N_ROWS * SUBS, TILE)),
            shape((NORMS + TILES, TILE)),
            shape((N_ROWS, SRC, FEAT), jnp.bfloat16),
            shape((TILES, FEAT, TILE), jnp.bfloat16),
        ),
        in_specs=[SMEM] + [ANY] * N_PIECES,
        out_specs=(VMEM, SMEM, VMEM, VMEM, VMEM, VMEM),
        scratch_shapes=ROW_SCRATCH
        + [
            pltpu.SemaphoreType.DMA((N_PIECES,)),
            pltpu.VMEM((TILES, TILE), jnp.float32),
            pltpu.VMEM((CAP * N_ROWS, TILE), jnp.int32),
            pltpu.VMEM((N_ROWS, TILE), jnp.int32),
            pltpu.SMEM((N_ROWS, TILE), jnp.int32),
            pltpu.VMEM((N_ROWS, EXTRA, FEAT), jnp.bfloat16),
            pltpu.VMEM((TILES, EXTRA, TILE), jnp.bfloat16),
            pltpu.SemaphoreType.DMA((N_PIECES,)),
            pltpu.SemaphoreType.DMA,
        ],
        compiler_params=limit(24),
        name="first_row_pass",
    )(at, *[pltpu.with_memory_space_constraint(piece, pltpu.HBM) for piece in pieces])


def row_pass(items, *operands):
    return pl.pallas_call(
        row_kernel,
        out_shape=ROW_PARTS,
        in_specs=[SMEM] + [VMEM] * len(operands),
        out_specs=VMEM,
        scratch_shapes=ROW_SCRATCH,
        compiler_params=limit(20),
        name="row_pass",
    )(items, *operands)


def col_pass(items, *operands):
    return pl.pallas_call(
        col_kernel,
        out_shape=shape((N_COLS, TILES, TILE)),
        in_specs=[SMEM] + [VMEM] * len(operands),
        out_specs=VMEM,
        scratch_shapes=COL_SCRATCH,
        compiler_params=limit(20),
        name="col_pass",
    )(items, *operands)


def last_col_pass(items, *operands):
    return pl.pallas_call(
        last_col_kernel,
        out_shape=(shape((1, TILES, TILE)), shape((SUBS, TILE))),
        in_specs=[SMEM] + [VMEM] * len(operands),
        out_specs=(VMEM, VMEM),
        scratch_shapes=[pltpu.VMEM((N_ROWS * SUBS, TILE), jnp.float32)] + COL_SCRATCH,
        compiler_params=limit(20),
        name="last_col_pass",
    )(items, *operands)


def swap(blocks, axes):
    return lax.all_to_all(blocks, axes, split_axis=0, concat_axis=0, tiled=True)


def exchange(block, partner):
    pairs = []
    for place in range(N_ROWS * N_COLS):
        at = tuple(int(k) for k in np.unravel_index(place, DIMS))
        pairs.append((place, int(np.ravel_multi_index(partner(*at), DIMS))))
    return lax.ppermute(block, NAMES, pairs)


def doubled(block, partner):
    return jnp.concatenate([block, exchange(block, partner)])


def after(value, events):
    return lax.optimization_barrier((value, events))[0]


def gather_all(sources, targets):
    along = [source_partner(0, flip) for flip in (1, 3)]
    across = [source_partner(1, flip) for flip in (1, 3)]
    beside = [target_partner(order) for order in (0, 1)]

    pair = jnp.stack([sources, exchange(sources, along[0])])
    tiles = jnp.concatenate([targets, exchange(targets, beside[0])])
    other = exchange(pair, along[1])
    first, second = exchange(pair, across[0]), exchange(pair, across[1])
    further = exchange(after(tiles, pair), beside[1])
    relayed = exchange(first, across[1])
    pieces = [pair, first, second, relayed]
    near = exchange(after(tiles, first), sibling)
    first, second = exchange(other, across[0]), exchange(other, across[1])
    pieces += [other, first, second, exchange(second, across[0])]
    far = exchange(after(further, (relayed, first, pieces[-1])), sibling)
    return pieces + [tiles, further, near, far]


def source_partner(stage, flip):
    def partner(x, y, z, core):
        return (x, y ^ flip, z, core) if stage == core else (x, y, z ^ flip, core)

    return partner


def target_partner(order):
    return lambda x, y, z, core: (x ^ (1, 3)[order ^ core], y, z, core)


def sibling(x, y, z, core):
    return (x, y, z, core ^ 1)


def body(
    source_points, target_points, source_mass, target_mass, target_init, pair_tiles, pair_count
):
    x_block, y_block, source_norm, target_part = prepare(
        source_points,
        target_points,
        source_mass.reshape(SUBS, TILE),
        target_mass.reshape(TSUB, TILE),
        target_init.reshape(TSUB, TILE),
        pair_tiles.T,
        pair_count.reshape(1, -1),
    )
    pieces = gather_all(x_block, y_block)

    at = jnp.stack([lax.axis_index(name) for name in NAMES]).astype(jnp.int32)
    row_parts, items, cols, rows, xs, ys = first_pass(at, pieces)
    for iteration in range(ITERS - 1):
        col_parts = col_pass(items, xs, ys, cols, swap(row_parts, ROWS))
        row_parts = row_pass(items, xs, ys, rows, swap(col_parts, COLS))
    col_parts, source_pot = last_col_pass(
        items, xs, ys, cols, swap(row_parts, ROWS), source_norm
    )
    last = swap(col_parts.reshape(N_COLS, TSUB, TILE), COLS)
    target_pot = target_part - EPSILON * lse_over_first(last)
    return (source_pot.reshape(-1), target_pot.reshape(-1))


def solution(mesh):
    grid = Mesh(mesh.devices.reshape(DIMS), NAMES)
    placed = (
        P(NAMES, None),
        P(NAMES, None),
        P(NAMES),
        P(NAMES),
        P(NAMES),
        P(NAMES, None),
        P(NAMES),
    )
    return jax.shard_map(
        body, mesh=grid, in_specs=placed, out_specs=(P(NAMES), P(NAMES)), check_vma=False
    )
```

```python
import functools
import math

import jax
import jax.numpy as jnp
import numpy as np
from jax import lax
from jax.experimental import pallas as pl
from jax.experimental.pallas import tpu as pltpu
from jax.sharding import Mesh
from jax.sharding import PartitionSpec as P

TSUB = 8
CAP = 2
ITERS = 2
EPSILON = 0.1

DIMS = (4, 4, 4, 2)
NAMES = ("x", "y", "z", "core")
ROWS = ("y", "z")
COLS = ("x", "core")
N_ROWS = 16
N_PIECES = 12
N_COLS = 8
RING = 4
SRC = 384
TILE = 128
SUBS = SRC // TILE
FEAT = 256
TILES = N_COLS * TSUB
SLOTS = N_ROWS * N_COLS * CAP
UNROLL = 16
LAST_UNROLL = 4
EXTRA = 16
LISTED = 8 + SLOTS + 4 * LAST_UNROLL
NOTHING = TILES << 8
NORMS = 16
GAIN = 2.0 / (FEAT * EPSILON)
UNIT = 1.0 / (FEAT * EPSILON)
LOG2E = math.log2(math.e)
SPAN = 70.0


def lse_over_first(parts):
    top = jnp.max(parts, axis=0)
    base = jnp.where(top == -jnp.inf, 0.0, top)
    return top + jnp.log(jnp.sum(jnp.exp(parts - base[None]), axis=0))


def spread(values, norm_ref):
    high, low = jnp.max(values), jnp.min(values)
    reach = GAIN * jnp.sqrt(jnp.max(norm_ref[0:8]) * jnp.max(norm_ref[8:16]))
    return 0.5 * high + 0.5 * low, 0.5 * high - 0.5 * low + reach <= SPAN


def diagonal():
    return lax.broadcasted_iota(jnp.int32, (TILE, TILE), 0) == lax.broadcasted_iota(
        jnp.int32, (TILE, TILE), 1
    )


def as_row(eye, col):
    return jnp.sum(jnp.where(eye, col, 0.0), axis=0, keepdims=True)


def as_col(eye, row):
    return jnp.sum(jnp.where(eye, row, 0.0), axis=1, keepdims=True)


def products(x, y):
    return jnp.dot(x, y, preferred_element_type=jnp.float32)


def item_at(item_ref, w):
    one, two = item_ref[8 + 2 * w], item_ref[9 + 2 * w]
    return (
        one >> 20,
        (one >> 16) & 15,
        (one >> 8) & 255,
        (two >> 8) & 255,
        one & 255,
        two & 255,
    )


def exps(x, y):
    return jnp.exp2((GAIN * LOG2E) * products(x, y))


def two_tiles(y_ref, r0, r1):
    return jnp.concatenate([y_ref[r0], y_ref[r1]], axis=1)


def sweep(n_items, work):
    def steps(first, size):
        def step(w, _):
            for k in range(size):
                work(first + size * w + k)
            return 0

        return step

    done = 0
    for size in (UNROLL, UNROLL // 2):
        whole = lax.div(n_items - done, size)
        lax.fori_loop(0, whole, steps(done, size), 0)
        done = done + size * whole
    left = lax.div(n_items - done + LAST_UNROLL - 1, LAST_UNROLL)
    lax.fori_loop(0, left, steps(done, LAST_UNROLL), 0)


def rescale(old, new):
    return jnp.where(old == new, 1.0, jnp.exp(old - new))


def split(values):
    high = values.astype(jnp.bfloat16).astype(jnp.float32)
    rest = values - high
    middle = rest.astype(jnp.bfloat16).astype(jnp.float32)
    return [high, middle, (rest - middle).astype(jnp.bfloat16).astype(jnp.float32)]


def start_all(pairs, sems):
    copies = [pltpu.make_async_copy(src, dst, sems.at[k]) for k, (src, dst) in enumerate(pairs)]
    for copy in copies:
        copy.start()
    return copies


def prepare_kernel(*refs):
    xo_ref, yo_ref, nx_ref, part_ref = refs[7:11]
    y_ref, mass_ref, goal_ref, init_ref, tile_ref, count_ref, sems = refs[11:]
    copies = start_all(
        zip(refs[:7], (xo_ref.at[0:SRC], y_ref, mass_ref, goal_ref, init_ref, tile_ref, count_ref)),
        sems,
    )
    eye = diagonal()
    for copy in copies[2:]:
        copy.wait()
    la = jnp.log(mass_ref[...])
    lb = jnp.log(goal_ref[...])

    copies[0].wait()
    norms = []
    for b in range(SUBS):
        x = xo_ref[b * TILE : (b + 1) * TILE, :].astype(jnp.float32)
        norms.append(as_row(eye, jnp.sum(x * x, axis=1, keepdims=True)))
    nx = jnp.concatenate(norms, axis=0)
    nx_ref[...] = nx
    bound = jnp.full((1, TILE), 1.01 * jnp.max(nx))
    left = split(la) + [bound, jnp.zeros((EXTRA - 10, TILE), jnp.float32)]
    right = [
        tile_ref[...].astype(jnp.float32),
        count_ref[...].astype(jnp.float32),
        jnp.zeros((EXTRA - 3, TILE), jnp.float32),
    ]
    extra = jnp.concatenate(
        [jnp.concatenate(left, axis=0), jnp.concatenate(right, axis=0)], axis=1
    )
    xo_ref[SRC:] = extra.astype(jnp.bfloat16)

    copies[1].wait()
    norms = []
    for t in range(TSUB):
        y = y_ref[t * TILE : (t + 1) * TILE, :].astype(jnp.float32).T
        norms.append(jnp.sum(y * y, axis=0, keepdims=True))
        yo_ref[t, 0:FEAT] = y.astype(jnp.bfloat16)
    ny = jnp.concatenate(norms, axis=0)
    part_ref[...] = EPSILON * (lb + UNIT * ny)
    a0 = init_ref[...] / EPSILON - ny * UNIT
    parts = split(a0) + split(lb)
    bound = jnp.full((1, TILE), 1.01 * jnp.max(ny))
    for t in range(TSUB):
        rows = [part[t : t + 1] for part in parts]
        rows += [bound, jnp.zeros((EXTRA - 7, TILE), jnp.float32)]
        yo_ref[t, FEAT:] = jnp.concatenate(rows, axis=0).astype(jnp.bfloat16)


def gray(k):
    return k ^ (k >> 1)


def ring_place(offset, first):
    place = gray(offset)
    other = ((place & 1) << 1) | (place >> 1)
    return jnp.where(first == 0, place, other)


def piece_copies(x_refs, y_refs, xs, ys, x_rows, y_rows):
    pairs = []
    for half in range(2):
        for later in range(RING):
            place = pl.ds(RING * later + 2 * half, 2)
            pairs.append((x_refs[RING * half + later].at[:, x_rows, :], xs.at[place]))
    start = 0
    for piece in y_refs:
        pairs.append((piece.at[:, y_rows, :], ys.at[pl.ds(start, piece.shape[0])]))
        start += piece.shape[0]
    return pairs


def first_kernel(*refs):
    at_ref, pieces = refs[0], refs[1 : 1 + N_PIECES]
    x_refs, y_refs = pieces[: 2 * RING], pieces[2 * RING :]
    out_ref, item_ref, cols_ref, rows_ref, xs, ys = refs[1 + N_PIECES : 7 + N_PIECES]
    a_buf, u_buf, acc, top, sems = refs[7 + N_PIECES : 12 + N_PIECES]
    a_ref, table, compact, numbers, x_extra, y_extra, small_sems, sem = refs[12 + N_PIECES :]
    la_ref, lb_ref = cols_ref.at[NORMS:], rows_ref.at[NORMS:]
    x, y, z, core = (at_ref[k] for k in range(4))

    small = start_all(
        piece_copies(
            x_refs, y_refs, x_extra, y_extra, slice(SRC, SRC + EXTRA), slice(FEAT, FEAT + EXTRA)
        ),
        small_sems,
    )
    large = start_all(
        piece_copies(x_refs, y_refs, xs, ys, slice(0, SRC), slice(0, FEAT)), sems
    )
    for copy in small:
        copy.wait()

    lane = lax.broadcasted_iota(jnp.int32, (CAP, TILE), 1)
    px, side = lane >> 5, lane & 1
    start = RING * (side ^ core) + ring_place(px ^ x, side)
    entry_base = ((TSUB * (2 * px + side)) << 8) + TSUB * start

    bound = None
    for later in range(RING):
        for sooner in range(RING):
            one, two = gray(sooner), gray(later)
            off_y = jnp.where(core == 0, one, two)
            off_z = jnp.where(core == 0, two, one)
            s = RING * (y ^ off_y) + (z ^ off_z)
            extra = x_extra[RING * later + sooner].astype(jnp.float32)
            la = extra[0:3, :TILE] + extra[3:6, :TILE] + extra[6:9, :TILE]
            for b in range(SUBS):
                la_ref[pl.ds(SUBS * s + b, 1), :] = la[b : b + 1]
            here = extra[9:10, :TILE]
            bound = here if bound is None else jnp.maximum(bound, here)
            numbers_here = extra[0:3, TILE:].astype(jnp.int32)
            head = (s << 20) | ((RING * later + sooner) << 16)
            entry = head | (entry_base + 257 * numbers_here[0:CAP])
            slot = lax.broadcasted_iota(jnp.int32, (CAP, TILE), 0)
            entry = jnp.where(slot < numbers_here[CAP : CAP + 1], entry, -1)
            for e in range(CAP):
                table[pl.ds(N_ROWS * e + s, 1), :] = entry[e : e + 1]
    for ref in (cols_ref, rows_ref):
        ref[0:8] = jnp.broadcast_to(bound, (8, TILE))

    lane = lax.broadcasted_iota(jnp.int32, (N_ROWS, TILE), 1) & (2 * N_ROWS - 1)
    moved = pltpu.roll(table[...], (TILE - 2 * (RING * y + z)) & (TILE - 1), axis=1)
    second = pltpu.roll(moved[N_ROWS:], 2, axis=1)
    compact[...] = jnp.where(lane < 2, moved[:N_ROWS], second)
    copy = pltpu.make_async_copy(compact, numbers, sem)
    copy.start()
    acc[...] = jnp.zeros_like(acc)

    bound = None
    for k in range(2 * RING):
        side = core ^ (k // RING)
        place = k % RING
        offset = jnp.where(side == 0, gray(place), (0, 3, 1, 2)[place])
        owner = 2 * (x ^ offset) + side
        extra = y_extra[TSUB * k : TSUB * (k + 1)].astype(jnp.float32)
        rows = pl.ds(pl.multiple_of(TSUB * owner, TSUB), TSUB)
        a_ref[rows, :] = extra[:, 0] + extra[:, 1] + extra[:, 2]
        lb_ref[rows, :] = extra[:, 3] + extra[:, 4] + extra[:, 5]
        here = extra[0, 6:7]
        bound = here if bound is None else jnp.maximum(bound, here)
    for ref in (cols_ref, rows_ref):
        ref[8:16] = jnp.broadcast_to(bound, (8, TILE))

    copy.wait()

    def block(s, place):
        for px in range(RING):
            for side in range(2):
                for e in range(CAP):
                    entry = numbers[s, 2 * N_ROWS * px + 2 * e + side]
                    item_ref[place] = entry
                    place = place + jnp.where(entry >= 0, 1, 0)
        item_ref[place] = jnp.int32(NOTHING)
        return place + (place & 1)

    end = lax.fori_loop(0, N_ROWS, block, jnp.int32(8))
    for k in range(2 * LAST_UNROLL):
        item_ref[end + k] = jnp.int32(NOTHING)
    item_ref[0] = (end - 8) >> 1
    item_ref[1] = RING * y + z
    for copy in large:
        copy.wait()
    row_core(a_ref[...], item_ref, xs, ys, cols_ref, out_ref, a_buf, u_buf, acc, top)


def row_kernel(item_ref, x_ref, y_ref, side_ref, parts_ref, out_ref, a_buf, u_buf, acc, top):
    acc[...] = jnp.zeros_like(acc)
    a = side_ref[NORMS:] - lse_over_first(parts_ref[...])
    row_core(a, item_ref, x_ref, y_ref, side_ref, out_ref, a_buf, u_buf, acc, top)


def row_core(a, item_ref, x_ref, y_ref, norm_ref, out_ref, a_buf, u_buf, acc, top):
    mid, fast = spread(a, norm_ref)
    n_items = item_ref[0]
    eye = diagonal()

    @pl.when(fast)
    def _():
        u_buf[0:TILES] = jnp.exp(a - mid)
        u_buf[TILES:] = jnp.zeros((8, TILE), jnp.float32)

        def work(w):
            s, h, t0, t1, r0, r1 = item_at(item_ref, w)
            u0, u1 = u_buf[pl.ds(t0, 1), :], u_buf[pl.ds(t1, 1), :]
            e = exps(x_ref[h], two_tiles(y_ref, r0, r1))
            acc[s] += e[:, :TILE] * u0 + e[:, TILE:] * u1

        sweep(n_items, work)
        for k in range(N_ROWS * SUBS):
            s, b = k // SUBS, k % SUBS
            col = jnp.sum(acc[s, b * TILE : (b + 1) * TILE, :], axis=1, keepdims=True)
            a_buf[k : k + 1, :] = as_row(eye, col)
        done = mid + jnp.log(a_buf[0 : N_ROWS * SUBS])
        out_ref[...] = jnp.broadcast_to(done[None], out_ref.shape)

    @pl.when(jnp.logical_not(fast))
    def _():
        a_buf[0:TILES] = a
        a_buf[TILES:] = jnp.zeros((8, TILE), jnp.float32)
        top[...] = jnp.full_like(top, -jnp.inf)

        def step(w, _):
            s, h, t0, t1, r0, r1 = item_at(item_ref, w)
            for t, r in ((t0, r0), (t1, r1)):

                @pl.when(t < TILES)
                def _(t=t, r=r):
                    score = GAIN * products(x_ref[h], y_ref[r]) + a_buf[pl.ds(t, 1), :]
                    old = top[s]
                    new = jnp.maximum(old, score)
                    acc[s] = acc[s] * rescale(old, new) + jnp.exp(score - new)
                    top[s] = new

            return 0

        lax.fori_loop(0, n_items, step, 0)

        def finish(k, _):
            s, b = lax.div(k, SUBS), lax.rem(k, SUBS)
            rows = pl.ds(pl.multiple_of(b * TILE, TILE), TILE)
            block = top[s, rows, :]
            high = jnp.max(block, axis=1, keepdims=True)
            base = jnp.where(high == -jnp.inf, 0.0, high)
            total = jnp.sum(acc[s, rows, :] * jnp.exp(block - base), axis=1, keepdims=True)
            high_row = jnp.max(jnp.where(eye, high, -jnp.inf), axis=0, keepdims=True)
            done = high_row + jnp.log(as_row(eye, total))
            out_ref[:, pl.ds(k, 1), :] = jnp.broadcast_to(done[None], (N_ROWS, 1, TILE))
            return 0

        lax.fori_loop(0, N_ROWS * SUBS, finish, 0)


def last_col_kernel(
    item_ref, x_ref, y_ref, side_ref, parts_ref, norm_ref, out_ref, f_ref, b_buf, *scratch
):
    b = side_ref[NORMS:] - lse_over_first(parts_ref[...])
    b_buf[...] = b
    for k in range(SUBS):
        here = b_buf[pl.ds(SUBS * item_ref[1] + k, 1), :]
        f_ref[k : k + 1, :] = EPSILON * (here + UNIT * norm_ref[k : k + 1, :])
    col_core(b, item_ref, x_ref, y_ref, side_ref, out_ref, *scratch)


def col_kernel(item_ref, x_ref, y_ref, side_ref, parts_ref, out_ref, *scratch):
    b = side_ref[NORMS:] - lse_over_first(parts_ref[...])
    col_core(b, item_ref, x_ref, y_ref, side_ref, out_ref, *scratch)


def col_core(b, item_ref, x_ref, y_ref, norm_ref, out_ref, spread_buf, acc, top):
    mid, fast = spread(b, norm_ref)
    n_items = item_ref[0]
    eye = diagonal()

    def lay_out(values):
        for k in range(N_ROWS * SUBS):
            s, part = k // SUBS, k % SUBS
            col = as_col(eye, values[k : k + 1, :])
            spread_buf[s, part * TILE : (part + 1) * TILE, :] = jnp.broadcast_to(col, (TILE, TILE))

    acc[...] = jnp.zeros_like(acc)

    @pl.when(fast)
    def _():
        lay_out(jnp.exp(b - mid))

        def work(w):
            s, h, t0, t1, r0, r1 = item_at(item_ref, w)
            e = exps(x_ref[h], two_tiles(y_ref, r0, r1))
            v = spread_buf[s]
            acc[t0] += jnp.sum((e[:, :TILE] * v).reshape(SRC // 8, 8, TILE), axis=0)
            acc[t1] += jnp.sum((e[:, TILE:] * v).reshape(SRC // 8, 8, TILE), axis=0)

        sweep(n_items, work)
        done = mid + jnp.log(jnp.sum(acc[0:TILES], axis=1))
        out_ref[...] = jnp.broadcast_to(done[None], out_ref.shape)

    @pl.when(jnp.logical_not(fast))
    def _():
        lay_out(b)
        top[...] = jnp.full_like(top, -jnp.inf)

        def step(w, _):
            s, h, t0, t1, r0, r1 = item_at(item_ref, w)
            for t, r in ((t0, r0), (t1, r1)):

                @pl.when(t < TILES)
                def _(t=t, r=r):
                    score = GAIN * products(x_ref[h], y_ref[r]) + spread_buf[s]
                    score = score.reshape(SRC // 8, 8, TILE)
                    old = top[t]
                    new = jnp.maximum(old, jnp.max(score, axis=0))
                    acc[t] = acc[t] * rescale(old, new) + jnp.sum(
                        jnp.exp(score - new[None]), axis=0
                    )
                    top[t] = new

            return 0

        lax.fori_loop(0, n_items, step, 0)
        high = jnp.max(top[0:TILES], axis=1)
        base = jnp.where(high == -jnp.inf, 0.0, high)
        total = jnp.sum(acc[0:TILES] * jnp.exp(top[0:TILES] - base[:, None, :]), axis=1)
        out_ref[...] = jnp.broadcast_to((high + jnp.log(total))[None], out_ref.shape)


VMEM = pl.BlockSpec(memory_space=pltpu.VMEM)
ANY = pl.BlockSpec(memory_space=pl.ANY)
SMEM = pl.BlockSpec(memory_space=pltpu.SMEM)


def limit(mebibytes):
    return pltpu.CompilerParams(vmem_limit_bytes=mebibytes * 1024 * 1024)


def shape(dims, dtype=jnp.float32):
    return jax.ShapeDtypeStruct(dims, dtype)


def prepare(*operands):
    return pl.pallas_call(
        prepare_kernel,
        out_shape=(
            shape((SRC + EXTRA, FEAT), jnp.bfloat16),
            shape((TSUB, FEAT + EXTRA, TILE), jnp.bfloat16),
            shape((SUBS, TILE)),
            shape((TSUB, TILE)),
        ),
        in_specs=[ANY] * 7,
        out_specs=(VMEM,) * 4,
        scratch_shapes=[
            pltpu.VMEM((TSUB * TILE, FEAT), jnp.bfloat16),
            pltpu.VMEM((SUBS, TILE), jnp.float32),
            pltpu.VMEM((TSUB, TILE), jnp.float32),
            pltpu.VMEM((TSUB, TILE), jnp.float32),
            pltpu.VMEM((CAP, TILE), jnp.int32),
            pltpu.VMEM((1, TILE), jnp.int32),
            pltpu.SemaphoreType.DMA((7,)),
        ],
        compiler_params=limit(60),
        name="prepare",
    )(*operands)


ROW_SCRATCH = [
    pltpu.VMEM((TILES + 8, TILE), jnp.float32),
    pltpu.VMEM((TILES + 8, TILE), jnp.float32),
    pltpu.VMEM((N_ROWS, SRC, TILE), jnp.float32),
    pltpu.VMEM((N_ROWS, SRC, TILE), jnp.float32),
]
COL_SCRATCH = [
    pltpu.VMEM((N_ROWS, SRC, TILE), jnp.float32),
    pltpu.VMEM((TILES + 1, 8, TILE), jnp.float32),
    pltpu.VMEM((TILES + 1, 8, TILE), jnp.float32),
]
ROW_PARTS = shape((N_ROWS, N_ROWS * SUBS, TILE))


def first_pass(at, pieces):
    return pl.pallas_call(
        first_kernel,
        out_shape=(
            ROW_PARTS,
            shape((LISTED,), jnp.int32),
            shape((NORMS + N_ROWS * SUBS, TILE)),
            shape((NORMS + TILES, TILE)),
            shape((N_ROWS, SRC, FEAT), jnp.bfloat16),
            shape((TILES, FEAT, TILE), jnp.bfloat16),
        ),
        in_specs=[SMEM] + [ANY] * N_PIECES,
        out_specs=(VMEM, SMEM, VMEM, VMEM, VMEM, VMEM),
        scratch_shapes=ROW_SCRATCH
        + [
            pltpu.SemaphoreType.DMA((N_PIECES,)),
            pltpu.VMEM((TILES, TILE), jnp.float32),
            pltpu.VMEM((CAP * N_ROWS, TILE), jnp.int32),
            pltpu.VMEM((N_ROWS, TILE), jnp.int32),
            pltpu.SMEM((N_ROWS, TILE), jnp.int32),
            pltpu.VMEM((N_ROWS, EXTRA, FEAT), jnp.bfloat16),
            pltpu.VMEM((TILES, EXTRA, TILE), jnp.bfloat16),
            pltpu.SemaphoreType.DMA((N_PIECES,)),
            pltpu.SemaphoreType.DMA,
        ],
        compiler_params=limit(24),
        name="first_row_pass",
    )(at, *[pltpu.with_memory_space_constraint(piece, pltpu.HBM) for piece in pieces])


def row_pass(items, *operands):
    return pl.pallas_call(
        row_kernel,
        out_shape=ROW_PARTS,
        in_specs=[SMEM] + [VMEM] * len(operands),
        out_specs=VMEM,
        scratch_shapes=ROW_SCRATCH,
        compiler_params=limit(20),
        name="row_pass",
    )(items, *operands)


def col_pass(items, *operands):
    return pl.pallas_call(
        col_kernel,
        out_shape=shape((N_COLS, TILES, TILE)),
        in_specs=[SMEM] + [VMEM] * len(operands),
        out_specs=VMEM,
        scratch_shapes=COL_SCRATCH,
        compiler_params=limit(20),
        name="col_pass",
    )(items, *operands)


def last_col_pass(items, *operands):
    return pl.pallas_call(
        last_col_kernel,
        out_shape=(shape((1, TILES, TILE)), shape((SUBS, TILE))),
        in_specs=[SMEM] + [VMEM] * len(operands),
        out_specs=(VMEM, VMEM),
        scratch_shapes=[pltpu.VMEM((N_ROWS * SUBS, TILE), jnp.float32)] + COL_SCRATCH,
        compiler_params=limit(20),
        name="last_col_pass",
    )(items, *operands)


def swap(blocks, axes):
    return lax.all_to_all(blocks, axes, split_axis=0, concat_axis=0, tiled=True)


def exchange(block, partner):
    pairs = []
    for place in range(N_ROWS * N_COLS):
        at = tuple(int(k) for k in np.unravel_index(place, DIMS))
        pairs.append((place, int(np.ravel_multi_index(partner(*at), DIMS))))
    return lax.ppermute(block, NAMES, pairs)


def doubled(block, partner):
    return jnp.concatenate([block, exchange(block, partner)])


def after(value, events):
    return lax.optimization_barrier((value, events))[0]


def gather_all(sources, targets):
    along = [source_partner(0, flip) for flip in (1, 3)]
    across = [source_partner(1, flip) for flip in (1, 3)]
    beside = [target_partner(order) for order in (0, 1)]

    pair = jnp.stack([sources, exchange(sources, along[0])])
    tiles = jnp.concatenate([targets, exchange(targets, beside[0])])
    other = exchange(pair, along[1])
    first, second = exchange(pair, across[0]), exchange(pair, across[1])
    further = exchange(after(tiles, pair), beside[1])
    relayed = exchange(first, across[1])
    pieces = [pair, first, second, relayed]
    near = exchange(after(tiles, (first, second)), sibling)
    first, second = exchange(other, across[0]), exchange(other, across[1])
    pieces += [other, first, second, exchange(second, across[0])]
    far = exchange(after(further, (relayed, first, pieces[-1])), sibling)
    return pieces + [tiles, further, near, far]


def source_partner(stage, flip):
    def partner(x, y, z, core):
        return (x, y ^ flip, z, core) if stage == core else (x, y, z ^ flip, core)

    return partner


def target_partner(order):
    return lambda x, y, z, core: (x ^ (1, 3)[order ^ core], y, z, core)


def sibling(x, y, z, core):
    return (x, y, z, core ^ 1)


def body(
    source_points, target_points, source_mass, target_mass, target_init, pair_tiles, pair_count
):
    x_block, y_block, source_norm, target_part = prepare(
        source_points,
        target_points,
        source_mass.reshape(SUBS, TILE),
        target_mass.reshape(TSUB, TILE),
        target_init.reshape(TSUB, TILE),
        pair_tiles.T,
        pair_count.reshape(1, -1),
    )
    pieces = gather_all(x_block, y_block)

    at = jnp.stack([lax.axis_index(name) for name in NAMES]).astype(jnp.int32)
    row_parts, items, cols, rows, xs, ys = first_pass(at, pieces)
    for iteration in range(ITERS - 1):
        col_parts = col_pass(items, xs, ys, cols, swap(row_parts, ROWS))
        row_parts = row_pass(items, xs, ys, rows, swap(col_parts, COLS))
    col_parts, source_pot = last_col_pass(
        items, xs, ys, cols, swap(row_parts, ROWS), source_norm
    )
    last = swap(col_parts.reshape(N_COLS, TSUB, TILE), COLS)
    target_pot = target_part - EPSILON * lse_over_first(last)
    return (source_pot.reshape(-1), target_pot.reshape(-1))


def solution(mesh):
    grid = Mesh(mesh.devices.reshape(DIMS), NAMES)
    placed = (
        P(NAMES, None),
        P(NAMES, None),
        P(NAMES),
        P(NAMES),
        P(NAMES),
        P(NAMES, None),
        P(NAMES),
    )
    return jax.shard_map(
        body, mesh=grid, in_specs=placed, out_specs=(P(NAMES), P(NAMES)), check_vma=False
    )
```
